32 devices in a mesh: cam: 8 (over y, x, core), fsdp: 4 (over z).
Axes of the slice: x: 2, y: 2, z: 4, core: 2. Of those that a mesh axis runs over, the one named last changes fastest.
Arguments:
- queries: bfloat16 [4, 1280, 4096], P('fsdp', 'cam'), may hold values from -16 to 16
- keys: bfloat16 [4, 1280, 4096], P('fsdp', 'cam'), may hold values from -16 to 16
- values: bfloat16 [4, 1280, 4096], P('fsdp', 'cam'), may hold values from -6 to 6
- out_weight: bfloat16 [4096, 5120], P('fsdp'), may hold values from -0.09375 to 0.09375
- block_counts: int32 [4, 8], P('fsdp', 'cam'), may hold values from 1 to 5, as said below
- row_mask: int32 [4, 1280], P('fsdp', 'cam'), may hold values from 0 to 1, as said below
Outputs:
- projected: bfloat16 [4, 1280, 5120], P('fsdp', 'cam')
The draws below stay inside these ranges and needn't reach their ends.
Inputs may be any that keep to these rules, and one draw needn't show every extreme that they name: `block_counts`: every view uses at least one block; in every clip one view uses all 5 blocks. `row_mask`: 0 or 1; the first two rows of every block are 1.
All inputs are finite; a program needn't handle non-finite values.
Results may differ from the reference program's by a relative error of at most 0.0057.
Values may be sent and summed in bfloat16 or wider, within the bound.
No kernel may reach another device: no remote copies, remote signals or barrier semaphores. Data moves between devices by JAX's collectives and lax.ppermute only.
A program may use at most 128 MiB of HBM per device.

```python
import math
import jax
import jax.numpy as jnp
from jax import lax

D = 5120
HEADS = 32
HEAD_DIM = 128
BLOCK = 32
NB = 5
VIEWS = 8
CLIPS = 4
ROWS = 160
TOK = 1280
HD = 4096


def pair_draw(key):
    full_shape = (CLIPS, TOK, HD)
    key_a = jax.random.fold_in(key, 101)
    key_b = jax.random.fold_in(key, 102)
    query_draw = jnp.clip(jax.random.normal(key_a, full_shape, jnp.float32), -4.0, 4.0)
    key_draw = jnp.clip(jax.random.normal(key_b, full_shape, jnp.float32), -4.0, 4.0)
    return (query_draw, key_draw)


def draw_queries(key, part):
    return pair_draw(key)[0].astype(jnp.bfloat16)


def draw_keys(key, part):
    return pair_draw(key)[1].astype(jnp.bfloat16)


def draw_block_counts(key, part):
    pick = jax.random.randint(jax.random.fold_in(key, 201), (CLIPS, VIEWS), 0, 3) == 0
    extra = jax.random.randint(jax.random.fold_in(key, 202), (CLIPS, VIEWS), 0, NB)
    counts = jnp.where(pick, 1 + extra, 1)
    fullest = jax.random.randint(jax.random.fold_in(key, 203), (CLIPS,), 0, VIEWS)
    view_ids = jnp.arange(VIEWS, dtype=jnp.int32)[None, :]
    return jnp.where(view_ids == fullest[:, None], NB, counts).astype(jnp.int32)


def draw_row_mask(key, part):
    coins = jax.random.randint(jax.random.fold_in(key, 301), (CLIPS, TOK), 0, 5) > 0
    inside = jnp.arange(TOK, dtype=jnp.int32) % BLOCK < 2
    return jnp.where(inside[None, :], 1, coins.astype(jnp.int32)).astype(jnp.int32)


def shard_levels(own_key, dims, cuts, least, largest):
    loudness, own = 1.0, jax.random.fold_in(own_key, 6)
    for position, shards_of in cuts:
        heights = jnp.exp(jax.random.uniform(jax.random.fold_in(own, position), (shards_of,), jnp.float32, least / len(cuts), largest / len(cuts)))
        loudness = loudness * jnp.repeat(heights, dims[position] // shards_of).reshape([-1 if axis == position else 1 for axis in range(len(dims))])
    return loudness


def bell_draw(key, extent, deviation, most, split=(), kind=jnp.bfloat16):
    level = shard_levels(key, extent, split, -0.22, 0.18) if split else 1.0
    entries = jax.random.normal(key, extent, jnp.float32) * deviation * level
    return jnp.minimum(jnp.maximum(entries, -most), most).astype(kind)


def setup_inputs(seed: int = 0) -> dict:
    streams_of = jax.random.split(jax.random.key(seed), 7)
    queries = draw_queries(jax.random.fold_in(streams_of[6], 71), 0)
    keys = draw_keys(jax.random.fold_in(streams_of[6], 71), 0)
    values = bell_draw(streams_of[2], (CLIPS, TOK, HD), 1.0, 6.0, ((0, 4), (1, 8)))
    out_weight = bell_draw(streams_of[3], (HD, D), HD ** -0.5, 0.09375, ((0, 4),))
    block_counts = draw_block_counts(jax.random.fold_in(streams_of[6], 71), 0)
    row_mask = draw_row_mask(jax.random.fold_in(streams_of[6], 71), 0)
    return dict(queries=queries, keys=keys, values=values, out_weight=out_weight, block_counts=block_counts, row_mask=row_mask)


def reference(queries, keys, values, out_weight, block_counts, row_mask):
    score_scale = 1.0 / math.sqrt(HEAD_DIM)
    positions = jnp.arange(TOK, dtype=jnp.int32)
    which_view = positions // ROWS
    which_block = positions % ROWS // BLOCK
    row_valid = (row_mask == 1) & (which_block[None, :] < block_counts[:, which_view])

    def split_heads(tensor):
        return tensor.reshape(CLIPS, TOK, HEADS, HEAD_DIM).transpose(0, 2, 1, 3).reshape(CLIPS * HEADS, TOK, HEAD_DIM)
    head_masks = jnp.repeat(row_valid, HEADS, axis=0)

    def one_head(pieces):
        query_h, key_h, value_h, key_ok = pieces
        scores = jnp.dot(query_h, key_h.T, preferred_element_type=jnp.float32) * score_scale
        scores = jnp.where(key_ok[None, :], scores, jnp.float32(-1e+30))
        row_top = lax.optimization_barrier(jnp.max(scores, axis=1, keepdims=True))
        raised = jnp.exp(scores - row_top)
        weights = (raised / lax.optimization_barrier(jnp.sum(raised, axis=1, keepdims=True))).astype(jnp.bfloat16)
        return jnp.dot(weights, value_h, preferred_element_type=jnp.float32).astype(jnp.bfloat16)
    heads_out = lax.map(one_head, (split_heads(queries), split_heads(keys), split_heads(values), head_masks))
    attended = heads_out.reshape(CLIPS, HEADS, TOK, HEAD_DIM).transpose(0, 2, 1, 3).reshape(CLIPS * TOK, HD)
    projected = jnp.dot(attended, out_weight, preferred_element_type=jnp.float32).reshape(CLIPS, TOK, D)
    return jnp.where(row_valid[:, :, None], projected, jnp.float32(0.0)).astype(jnp.bfloat16)
```

```python
import math

import jax
import jax.numpy as jnp
from jax import lax
from jax.sharding import PartitionSpec as P

HEAD_DIM = 128
BLOCK = 32


def attend(query_rows, key_rows, value_rows, key_ok):
    score_scale = 1.0 / math.sqrt(HEAD_DIM)
    count_all = query_rows.shape[0]
    head_count = query_rows.shape[1] // HEAD_DIM
    block_rows = 512 if count_all % 512 == 0 else count_all
    outputs = []
    for head_number in range(head_count):
        column = head_number * HEAD_DIM
        query_h = query_rows[:, column : column + HEAD_DIM].reshape(
            count_all // block_rows, block_rows, HEAD_DIM
        )
        key_h = key_rows[:, column : column + HEAD_DIM]
        value_h = value_rows[:, column : column + HEAD_DIM]

        def one_block(query_block):
            scores = (
                jnp.einsum("qd,kd->qk", query_block, key_h, preferred_element_type=jnp.float32)
                * score_scale
            )
            scores = jnp.where(key_ok[None, :], scores, jnp.float32(-1e30))
            row_top = jnp.max(scores, axis=1, keepdims=True)
            raised = jnp.exp(scores - row_top)
            weights = (raised / jnp.sum(raised, axis=1, keepdims=True)).astype(jnp.bfloat16)
            return jnp.dot(weights, value_h, preferred_element_type=jnp.float32).astype(
                jnp.bfloat16
            )

        outputs.append(lax.map(one_block, query_h).reshape(count_all, HEAD_DIM))
    return jnp.concatenate(outputs, axis=1)


def local(queries, keys, values, out_weight, block_counts, row_mask):
    row_count = queries.shape[1]
    cam_count = lax.axis_size("cam")
    place = lax.axis_index("cam")
    columns = out_weight.shape[1] // cam_count
    offsets = jnp.arange(row_count, dtype=jnp.int32)
    row_valid = (row_mask[0] == 1) & (offsets // BLOCK < block_counts[0, 0])
    weight_part = lax.dynamic_slice_in_dim(out_weight, place * columns, columns, axis=1)
    weight_all = lax.all_gather(weight_part, "fsdp", axis=0, tiled=True)

    key_flag = lax.all_gather(row_valid.astype(jnp.bfloat16), "cam", axis=0, tiled=True)
    stacked = jnp.concatenate([queries, keys, values], axis=0)
    exchanged = lax.all_to_all(stacked, "cam", split_axis=2, concat_axis=1, tiled=True)
    head_rows = attend(exchanged[0], exchanged[1], exchanged[2], key_flag > 0.5)
    attended = lax.all_gather(head_rows, "cam", axis=1, tiled=True)
    projected = jnp.dot(attended, weight_all, preferred_element_type=jnp.float32).astype(
        jnp.bfloat16
    )
    result = lax.all_to_all(projected, "cam", split_axis=0, concat_axis=1, tiled=True)
    return jnp.where(row_valid[:, None], result, jnp.bfloat16(0.0))[None]


def solution(mesh):
    in_specs = (
        P("fsdp", "cam", None),
        P("fsdp", "cam", None),
        P("fsdp", "cam", None),
        P("fsdp", None),
        P("fsdp", "cam"),
        P("fsdp", "cam"),
    )
    out_specs = P("fsdp", "cam", None)
    return jax.shard_map(local, mesh=mesh, in_specs=in_specs, out_specs=out_specs, check_vma=False)
```

```python
import math

import jax
import jax.numpy as jnp
from jax import lax
from jax.experimental import pallas as pl
from jax.experimental.pallas import tpu as pltpu
from jax.sharding import PartitionSpec as P

HEAD_DIM = 128
BLOCK = 32
SENTINEL = 32.0
LIMIT = 24.0
VMEM = 56 * 1024 * 1024
QUERY_TILE = 256


def params(limit=VMEM):
    return pltpu.CompilerParams(vmem_limit_bytes=limit)


def xor_permute(array, mask, count):
    return lax.ppermute(array, "cam", [(place, place ^ mask) for place in range(count)])


def pack(place, queries, keys, values, valid_column, count):
    rows, features = queries.shape
    width = features // count
    step = BLOCK

    def body(place_ref, q_ref, k_ref, v_ref, valid_ref, *out_refs):
        good = valid_ref[...] > 0.5
        for mask in range(count):
            start = pl.multiple_of((place_ref[0] ^ mask) * width, HEAD_DIM)
            chosen = pl.ds(start, width)
            out_refs[mask][0] = q_ref[:, chosen]
            out_refs[mask][1] = jnp.where(good, k_ref[:, chosen], jnp.bfloat16(SENTINEL))
            out_refs[mask][2] = v_ref[:, chosen]

    row_spec = pl.BlockSpec((step, features), lambda i, place_ref: (i, 0))
    return pl.pallas_call(
        body,
        grid_spec=pltpu.PrefetchScalarGridSpec(
            num_scalar_prefetch=1,
            grid=(rows // step,),
            in_specs=[row_spec, row_spec, row_spec]
            + [pl.BlockSpec((step, 1), lambda i, place_ref: (i, 0))],
            out_specs=[pl.BlockSpec((3, step, width), lambda i, place_ref: (0, i, 0))] * count,
        ),
        out_shape=[jax.ShapeDtypeStruct((3, rows, width), jnp.bfloat16)] * count,
        compiler_params=params(),
        cost_estimate=pl.CostEstimate(
            flops=0, bytes_accessed=12 * rows * features, transcendentals=0
        ),
        name="pack",
    )(place, queries, keys, values, valid_column)


def attend(place, received, rows):
    count = len(received)
    width = received[0].shape[2]
    total = count * rows
    factor = math.log2(math.e) / math.sqrt(HEAD_DIM)

    def body(place_ref, *refs):
        parts = refs[:count]
        out_ref = refs[count]
        query_all, key_all, value_t, result = refs[count + 1 :]
        for mask in range(count):
            where = pl.ds(mask * rows, rows)
            query_all[where, :] = parts[mask][0]
            key_all[where, :] = parts[mask][1]
        value_all = jnp.concatenate([parts[mask][2] for mask in range(count)], axis=0)
        value_t[...] = value_all.T
        key_rows = key_all[...]
        bias = jnp.where(key_rows.astype(jnp.float32) > LIMIT, jnp.float32(-1e30), 0.0)
        bias = jnp.concatenate([bias] * (QUERY_TILE // HEAD_DIM), axis=1)
        for tile in range(total // QUERY_TILE):
            where = pl.ds(tile * QUERY_TILE, QUERY_TILE)
            scores = lax.dot_general(
                key_rows,
                query_all[where, :],
                (((1,), (1,)), ((), ())),
                preferred_element_type=jnp.float32,
            )
            scores = scores + bias
            top = jnp.max(scores, axis=0, keepdims=True)
            raised = jnp.exp2((scores - top) * factor)
            norm = jnp.sum(raised, axis=0, keepdims=True)
            summed = jnp.dot(
                value_t[...], raised.astype(jnp.bfloat16), preferred_element_type=jnp.float32
            )
            result[where, :] = (summed / norm).T.astype(jnp.bfloat16)
        for mask in range(count):
            out_ref[pl.ds(place_ref[0] ^ mask, 1)] = result[pl.ds(mask * rows, rows), :][None]

    flops = 4 * total * total * width
    return pl.pallas_call(
        body,
        grid_spec=pltpu.PrefetchScalarGridSpec(
            num_scalar_prefetch=1,
            grid=(width // HEAD_DIM,),
            in_specs=[pl.BlockSpec((3, rows, HEAD_DIM), lambda h, place_ref: (0, 0, h))] * count,
            out_specs=pl.BlockSpec((count, rows, HEAD_DIM), lambda h, place_ref: (0, 0, h)),
            scratch_shapes=[
                pltpu.VMEM((total, HEAD_DIM), jnp.bfloat16),
                pltpu.VMEM((total, HEAD_DIM), jnp.bfloat16),
                pltpu.VMEM((HEAD_DIM, total), jnp.bfloat16),
                pltpu.VMEM((total, HEAD_DIM), jnp.bfloat16),
            ],
        ),
        out_shape=jax.ShapeDtypeStruct((count, rows, width), jnp.bfloat16),
        compiler_params=params(),
        cost_estimate=pl.CostEstimate(
            flops=flops, bytes_accessed=8 * total * width, transcendentals=flops // 512
        ),
        name="attend",
    )(place, *received)


def gather_features(own, count):
    half = count // 2
    held = {0: [own[:half], own[half:]]}
    if count == 8:
        over_x_0 = xor_permute(held[0][0], 2, count)
        over_y_1 = xor_permute(held[0][1], 4, count)
        over_x_1 = xor_permute(held[0][1], 2, count)
        over_y_0 = xor_permute(held[0][0], 4, count)
        diagonal_0 = xor_permute(over_x_0, 4, count)
        diagonal_1 = xor_permute(over_y_1, 2, count)
        held[2] = [over_x_0, over_x_1]
        held[4] = [over_y_0, over_y_1]
        held[6] = [diagonal_0, diagonal_1]
    else:
        for mask in range(2, count, 2):
            held[mask] = [xor_permute(piece, mask, count) for piece in held[0]]
    for mask in range(0, count, 2):
        held[mask + 1] = [xor_permute(piece, 1, count) for piece in held[mask]]
    return [held[mask] for mask in range(count)]


def project(place, features, weight):
    count = len(features)
    half, rows, width = features[0][0].shape
    columns = weight.shape[1]

    def body(place_ref, *refs):
        halves = refs[: 2 * count]
        weight_ref = refs[2 * count]
        out_refs = refs[2 * count + 1 : 3 * count + 1]
        landed, weight_all, total, sems, weight_sems = refs[3 * count + 1 :]
        copies = []
        weight_copies = []
        for mask in range(count):
            start = pl.multiple_of((place_ref[0] ^ mask) * width, width)
            copy = pltpu.make_async_copy(
                weight_ref.at[pl.ds(start, width), :], weight_all.at[mask], weight_sems.at[mask]
            )
            copy.start()
            weight_copies.append(copy)
            for side in range(2):
                copy = pltpu.make_async_copy(
                    halves[2 * mask + side], landed.at[mask, side], sems.at[mask, side]
                )
                copy.start()
                copies.append(copy)
        for mask in range(count):
            weight_copies[mask].wait()
            for side in range(2):
                copies[2 * mask + side].wait()
                part = jnp.dot(
                    landed[mask, side].reshape(half * rows, width),
                    weight_all[mask],
                    preferred_element_type=jnp.float32,
                )
                if mask == 0:
                    total[side] = part.reshape(half, rows, columns)
                else:
                    total[side] += part.reshape(half, rows, columns)
        for mask in range(count):
            view = place_ref[0] ^ mask
            out_refs[mask][...] = total[view // half, view % half].astype(jnp.bfloat16)

    any_spec = pl.BlockSpec(memory_space=pl.ANY)
    flat = [piece for pair in features for piece in pair]
    return pl.pallas_call(
        body,
        grid_spec=pltpu.PrefetchScalarGridSpec(
            num_scalar_prefetch=1,
            grid=(1,),
            in_specs=[any_spec] * (2 * count + 1),
            out_specs=[pl.BlockSpec((rows, columns), lambda i, place_ref: (0, 0))] * count,
            scratch_shapes=[
                pltpu.VMEM((count, 2, half, rows, width), jnp.bfloat16),
                pltpu.VMEM((count, width, columns), jnp.bfloat16),
                pltpu.VMEM((2, half, rows, columns), jnp.float32),
                pltpu.SemaphoreType.DMA((count, 2)),
                pltpu.SemaphoreType.DMA((count,)),
            ],
        ),
        out_shape=[jax.ShapeDtypeStruct((rows, columns), jnp.bfloat16)] * count,
        compiler_params=params(),
        cost_estimate=pl.CostEstimate(
            flops=2 * count * rows * count * width * columns,
            bytes_accessed=2 * count * count * rows * width,
            transcendentals=0,
        ),
        name="project",
    )(place, *flat, weight)


def assemble(place, chunks, sizes, valid_column, count):
    rows = valid_column.shape[0]
    columns = sum(sizes)
    if any(size % HEAD_DIM for size in sizes):
        joined = [
            jnp.concatenate([chunk[mask] for chunk in chunks], axis=1) for mask in range(count)
        ]
        stacked = jnp.stack(joined)[jnp.arange(count) ^ place[0]]
        result = jnp.moveaxis(stacked, 0, 1).reshape(rows, count * columns)
        return jnp.where(valid_column > 0.5, result, jnp.bfloat16(0.0))

    def body(place_ref, valid_ref, *refs):
        out_ref = refs[-1]
        good = valid_ref[...] > 0.5
        for index in range(len(sizes)):
            for mask in range(count):
                start = (place_ref[0] ^ mask) * columns + sum(sizes[:index])
                chosen = pl.ds(pl.multiple_of(start, HEAD_DIM), sizes[index])
                piece = refs[index * count + mask][...]
                out_ref[:, chosen] = jnp.where(good, piece, jnp.bfloat16(0.0))

    step = BLOCK
    return pl.pallas_call(
        body,
        grid_spec=pltpu.PrefetchScalarGridSpec(
            num_scalar_prefetch=1,
            grid=(rows // step,),
            in_specs=[pl.BlockSpec((step, 1), lambda i, place_ref: (i, 0))]
            + [
                pl.BlockSpec((step, size), lambda i, place_ref: (i, 0))
                for size in sizes
                for mask in range(count)
            ],
            out_specs=pl.BlockSpec((step, count * columns), lambda i, place_ref: (i, 0)),
        ),
        out_shape=jax.ShapeDtypeStruct((rows, count * columns), jnp.bfloat16),
        compiler_params=params(),
        cost_estimate=pl.CostEstimate(
            flops=0, bytes_accessed=4 * rows * count * columns, transcendentals=0
        ),
        name="assemble",
    )(place, valid_column, *[piece for chunk in chunks for piece in chunk])


def local(queries, keys, values, out_weight, block_counts, row_mask):
    rows = queries.shape[1]
    count = lax.axis_size("cam")
    place = lax.axis_index("cam")
    place_array = jnp.full((1,), place, jnp.int32)
    columns = out_weight.shape[1] // count
    first = max(HEAD_DIM, -(-columns * 3 // 5 // HEAD_DIM) * HEAD_DIM)
    sizes = [first, columns - first]

    offsets = jnp.arange(rows, dtype=jnp.int32)
    row_valid = (row_mask[0] == 1) & (offsets // BLOCK < block_counts[0, 0])
    valid_column = row_valid.astype(jnp.float32)[:, None]

    weights = []
    for index, size in enumerate(sizes):
        start = place * columns + sum(sizes[:index])
        part = lax.dynamic_slice_in_dim(out_weight, start, size, axis=1)
        weights.append(part)
    weights[0], weights[1], queries = lax.optimization_barrier((weights[0], weights[1], queries))
    weights = [lax.all_gather(part, "fsdp", axis=0, tiled=True) for part in weights]

    payloads = pack(place_array, queries[0], keys[0], values[0], valid_column, count)
    received = [payloads[0]] + [
        xor_permute(payloads[mask], mask, count) for mask in range(1, count)
    ]
    attended = attend(place_array, received, rows)
    features = gather_features(attended, count)
    chunks = []
    for weight in weights:
        pieces = project(place_array, features, weight)
        chunks.append(
            [pieces[0]] + [xor_permute(pieces[mask], mask, count) for mask in range(1, count)]
        )
    return assemble(place_array, chunks, sizes, valid_column, count)[None]


def solution(mesh):
    in_specs = (
        P("fsdp", "cam", None),
        P("fsdp", "cam", None),
        P("fsdp", "cam", None),
        P("fsdp", None),
        P("fsdp", "cam"),
        P("fsdp", "cam"),
    )
    out_specs = P("fsdp", "cam", None)
    return jax.shard_map(local, mesh=mesh, in_specs=in_specs, out_specs=out_specs, check_vma=False)
```

```python
import math

import jax
import jax.numpy as jnp
from jax import lax
from jax.experimental import pallas as pl
from jax.experimental.pallas import tpu as pltpu
from jax.sharding import PartitionSpec as P

HEAD_DIM = 128
BLOCK = 32
SENTINEL = 32.0
LIMIT = 24.0
VMEM = 56 * 1024 * 1024
QUERY_TILE = 256
UNIT = 128


def params(limit=VMEM):
    return pltpu.CompilerParams(vmem_limit_bytes=limit)


def order(count):
    return sorted(range(1, count), key=lambda mask: (mask == 1, mask & 1, -bin(mask).count("1")))


def variants(total):
    return sorted({-(-total * tenths // (10 * UNIT)) * UNIT for tenths in (4, 5, 6, 8, 10)})


def full_spec(shape):
    return pl.BlockSpec(shape, lambda i, *_: (0,) * len(shape))


def column_of(row):
    n = row.shape[1]
    diagonal = lax.broadcasted_iota(jnp.int32, (n, n), 0) == lax.broadcasted_iota(
        jnp.int32, (n, n), 1
    )
    return jnp.sum(jnp.where(diagonal, row, 0.0), axis=1, keepdims=True)


def valid_column(mask_ref, blocks):
    rows = mask_ref.shape[1]
    inside = lax.broadcasted_iota(jnp.int32, (1, rows), 1) < blocks * BLOCK
    return column_of(jnp.where((mask_ref[...] == 1) & inside, 1.0, 0.0))


def xor_permute(array, mask, count):
    return lax.ppermute(array, "cam", [(place, place ^ mask) for place in range(count)])


def pack(place, block_counts, row_mask, queries, keys, values, out_weight, sizes, count):
    _, rows, features = queries.shape
    width = features // count
    depth = out_weight.shape[0]
    columns = out_weight.shape[1] // count
    slicing = all(size % HEAD_DIM == 0 for size in sizes)
    chunks = len(sizes) if slicing else 0

    def body(place_ref, blocks_ref, mask_ref, q_ref, k_ref, v_ref, w_ref, *refs):
        out_refs = refs[:count]
        weight_refs = refs[count : count + chunks]
        key_in, key_out, key_sem, sems, weight_sems = refs[count + chunks :]
        load = pltpu.make_async_copy(k_ref.at[0], key_in, key_sem.at[0])
        load.start()
        copies = []
        for index in range(chunks):
            start = pl.multiple_of(place_ref[0] * columns + sum(sizes[:index]), HEAD_DIM)
            copy = pltpu.make_async_copy(
                w_ref.at[:, pl.ds(start, sizes[index])],
                weight_refs[index],
                weight_sems.at[index],
            )
            copy.start()
            copies.append(copy)
        starts = [pl.multiple_of((place_ref[0] ^ m) * width, HEAD_DIM) for m in range(count)]
        for mask in range(count):
            for slot, ref in ((0, q_ref), (2, v_ref)):
                copy = pltpu.make_async_copy(
                    ref.at[0, :, pl.ds(starts[mask], width)],
                    out_refs[mask].at[slot],
                    sems.at[mask, slot],
                )
                copy.start()
                copies.append(copy)
        good = valid_column(mask_ref, blocks_ref[0, 0]) > 0.5
        load.wait()
        for mask in range(count):
            part = key_in[:, pl.ds(starts[mask], width)]
            key_out[mask] = jnp.where(good, part, jnp.bfloat16(SENTINEL))
            copy = pltpu.make_async_copy(key_out.at[mask], out_refs[mask].at[1], sems.at[mask, 1])
            copy.start()
            copies.append(copy)
        for copy in copies:
            copy.wait()

    any_spec = pl.BlockSpec(memory_space=pl.ANY)
    weight_shapes = [
        jax.ShapeDtypeStruct((depth, size), jnp.bfloat16) for size in sizes[:chunks]
    ]
    outputs = pl.pallas_call(
        body,
        grid_spec=pltpu.PrefetchScalarGridSpec(
            num_scalar_prefetch=2,
            grid=(1,),
            in_specs=[full_spec((1, rows))] + [any_spec] * 4,
            out_specs=[any_spec] * (count + chunks),
            scratch_shapes=[
                pltpu.VMEM((rows, features), jnp.bfloat16),
                pltpu.VMEM((count, rows, width), jnp.bfloat16),
                pltpu.SemaphoreType.DMA((1,)),
                pltpu.SemaphoreType.DMA((count, 3)),
                pltpu.SemaphoreType.DMA((len(sizes),)),
            ],
        ),
        out_shape=[jax.ShapeDtypeStruct((3, rows, width), jnp.bfloat16)] * count + weight_shapes,
        compiler_params=params(),
        cost_estimate=pl.CostEstimate(
            flops=0, bytes_accessed=12 * rows * features, transcendentals=0
        ),
        name="pack",
    )(place, block_counts, row_mask, queries, keys, values, out_weight)
    weights = list(outputs[count:])
    if not slicing:
        for index, size in enumerate(sizes):
            start = place[0] * columns + sum(sizes[:index])
            weights.append(lax.dynamic_slice_in_dim(out_weight, start, size, axis=1))
    return list(outputs[:count]), weights


def packed_offsets(place_ref, counts_ref, table, count):
    by_mask, running = [], 0
    for mask in range(count):
        by_mask.append(running)
        table[mask] = running
        running = running + counts_ref[mask] * BLOCK
    by_view, position = [], 0
    for view in range(count):
        by_view.append(position)
        position = position + counts_ref[place_ref[0] ^ view] * BLOCK
    return by_mask, by_view, running


def rows_at(start, size):
    return pl.ds(start if isinstance(start, int) else pl.multiple_of(start, BLOCK), size)


def attend(place, counts, received, rows):
    count = len(received)
    width = received[0].shape[2]
    total = count * rows
    factor = math.log2(math.e) / math.sqrt(HEAD_DIM)

    def body(place_ref, counts_ref, *refs):
        parts = refs[:count]
        out_ref = refs[count]
        query_all, key_all, value_all, value_t, result, table = refs[count + 1 :]
        by_mask, by_view, used = packed_offsets(place_ref, counts_ref, table, count)

        @pl.when(pl.program_id(0) == 0)
        def _():
            value_all[...] = jnp.zeros_like(value_all)

        for mask in range(count):
            where = rows_at(by_mask[mask], rows)
            query_all[where, :] = parts[mask][0]
            key_all[where, :] = parts[mask][1]
            value_all[where, :] = parts[mask][2]
        key_all[rows_at(used, total // 5), :] = jnp.full(
            (total // 5, HEAD_DIM), SENTINEL, jnp.bfloat16
        )
        below = 0
        for size in variants(total):

            @pl.when((used > below) & (used <= size))
            def _(size=size):
                value_t[:, :size] = value_all[:size, :].T
                key_rows = key_all[:size, :]
                bias = jnp.where(key_rows.astype(jnp.float32) > LIMIT, jnp.float32(-1e30), 0.0)
                bias = jnp.concatenate([bias] * (QUERY_TILE // HEAD_DIM), axis=1)

                def tile(index, carry):
                    where = pl.ds(pl.multiple_of(index * QUERY_TILE, QUERY_TILE), QUERY_TILE)
                    scores = lax.dot_general(
                        key_rows,
                        query_all[where, :],
                        (((1,), (1,)), ((), ())),
                        preferred_element_type=jnp.float32,
                    )
                    scores = scores + bias
                    top = jnp.max(scores, axis=0, keepdims=True)
                    raised = jnp.exp2((scores - top) * factor)
                    norm = jnp.sum(raised, axis=0, keepdims=True)
                    summed = jnp.dot(
                        value_t[:, :size],
                        raised.astype(jnp.bfloat16),
                        preferred_element_type=jnp.float32,
                    )
                    result[where, :] = (summed / norm).T.astype(jnp.bfloat16)
                    return carry

                lax.fori_loop(0, (used + QUERY_TILE - 1) // QUERY_TILE, tile, 0)

            below = size
        for view in range(count):
            moved = result[rows_at(table[place_ref[0] ^ view], rows), :]
            out_ref[rows_at(by_view[view], rows), :] = moved

    flops = 4 * total * total * width // 4
    return pl.pallas_call(
        body,
        grid_spec=pltpu.PrefetchScalarGridSpec(
            num_scalar_prefetch=2,
            grid=(width // HEAD_DIM,),
            in_specs=[pl.BlockSpec((3, rows, HEAD_DIM), lambda h, *_: (0, 0, h))] * count,
            out_specs=pl.BlockSpec((total, HEAD_DIM), lambda h, *_: (0, h)),
            scratch_shapes=[
                pltpu.VMEM((total, HEAD_DIM), jnp.bfloat16),
                pltpu.VMEM((total + total // 5, HEAD_DIM), jnp.bfloat16),
                pltpu.VMEM((total, HEAD_DIM), jnp.bfloat16),
                pltpu.VMEM((HEAD_DIM, total), jnp.bfloat16),
                pltpu.VMEM((total, HEAD_DIM), jnp.bfloat16),
                pltpu.SMEM((count,), jnp.int32),
            ],
        ),
        out_shape=jax.ShapeDtypeStruct((total, width), jnp.bfloat16),
        compiler_params=params(),
        cost_estimate=pl.CostEstimate(
            flops=flops, bytes_accessed=8 * total * width, transcendentals=flops // 512
        ),
        name="attend",
    )(place, counts, *received)


def gather_features(own, count):
    half = own.shape[0] // 2
    held = {0: [own[:half], own[half:]]}
    if count == 8:
        over_x_0 = xor_permute(held[0][0], 2, count)
        over_y_1 = xor_permute(held[0][1], 4, count)
        over_x_1 = xor_permute(held[0][1], 2, count)
        over_y_0 = xor_permute(held[0][0], 4, count)
        diagonal_0 = xor_permute(over_x_0, 4, count)
        diagonal_1 = xor_permute(over_y_1, 2, count)
        held[2] = [over_x_0, over_x_1]
        held[4] = [over_y_0, over_y_1]
        held[6] = [diagonal_0, diagonal_1]
    else:
        for mask in range(2, count, 2):
            held[mask] = [xor_permute(piece, mask, count) for piece in held[0]]
    for mask in range(0, count, 2):
        held[mask + 1] = [xor_permute(piece, 1, count) for piece in held[mask]]
    return [held[mask] for mask in range(count)]


def unfilled(shapes):
    def body(*refs):
        pass

    return pl.pallas_call(
        body,
        out_specs=[pl.BlockSpec(memory_space=pl.ANY)] * len(shapes),
        out_shape=shapes,
        name="unfilled",
    )()


def project(place, counts, features, weight, rows):
    count = len(features)
    pieces = len(features[0])
    lengths = [piece.shape[0] for piece in features[0]]
    width = features[0][0].shape[1]
    columns = weight.shape[1]
    total = count * rows
    bounds = [size for size in variants(total) if size <= lengths[0] + lengths[1]] + [total]

    def body(place_ref, counts_ref, *refs):
        flat = refs[: pieces * count]
        weight_ref = refs[pieces * count]
        out_refs = refs[pieces * count + 1 : (pieces + 1) * count + 1]
        landed, weight_all, sums, sems, weight_sems = refs[(pieces + 1) * count + 1 :]
        used = sum(counts_ref[mask] for mask in range(count)) * BLOCK
        weight_copies = []
        for mask in range(count):
            start = pl.multiple_of((place_ref[0] ^ mask) * width, width)
            copy = pltpu.make_async_copy(
                weight_ref.at[pl.ds(start, width), :], weight_all.at[mask], weight_sems.at[mask]
            )
            copy.start()
            weight_copies.append(copy)
        below = 0
        for size in bounds:

            @pl.when((used > below) & (used <= size))
            def _(size=size):
                copies = []
                for mask in range(count):
                    first = 0
                    for index in range(pieces):
                        length = min(lengths[index], size - first)
                        if length <= 0:
                            break
                        copy = pltpu.make_async_copy(
                            flat[pieces * mask + index].at[:length, :],
                            landed.at[mask, first : first + length, :],
                            sems.at[mask, index],
                        )
                        copy.start()
                        copies.append((mask, copy))
                        first += length
                for mask in range(count):
                    weight_copies[mask].wait()
                    for owner, copy in copies:
                        if owner == mask:
                            copy.wait()
                    part = jnp.dot(
                        landed[mask, :size, :],
                        weight_all[mask],
                        preferred_element_type=jnp.float32,
                    )
                    if mask == 0:
                        sums[:size, :] = part
                    else:
                        sums[:size, :] += part

            below = size
        for mask in range(count):
            position = 0
            for view in range(count):
                position = position + jnp.where(
                    view < (place_ref[0] ^ mask), counts_ref[place_ref[0] ^ view], 0
                )
            moved = sums[rows_at(position * BLOCK, rows), :]
            out_refs[mask][...] = moved.astype(jnp.bfloat16)

    any_spec = pl.BlockSpec(memory_space=pl.ANY)
    flat = [piece for group in features for piece in group]
    return pl.pallas_call(
        body,
        grid_spec=pltpu.PrefetchScalarGridSpec(
            num_scalar_prefetch=2,
            grid=(1,),
            in_specs=[any_spec] * (pieces * count + 1),
            out_specs=[full_spec((rows, columns))] * count,
            scratch_shapes=[
                pltpu.VMEM((count, total, width), jnp.bfloat16),
                pltpu.VMEM((count, width, columns), jnp.bfloat16),
                pltpu.VMEM((total, columns), jnp.float32),
                pltpu.SemaphoreType.DMA((count, pieces)),
                pltpu.SemaphoreType.DMA((count,)),
            ],
        ),
        out_shape=[jax.ShapeDtypeStruct((rows, columns), jnp.bfloat16)] * count,
        compiler_params=params(),
        cost_estimate=pl.CostEstimate(
            flops=total * count * width * columns,
            bytes_accessed=total * count * width,
            transcendentals=0,
        ),
        name="project",
    )(place, counts, *flat, weight)


def assemble(place, block_counts, row_mask, chunks, sizes, count):
    rows = row_mask.shape[1]
    columns = sum(sizes)
    if any(size % HEAD_DIM for size in sizes):
        joined = [
            jnp.concatenate([chunk[mask] for chunk in chunks], axis=1) for mask in range(count)
        ]
        stacked = jnp.stack(joined)[jnp.arange(count) ^ place[0]]
        result = jnp.moveaxis(stacked, 0, 1).reshape(rows, count * columns)
        offsets = jnp.arange(rows, dtype=jnp.int32)
        good = (row_mask[0] == 1) & (offsets // BLOCK < block_counts[0, 0])
        return jnp.where(good[:, None], result, jnp.bfloat16(0.0))

    def body(place_ref, blocks_ref, mask_ref, *refs):
        out_ref = refs[-1]
        good = valid_column(mask_ref, blocks_ref[0, 0]) > 0.5
        for index in range(len(sizes)):
            for mask in range(count):
                start = (place_ref[0] ^ mask) * columns + sum(sizes[:index])
                chosen = pl.ds(pl.multiple_of(start, HEAD_DIM), sizes[index])
                piece = refs[index * count + mask][...]
                out_ref[:, chosen] = jnp.where(good, piece, jnp.bfloat16(0.0))

    return pl.pallas_call(
        body,
        grid_spec=pltpu.PrefetchScalarGridSpec(
            num_scalar_prefetch=2,
            grid=(1,),
            in_specs=[full_spec((1, rows))]
            + [full_spec((rows, size)) for size in sizes for mask in range(count)],
            out_specs=full_spec((rows, count * columns)),
        ),
        out_shape=jax.ShapeDtypeStruct((rows, count * columns), jnp.bfloat16),
        compiler_params=params(),
        cost_estimate=pl.CostEstimate(
            flops=0, bytes_accessed=4 * rows * count * columns, transcendentals=0
        ),
        name="assemble",
    )(place, block_counts, row_mask, *[piece for chunk in chunks for piece in chunk])


def share_counts(block_counts, count):
    counts = block_counts[0]
    step = 1
    while step < count:
        counts = jnp.concatenate([counts, xor_permute(counts, step, count)])
        step *= 2
    most = jnp.sum(counts)[None]
    groups = lax.axis_size("fsdp")
    step = 1
    while step < groups:
        pairs = [(group, group ^ step) for group in range(groups)]
        most = jnp.maximum(most, lax.ppermute(most, "fsdp", pairs))
        step *= 2
    return counts, most[0]


def local(queries, keys, values, out_weight, block_counts, row_mask):
    rows = queries.shape[1]
    count = lax.axis_size("cam")
    total = count * rows
    place_array = jnp.full((1,), lax.axis_index("cam"), jnp.int32)
    columns = out_weight.shape[1] // count
    first = max(HEAD_DIM, -(-columns * 3 // 5 // HEAD_DIM) * HEAD_DIM)
    sizes = [first, columns - first]

    payloads, weights = pack(
        place_array, block_counts, row_mask, queries, keys, values, out_weight, sizes, count
    )
    weights = [lax.all_gather(part, "fsdp", axis=0, tiled=True) for part in weights]
    received = [payloads[0]] + [None] * (count - 1)
    for mask in order(count):
        received[mask] = xor_permute(payloads[mask], mask, count)
    counts, most = share_counts(block_counts, count)
    attended = attend(place_array, counts, received, rows)

    always = total * 3 // 5
    features = gather_features(attended[:always], count)
    rest = attended[always:]
    shapes = [jax.ShapeDtypeStruct((rest.shape[0] // 2, rest.shape[1]), rest.dtype)] * 2 * count
    more = lax.cond(
        most * BLOCK > always,
        lambda part: [piece for pair in gather_features(part, count) for piece in pair],
        lambda part: list(unfilled(shapes)),
        rest,
    )
    features = [features[mask] + more[2 * mask : 2 * mask + 2] for mask in range(count)]
    chunks = []
    for weight in weights:
        pieces = project(place_array, counts, features, weight, rows)
        chunk = [pieces[0]] + [None] * (count - 1)
        for mask in order(count):
            chunk[mask] = xor_permute(pieces[mask], mask, count)
        chunks.append(chunk)
    return assemble(place_array, block_counts, row_mask, chunks, sizes, count)[None]


def solution(mesh):
    in_specs = (
        P("fsdp", "cam", None),
        P("fsdp", "cam", None),
        P("fsdp", "cam", None),
        P("fsdp", None),
        P("fsdp", "cam"),
        P("fsdp", "cam"),
    )
    out_specs = P("fsdp", "cam", None)
    return jax.shard_map(local, mesh=mesh, in_specs=in_specs, out_specs=out_specs, check_vma=False)
```

```python
import math

import jax
import jax.numpy as jnp
from jax import lax
from jax.experimental import pallas as pl
from jax.experimental.pallas import tpu as pltpu
from jax.sharding import PartitionSpec as P

HEAD_DIM = 128
BLOCK = 32
SENTINEL = 32.0
LIMIT = 24.0
QUERY_TILE = 256
UNIT = 128


def params(mebibytes):
    return pltpu.CompilerParams(vmem_limit_bytes=mebibytes * 1024 * 1024)


def order(count):
    return sorted(range(1, count), key=lambda mask: (mask == 1, mask & 1, -bin(mask).count("1")))


def variants(total):
    return sorted({-(-total * tenths // (10 * UNIT)) * UNIT for tenths in (4, 5, 6, 8, 10)})


def full_spec(shape):
    return pl.BlockSpec(shape, lambda i, *_: (0,) * len(shape))


def column_of(row):
    n = row.shape[1]
    diagonal = lax.broadcasted_iota(jnp.int32, (n, n), 0) == lax.broadcasted_iota(
        jnp.int32, (n, n), 1
    )
    return jnp.sum(jnp.where(diagonal, row, 0.0), axis=1, keepdims=True)


def valid_column(mask_ref, blocks):
    rows = mask_ref.shape[1]
    inside = lax.broadcasted_iota(jnp.int32, (1, rows), 1) < blocks * BLOCK
    return column_of(jnp.where((mask_ref[...] == 1) & inside, 1.0, 0.0))


def xor_permute(array, mask, count):
    return lax.ppermute(array, "cam", [(place, place ^ mask) for place in range(count)])


def pack(place, block_counts, row_mask, queries, keys, values, out_weight, sizes, count):
    _, rows, features = queries.shape
    width = features // count
    depth = out_weight.shape[0]
    columns = out_weight.shape[1] // count
    slicing = all(size % HEAD_DIM == 0 for size in sizes)
    chunks = len(sizes) if slicing else 0
    staged = columns if slicing else HEAD_DIM

    def body(place_ref, blocks_ref, mask_ref, q_ref, k_ref, v_ref, w_ref, *refs):
        out_refs = refs[:count]
        weight_refs = refs[count : count + chunks]
        held, key_out, w_held, load_sems, sems, weight_sems = refs[count + chunks :]
        loads = []
        for slot, ref in enumerate((k_ref, q_ref, v_ref)):
            load = pltpu.make_async_copy(ref.at[0], held.at[slot], load_sems.at[slot])
            load.start()
            loads.append(load)
        if chunks:
            start = pl.multiple_of(place_ref[0] * columns, HEAD_DIM)
            load = pltpu.make_async_copy(
                w_ref.at[:, pl.ds(start, columns)], w_held, load_sems.at[3]
            )
            load.start()
            loads.append(load)
        starts = [pl.multiple_of((place_ref[0] ^ m) * width, HEAD_DIM) for m in range(count)]
        good = valid_column(mask_ref, blocks_ref[0, 0]) > 0.5
        copies = []

        def send(source, target, sem):
            copy = pltpu.make_async_copy(source, target, sem)
            copy.start()
            copies.append(copy)

        loads[0].wait()
        for mask in range(count):
            part = held[0, :, pl.ds(starts[mask], width)]
            key_out[mask] = jnp.where(good, part, jnp.bfloat16(SENTINEL))
            send(key_out.at[mask], out_refs[mask].at[1], sems.at[mask, 1])
        for slot, target in ((1, 0), (2, 2)):
            loads[slot].wait()
            for mask in range(count):
                source = held.at[slot, :, pl.ds(starts[mask], width)]
                send(source, out_refs[mask].at[target], sems.at[mask, target])
        if chunks:
            loads[3].wait()
            for index in range(chunks):
                first = sum(sizes[:index])
                source = w_held.at[:, first : first + sizes[index]]
                send(source, weight_refs[index], weight_sems.at[index])
        for copy in copies:
            copy.wait()

    any_spec = pl.BlockSpec(memory_space=pl.ANY)
    weight_shapes = [
        jax.ShapeDtypeStruct((depth, size), jnp.bfloat16) for size in sizes[:chunks]
    ]
    outputs = pl.pallas_call(
        body,
        grid_spec=pltpu.PrefetchScalarGridSpec(
            num_scalar_prefetch=2,
            grid=(1,),
            in_specs=[full_spec((1, rows))] + [any_spec] * 4,
            out_specs=[any_spec] * (count + chunks),
            scratch_shapes=[
                pltpu.VMEM((3, rows, features), jnp.bfloat16),
                pltpu.VMEM((count, rows, width), jnp.bfloat16),
                pltpu.VMEM((depth, staged), jnp.bfloat16),
                pltpu.SemaphoreType.DMA((4,)),
                pltpu.SemaphoreType.DMA((count, 3)),
                pltpu.SemaphoreType.DMA((len(sizes),)),
            ],
        ),
        out_shape=[jax.ShapeDtypeStruct((3, rows, width), jnp.bfloat16)] * count + weight_shapes,
        compiler_params=params(56),
        cost_estimate=pl.CostEstimate(
            flops=0, bytes_accessed=12 * rows * features, transcendentals=0
        ),
        name="pack",
    )(place, block_counts, row_mask, queries, keys, values, out_weight)
    weights = list(outputs[count:])
    if not slicing:
        for index, size in enumerate(sizes):
            start = place[0] * columns + sum(sizes[:index])
            weights.append(lax.dynamic_slice_in_dim(out_weight, start, size, axis=1))
    return list(outputs[:count]), weights


def packed_offsets(place_ref, counts_ref, table, count):
    by_mask, running = [], 0
    for mask in range(count):
        by_mask.append(running)
        table[mask] = running
        running = running + counts_ref[mask] * BLOCK
    by_view, position = [], 0
    for view in range(count):
        by_view.append(position)
        position = position + counts_ref[place_ref[0] ^ view] * BLOCK
    return by_mask, by_view, running


def rows_at(start, size):
    return pl.ds(start if isinstance(start, int) else pl.multiple_of(start, BLOCK), size)


def attend(place, received, rows):
    count = len(received)
    width = received[0].shape[2]
    total = count * rows
    factor = math.log2(math.e) / math.sqrt(HEAD_DIM)

    def body(place_ref, *refs):
        parts = refs[:count]
        out_ref, counts_ref = refs[count : count + 2]
        query_all, key_all, value_all, value_t, result, table = refs[count + 2 :]

        @pl.when(pl.program_id(0) == 0)
        def _():
            value_all[...] = jnp.zeros_like(value_all)
            for mask in range(count):
                blocks = jnp.zeros((1, HEAD_DIM), jnp.float32)
                for first in range(0, rows, BLOCK):
                    row = parts[mask][1, first : first + 16, :].astype(jnp.float32)[:1]
                    blocks = blocks + jnp.where(row < LIMIT, 1.0, 0.0)
                counts_ref[mask] = jnp.max(blocks).astype(jnp.int32)

        by_mask, by_view, used = packed_offsets(place_ref, counts_ref, table, count)

        for mask in range(count):
            where = rows_at(by_mask[mask], rows)
            query_all[where, :] = parts[mask][0]
            key_all[where, :] = parts[mask][1]
            value_all[where, :] = parts[mask][2]
        key_all[rows_at(used, total // 5), :] = jnp.full(
            (total // 5, HEAD_DIM), SENTINEL, jnp.bfloat16
        )
        below = 0
        for size in variants(total):

            @pl.when((used > below) & (used <= size))
            def _(size=size):
                value_t[:, :size] = value_all[:size, :].T
                key_rows = key_all[:size, :]
                bias = jnp.where(key_rows.astype(jnp.float32) > LIMIT, jnp.float32(-1e30), 0.0)
                bias = jnp.concatenate([bias] * (QUERY_TILE // HEAD_DIM), axis=1)

                def tile(index, carry):
                    where = pl.ds(pl.multiple_of(index * QUERY_TILE, QUERY_TILE), QUERY_TILE)
                    scores = lax.dot_general(
                        key_rows,
                        query_all[where, :],
                        (((1,), (1,)), ((), ())),
                        preferred_element_type=jnp.float32,
                    )
                    scores = scores + bias
                    top = jnp.max(scores, axis=0, keepdims=True)
                    raised = jnp.exp2((scores - top) * factor)
                    norm = jnp.sum(raised, axis=0, keepdims=True)
                    summed = jnp.dot(
                        value_t[:, :size],
                        raised.astype(jnp.bfloat16),
                        preferred_element_type=jnp.float32,
                    )
                    result[where, :] = (summed / norm).T.astype(jnp.bfloat16)
                    return carry

                lax.fori_loop(0, (used + QUERY_TILE - 1) // QUERY_TILE, tile, 0)

            below = size
        for view in range(count):
            moved = result[rows_at(table[place_ref[0] ^ view], rows), :]
            out_ref[rows_at(by_view[view], rows), :] = moved

    flops = 4 * total * total * width // 4
    return pl.pallas_call(
        body,
        grid_spec=pltpu.PrefetchScalarGridSpec(
            num_scalar_prefetch=1,
            grid=(width // HEAD_DIM,),
            in_specs=[pl.BlockSpec((3, rows, HEAD_DIM), lambda h, *_: (0, 0, h))] * count,
            out_specs=[
                pl.BlockSpec((total, HEAD_DIM), lambda h, *_: (0, h)),
                pl.BlockSpec(memory_space=pltpu.SMEM),
            ],
            scratch_shapes=[
                pltpu.VMEM((total, HEAD_DIM), jnp.bfloat16),
                pltpu.VMEM((total + total // 5, HEAD_DIM), jnp.bfloat16),
                pltpu.VMEM((total, HEAD_DIM), jnp.bfloat16),
                pltpu.VMEM((HEAD_DIM, total), jnp.bfloat16),
                pltpu.VMEM((total, HEAD_DIM), jnp.bfloat16),
                pltpu.SMEM((count,), jnp.int32),
            ],
        ),
        out_shape=[
            jax.ShapeDtypeStruct((total, width), jnp.bfloat16),
            jax.ShapeDtypeStruct((count,), jnp.int32),
        ],
        compiler_params=params(24),
        cost_estimate=pl.CostEstimate(
            flops=flops, bytes_accessed=8 * total * width, transcendentals=flops // 512
        ),
        name="attend",
    )(place, *received)


def gather_features(own, count):
    half = own.shape[0] // 2
    held = {0: [own[:half], own[half:]]}
    if count == 8:
        over_x_0 = xor_permute(held[0][0], 2, count)
        over_y_1 = xor_permute(held[0][1], 4, count)
        over_x_1 = xor_permute(held[0][1], 2, count)
        over_y_0 = xor_permute(held[0][0], 4, count)
        diagonal_0 = xor_permute(over_x_0, 4, count)
        diagonal_1 = xor_permute(over_y_1, 2, count)
        held[2] = [over_x_0, over_x_1]
        held[4] = [over_y_0, over_y_1]
        held[6] = [diagonal_0, diagonal_1]
    else:
        for mask in range(2, count, 2):
            held[mask] = [xor_permute(piece, mask, count) for piece in held[0]]
    for mask in range(0, count, 2):
        held[mask + 1] = [xor_permute(piece, 1, count) for piece in held[mask]]
    return [held[mask] for mask in range(count)]


def unfilled(shapes):
    def body(*refs):
        pass

    return pl.pallas_call(
        body,
        out_specs=[pl.BlockSpec(memory_space=pl.ANY)] * len(shapes),
        out_shape=shapes,
        name="unfilled",
    )()


def project(place, counts, features, weight, rows):
    count = len(features)
    pieces = len(features[0])
    lengths = [piece.shape[0] for piece in features[0]]
    width = features[0][0].shape[1]
    columns = weight.shape[1]
    total = count * rows
    bounds = [size for size in variants(total) if size <= lengths[0] + lengths[1]] + [total]

    def body(place_ref, counts_ref, *refs):
        flat = refs[: pieces * count]
        weight_ref = refs[pieces * count]
        out_refs = refs[pieces * count + 1 : (pieces + 1) * count + 1]
        landed, weight_all, sums, sems, weight_sems = refs[(pieces + 1) * count + 1 :]
        used = sum(counts_ref[mask] for mask in range(count)) * BLOCK
        weight_copies = []
        for mask in range(count):
            start = pl.multiple_of((place_ref[0] ^ mask) * width, width)
            copy = pltpu.make_async_copy(
                weight_ref.at[pl.ds(start, width), :], weight_all.at[mask], weight_sems.at[mask]
            )
            copy.start()
            weight_copies.append(copy)
        below = 0
        for size in bounds:

            @pl.when((used > below) & (used <= size))
            def _(size=size):
                copies = []
                for mask in range(count):
                    first = 0
                    for index in range(pieces):
                        length = min(lengths[index], size - first)
                        if length <= 0:
                            break
                        copy = pltpu.make_async_copy(
                            flat[pieces * mask + index].at[:length, :],
                            landed.at[mask, first : first + length, :],
                            sems.at[mask, index],
                        )
                        copy.start()
                        copies.append((mask, copy))
                        first += length
                for mask in range(count):
                    weight_copies[mask].wait()
                    for owner, copy in copies:
                        if owner == mask:
                            copy.wait()
                    part = jnp.dot(
                        landed[mask, :size, :],
                        weight_all[mask],
                        preferred_element_type=jnp.float32,
                    )
                    if mask == 0:
                        sums[:size, :] = part
                    else:
                        sums[:size, :] += part

            below = size
        for mask in range(count):
            position = 0
            for view in range(count):
                position = position + jnp.where(
                    view < (place_ref[0] ^ mask), counts_ref[place_ref[0] ^ view], 0
                )
            moved = sums[rows_at(position * BLOCK, rows), :]
            out_refs[mask][...] = moved.astype(jnp.bfloat16)

    any_spec = pl.BlockSpec(memory_space=pl.ANY)
    flat = [piece for group in features for piece in group]
    return pl.pallas_call(
        body,
        grid_spec=pltpu.PrefetchScalarGridSpec(
            num_scalar_prefetch=2,
            grid=(1,),
            in_specs=[any_spec] * (pieces * count + 1),
            out_specs=[full_spec((rows, columns))] * count,
            scratch_shapes=[
                pltpu.VMEM((count, total, width), jnp.bfloat16),
                pltpu.VMEM((count, width, columns), jnp.bfloat16),
                pltpu.VMEM((total, columns), jnp.float32),
                pltpu.SemaphoreType.DMA((count, pieces)),
                pltpu.SemaphoreType.DMA((count,)),
            ],
        ),
        out_shape=[jax.ShapeDtypeStruct((rows, columns), jnp.bfloat16)] * count,
        compiler_params=params(36),
        cost_estimate=pl.CostEstimate(
            flops=total * count * width * columns,
            bytes_accessed=total * count * width,
            transcendentals=0,
        ),
        name="project",
    )(place, counts, *flat, weight)


def assemble(place, block_counts, row_mask, chunks, sizes, count):
    rows = row_mask.shape[1]
    columns = sum(sizes)
    if any(size % HEAD_DIM for size in sizes):
        joined = [
            jnp.concatenate([chunk[mask] for chunk in chunks], axis=1) for mask in range(count)
        ]
        stacked = jnp.stack(joined)[jnp.arange(count) ^ place[0]]
        result = jnp.moveaxis(stacked, 0, 1).reshape(rows, count * columns)
        offsets = jnp.arange(rows, dtype=jnp.int32)
        good = (row_mask[0] == 1) & (offsets // BLOCK < block_counts[0, 0])
        return jnp.where(good[:, None], result, jnp.bfloat16(0.0))

    def body(place_ref, blocks_ref, mask_ref, *refs):
        out_ref = refs[-1]
        good = valid_column(mask_ref, blocks_ref[0, 0]) > 0.5
        for index in range(len(sizes)):
            for mask in range(count):
                start = (place_ref[0] ^ mask) * columns + sum(sizes[:index])
                chosen = pl.ds(pl.multiple_of(start, HEAD_DIM), sizes[index])
                piece = refs[index * count + mask][...]
                out_ref[:, chosen] = jnp.where(good, piece, jnp.bfloat16(0.0))

    return pl.pallas_call(
        body,
        grid_spec=pltpu.PrefetchScalarGridSpec(
            num_scalar_prefetch=2,
            grid=(1,),
            in_specs=[full_spec((1, rows))]
            + [full_spec((rows, size)) for size in sizes for mask in range(count)],
            out_specs=full_spec((rows, count * columns)),
        ),
        out_shape=jax.ShapeDtypeStruct((rows, count * columns), jnp.bfloat16),
        compiler_params=params(16),
        cost_estimate=pl.CostEstimate(
            flops=0, bytes_accessed=4 * rows * count * columns, transcendentals=0
        ),
        name="assemble",
    )(place, block_counts, row_mask, *[piece for chunk in chunks for piece in chunk])


def largest(value):
    groups = lax.axis_size("fsdp")
    step = 1
    while step < groups:
        pairs = [(group, group ^ step) for group in range(groups)]
        value = jnp.maximum(value, lax.ppermute(value, "fsdp", pairs))
        step *= 2
    return value


def local(queries, keys, values, out_weight, block_counts, row_mask):
    rows = queries.shape[1]
    count = lax.axis_size("cam")
    total = count * rows
    place_array = jnp.full((1,), lax.axis_index("cam"), jnp.int32)
    columns = out_weight.shape[1] // count
    sizes = [columns - columns // 5, columns // 5]

    payloads, weights = pack(
        place_array, block_counts, row_mask, queries, keys, values, out_weight, sizes, count
    )
    weights = [lax.all_gather(part, "fsdp", axis=0, tiled=True) for part in weights]
    received = [payloads[0]] + [None] * (count - 1)
    for mask in order(count):
        received[mask] = xor_permute(payloads[mask], mask, count)
    attended, counts = attend(place_array, received, rows)
    most = largest(jnp.sum(counts)[None])[0]

    always = total * 3 // 5
    features = gather_features(attended[:always], count)
    rest = attended[always:]
    features, rest = lax.optimization_barrier((features, rest))
    shapes = [jax.ShapeDtypeStruct((rest.shape[0] // 2, rest.shape[1]), rest.dtype)] * 2 * count
    more = lax.cond(
        most * BLOCK > always,
        lambda part: [piece for pair in gather_features(part, count) for piece in pair],
        lambda part: list(unfilled(shapes)),
        rest,
    )
    features = [features[mask] + more[2 * mask : 2 * mask + 2] for mask in range(count)]
    chunks = []
    for weight in weights:
        pieces = project(place_array, counts, features, weight, rows)
        chunk = [pieces[0]] + [None] * (count - 1)
        for mask in order(count):
            chunk[mask] = xor_permute(pieces[mask], mask, count)
        chunks.append(chunk)
    return assemble(place_array, block_counts, row_mask, chunks, sizes, count)[None]


def solution(mesh):
    in_specs = (
        P("fsdp", "cam", None),
        P("fsdp", "cam", None),
        P("fsdp", "cam", None),
        P("fsdp", None),
        P("fsdp", "cam"),
        P("fsdp", "cam"),
    )
    out_specs = P("fsdp", "cam", None)
    return jax.shard_map(local, mesh=mesh, in_specs=in_specs, out_specs=out_specs, check_vma=False)
```

```python
import math

import jax
import jax.numpy as jnp
from jax import lax
from jax.experimental import pallas as pl
from jax.experimental.pallas import tpu as pltpu
from jax.sharding import PartitionSpec as P

HEAD_DIM = 128
BLOCK = 32
SENTINEL = 32.0
LIMIT = 24.0
UNIT = 128


def params(mebibytes):
    return pltpu.CompilerParams(vmem_limit_bytes=mebibytes * 1024 * 1024)


def order(count):
    return sorted(range(1, count), key=lambda mask: (mask == 1, mask & 1, -bin(mask).count("1")))


def variants(total):
    return sorted({-(-total * tenths // (10 * UNIT)) * UNIT for tenths in (4, 5, 6, 8, 10)})


def full_spec(shape):
    return pl.BlockSpec(shape, lambda i, *_: (0,) * len(shape))


def column_of(row):
    n = row.shape[1]
    diagonal = lax.broadcasted_iota(jnp.int32, (n, n), 0) == lax.broadcasted_iota(
        jnp.int32, (n, n), 1
    )
    return jnp.sum(jnp.where(diagonal, row, 0.0), axis=1, keepdims=True)


def valid_column(mask_ref, blocks):
    rows = mask_ref.shape[1]
    inside = lax.broadcasted_iota(jnp.int32, (1, rows), 1) < blocks * BLOCK
    return column_of(jnp.where((mask_ref[...] == 1) & inside, 1.0, 0.0))


def xor_permute(array, mask, count):
    return lax.ppermute(array, "cam", [(place, place ^ mask) for place in range(count)])


def pack(place, block_counts, row_mask, queries, keys, values, out_weight, sizes, count):
    _, rows, features = queries.shape
    width = features // count
    depth = out_weight.shape[0]
    columns = out_weight.shape[1] // count
    slicing = all(size % HEAD_DIM == 0 for size in sizes)
    chunks = len(sizes) if slicing else 0
    staged = columns if slicing else HEAD_DIM

    def body(place_ref, blocks_ref, mask_ref, q_ref, k_ref, v_ref, w_ref, *refs):
        out_refs = refs[:count]
        weight_refs = refs[count : count + chunks]
        held, key_out, w_held, load_sems, sems, weight_sems = refs[count + chunks :]
        loads = []
        for slot, ref in enumerate((k_ref, q_ref, v_ref)):
            load = pltpu.make_async_copy(ref.at[0], held.at[slot], load_sems.at[slot])
            load.start()
            loads.append(load)
        if chunks:
            start = pl.multiple_of(place_ref[0] * columns, HEAD_DIM)
            load = pltpu.make_async_copy(
                w_ref.at[:, pl.ds(start, columns)], w_held, load_sems.at[3]
            )
            load.start()
            loads.append(load)
        starts = [pl.multiple_of((place_ref[0] ^ m) * width, HEAD_DIM) for m in range(count)]
        good = valid_column(mask_ref, blocks_ref[0, 0]) > 0.5
        copies = []

        def send(source, target, sem):
            copy = pltpu.make_async_copy(source, target, sem)
            copy.start()
            copies.append(copy)

        loads[0].wait()
        for mask in range(count):
            part = held[0, :, pl.ds(starts[mask], width)]
            key_out[mask] = jnp.where(good, part, jnp.bfloat16(SENTINEL))
            send(key_out.at[mask], out_refs[mask].at[1], sems.at[mask, 1])
        for slot, target in ((1, 0), (2, 2)):
            loads[slot].wait()
            for mask in range(count):
                source = held.at[slot, :, pl.ds(starts[mask], width)]
                send(source, out_refs[mask].at[target], sems.at[mask, target])
        if chunks:
            loads[3].wait()
            for index in range(chunks):
                first = sum(sizes[:index])
                source = w_held.at[:, first : first + sizes[index]]
                send(source, weight_refs[index], weight_sems.at[index])
        for copy in copies:
            copy.wait()

    any_spec = pl.BlockSpec(memory_space=pl.ANY)
    weight_shapes = [
        jax.ShapeDtypeStruct((depth, size), jnp.bfloat16) for size in sizes[:chunks]
    ]
    outputs = pl.pallas_call(
        body,
        grid_spec=pltpu.PrefetchScalarGridSpec(
            num_scalar_prefetch=2,
            grid=(1,),
            in_specs=[full_spec((1, rows))] + [any_spec] * 4,
            out_specs=[any_spec] * (count + chunks),
            scratch_shapes=[
                pltpu.VMEM((3, rows, features), jnp.bfloat16),
                pltpu.VMEM((count, rows, width), jnp.bfloat16),
                pltpu.VMEM((depth, staged), jnp.bfloat16),
                pltpu.SemaphoreType.DMA((4,)),
                pltpu.SemaphoreType.DMA((count, 3)),
                pltpu.SemaphoreType.DMA((len(sizes),)),
            ],
        ),
        out_shape=[jax.ShapeDtypeStruct((3, rows, width), jnp.bfloat16)] * count + weight_shapes,
        compiler_params=params(56),
        cost_estimate=pl.CostEstimate(
            flops=0, bytes_accessed=12 * rows * features, transcendentals=0
        ),
        name="pack",
    )(place, block_counts, row_mask, queries, keys, values, out_weight)
    weights = list(outputs[count:])
    if not slicing:
        for index, size in enumerate(sizes):
            start = place[0] * columns + sum(sizes[:index])
            weights.append(lax.dynamic_slice_in_dim(out_weight, start, size, axis=1))
    return list(outputs[:count]), weights


def packed_offsets(place_ref, counts_ref, table, count):
    by_mask, running = [], 0
    for mask in range(count):
        by_mask.append(running)
        table[mask] = running
        running = running + counts_ref[mask] * BLOCK
    by_view, position = [], 0
    for view in range(count):
        by_view.append(position)
        position = position + counts_ref[place_ref[0] ^ view] * BLOCK
    return by_mask, by_view, running


def rows_at(start, size):
    return pl.ds(start if isinstance(start, int) else pl.multiple_of(start, BLOCK), size)


def tile_of(size):
    return max(rows for rows in range(UNIT, 6 * UNIT + 1, UNIT) if size % rows == 0)


def attend(place, received, rows):
    count = len(received)
    width = received[0].shape[2]
    total = count * rows
    span = 2 * HEAD_DIM
    factor = math.log2(math.e) / math.sqrt(HEAD_DIM)

    def body(place_ref, *refs):
        parts = refs[:count]
        out_ref, counts_ref = refs[count : count + 2]
        query_all, key_all, value_all, result, table = refs[count + 2 :]

        @pl.when(pl.program_id(0) == 0)
        def _():
            value_all[...] = jnp.zeros_like(value_all)
            for mask in range(count):
                blocks = jnp.zeros((1, HEAD_DIM), jnp.float32)
                for first in range(0, rows, BLOCK):
                    row = parts[mask][1, first : first + 16, :HEAD_DIM].astype(jnp.float32)[:1]
                    blocks = blocks + jnp.where(row < LIMIT, 1.0, 0.0)
                counts_ref[mask] = jnp.max(blocks).astype(jnp.int32)

        by_mask, by_view, used = packed_offsets(place_ref, counts_ref, table, count)
        for mask in range(count):
            where = rows_at(by_mask[mask], rows)
            query_all[where, :] = parts[mask][0]
            key_all[where, :] = parts[mask][1]
            value_all[where, :] = parts[mask][2]
        key_all[rows_at(used, total // 5), :] = jnp.full((total // 5, span), SENTINEL, jnp.bfloat16)
        below = 0
        for size in variants(total):

            @pl.when((used > below) & (used <= size))
            def _(size=size):
                step = tile_of(size)
                key_mask = key_all[:size, :HEAD_DIM].astype(jnp.float32) > LIMIT
                bias = jnp.where(key_mask, jnp.float32(-1e30), 0.0)
                bias = jnp.concatenate([bias] * (step // HEAD_DIM), axis=1)
                values_t = [
                    value_all[:size, first : first + HEAD_DIM].T
                    for first in range(0, span, HEAD_DIM)
                ]

                def tile(index, carry):
                    if isinstance(index, int):
                        where = pl.ds(index * step, step)
                    else:
                        where = pl.ds(pl.multiple_of(index * step, UNIT), step)
                    for head in range(span // HEAD_DIM):
                        lanes = slice(head * HEAD_DIM, (head + 1) * HEAD_DIM)
                        scores = lax.dot_general(
                            key_all[:size, lanes],
                            query_all[where, lanes],
                            (((1,), (1,)), ((), ())),
                            preferred_element_type=jnp.float32,
                        )
                        scores = scores + bias
                        top = jnp.max(scores, axis=0, keepdims=True)
                        raised = jnp.exp2((scores - top) * factor)
                        norm = jnp.sum(raised, axis=0, keepdims=True)
                        summed = jnp.dot(
                            values_t[head],
                            raised.astype(jnp.bfloat16),
                            preferred_element_type=jnp.float32,
                        )
                        result[where, lanes] = (summed / norm).T.astype(jnp.bfloat16)
                    return carry

                if size == step:
                    tile(0, 0)
                else:
                    lax.fori_loop(0, size // step, tile, 0)

            below = size
        for view in range(count):
            moved = result[rows_at(table[place_ref[0] ^ view], rows), :]
            out_ref[rows_at(by_view[view], rows), :] = moved

    flops = 4 * total * total * width // 4
    return pl.pallas_call(
        body,
        grid_spec=pltpu.PrefetchScalarGridSpec(
            num_scalar_prefetch=1,
            grid=(width // span,),
            in_specs=[pl.BlockSpec((3, rows, span), lambda h, *_: (0, 0, h))] * count,
            out_specs=[
                pl.BlockSpec((total, span), lambda h, *_: (0, h)),
                pl.BlockSpec(memory_space=pltpu.SMEM),
            ],
            scratch_shapes=[
                pltpu.VMEM((total, span), jnp.bfloat16),
                pltpu.VMEM((total + total // 5, span), jnp.bfloat16),
                pltpu.VMEM((total, span), jnp.bfloat16),
                pltpu.VMEM((total, span), jnp.bfloat16),
                pltpu.SMEM((count,), jnp.int32),
            ],
        ),
        out_shape=[
            jax.ShapeDtypeStruct((total, width), jnp.bfloat16),
            jax.ShapeDtypeStruct((count,), jnp.int32),
        ],
        compiler_params=params(40),
        cost_estimate=pl.CostEstimate(
            flops=flops, bytes_accessed=8 * total * width, transcendentals=flops // 512
        ),
        name="attend",
    )(place, *received)


def gather_features(own, count):
    half = own.shape[0] // 2
    held = {0: [own[:half], own[half:]]}
    if count == 8:
        over_x_0 = xor_permute(held[0][0], 2, count)
        over_y_1 = xor_permute(held[0][1], 4, count)
        over_x_1 = xor_permute(held[0][1], 2, count)
        over_y_0 = xor_permute(held[0][0], 4, count)
        diagonal_0 = xor_permute(over_x_0, 4, count)
        diagonal_1 = xor_permute(over_y_1, 2, count)
        held[2] = [over_x_0, over_x_1]
        held[4] = [over_y_0, over_y_1]
        held[6] = [diagonal_0, diagonal_1]
    else:
        for mask in range(2, count, 2):
            held[mask] = [xor_permute(piece, mask, count) for piece in held[0]]
    for mask in range(0, count, 2):
        held[mask + 1] = [xor_permute(piece, 1, count) for piece in held[mask]]
    return [held[mask] for mask in range(count)]


def unfilled(shape):
    def body(out_ref):
        pass

    return pl.pallas_call(
        body,
        out_specs=pl.BlockSpec(memory_space=pl.ANY),
        out_shape=shape,
        name="unfilled",
    )()


def project(place, counts, features, more, weight, rows):
    count = len(features)
    half, width = features[0][0].shape
    extra = more.shape[1]
    columns = weight.shape[1]
    total = count * rows
    bounds = [size for size in variants(total) if size <= 2 * half] + [total]

    def body(place_ref, counts_ref, *refs):
        flat = refs[: 2 * count]
        more_ref, weight_ref = refs[2 * count : 2 * count + 2]
        out_refs = refs[2 * count + 2 : 3 * count + 2]
        landed, weight_all, sums, sems, weight_sems = refs[3 * count + 2 :]
        used = sum(counts_ref[mask] for mask in range(count)) * BLOCK
        weight_copies = []
        for mask in range(count):
            start = pl.multiple_of((place_ref[0] ^ mask) * width, width)
            copy = pltpu.make_async_copy(
                weight_ref.at[pl.ds(start, width), :], weight_all.at[mask], weight_sems.at[mask]
            )
            copy.start()
            weight_copies.append(copy)
        below = 0
        for size in bounds:

            @pl.when((used > below) & (used <= size))
            def _(size=size):
                pieces = [(side * half, min(half, size - side * half)) for side in range(2)]
                copies = []
                if size > 2 * half:
                    for side in range(2):
                        pieces.append((2 * half + side * extra, extra))
                    for mask in range(count):
                        copy = pltpu.make_async_copy(
                            more_ref.at[pl.ds(2 * mask, 2)], landed.at[mask], sems.at[mask]
                        )
                        copy.start()
                        copies.append(copy)
                for mask in range(count):
                    weight_copies[mask].wait()
                    if copies:
                        copies[mask].wait()
                    for side, (first, length) in enumerate(pieces):
                        if side < 2:
                            block = flat[2 * mask + side][:length, :]
                        else:
                            block = landed[mask, side - 2]
                        part = jnp.dot(block, weight_all[mask], preferred_element_type=jnp.float32)
                        if mask == 0:
                            sums[first : first + length, :] = part
                        else:
                            sums[first : first + length, :] += part

            below = size
        for mask in range(count):
            position = 0
            for view in range(count):
                position = position + jnp.where(
                    view < (place_ref[0] ^ mask), counts_ref[place_ref[0] ^ view], 0
                )
            moved = sums[rows_at(position * BLOCK, rows), :]
            out_refs[mask][...] = moved.astype(jnp.bfloat16)

    any_spec = pl.BlockSpec(memory_space=pl.ANY)
    vmem_spec = pl.BlockSpec(memory_space=pltpu.VMEM)
    flat = [
        pltpu.with_memory_space_constraint(piece, pltpu.VMEM)
        for group in features
        for piece in group
    ]
    return pl.pallas_call(
        body,
        grid_spec=pltpu.PrefetchScalarGridSpec(
            num_scalar_prefetch=2,
            grid=(1,),
            in_specs=[vmem_spec] * (2 * count) + [any_spec] * 2,
            out_specs=[full_spec((rows, columns))] * count,
            scratch_shapes=[
                pltpu.VMEM((count, 2, extra, width), jnp.bfloat16),
                pltpu.VMEM((count, width, columns), jnp.bfloat16),
                pltpu.VMEM((total, columns), jnp.float32),
                pltpu.SemaphoreType.DMA((count,)),
                pltpu.SemaphoreType.DMA((count,)),
            ],
        ),
        out_shape=[jax.ShapeDtypeStruct((rows, columns), jnp.bfloat16)] * count,
        compiler_params=params(28),
        cost_estimate=pl.CostEstimate(
            flops=total * count * width * columns,
            bytes_accessed=total * count * width,
            transcendentals=0,
        ),
        name="project",
    )(
        place,
        counts,
        *flat,
        pltpu.with_memory_space_constraint(more, pltpu.HBM),
        pltpu.with_memory_space_constraint(weight, pltpu.HBM),
    )


def assemble(place, block_counts, row_mask, chunks, sizes, count):
    rows = row_mask.shape[1]
    columns = sum(sizes)
    if any(size % HEAD_DIM for size in sizes):
        joined = [
            jnp.concatenate([chunk[mask] for chunk in chunks], axis=1) for mask in range(count)
        ]
        stacked = jnp.stack(joined)[jnp.arange(count) ^ place[0]]
        result = jnp.moveaxis(stacked, 0, 1).reshape(rows, count * columns)
        offsets = jnp.arange(rows, dtype=jnp.int32)
        good = (row_mask[0] == 1) & (offsets // BLOCK < block_counts[0, 0])
        return jnp.where(good[:, None], result, jnp.bfloat16(0.0))

    def body(place_ref, blocks_ref, mask_ref, *refs):
        out_ref = refs[-1]
        good = valid_column(mask_ref, blocks_ref[0, 0]) > 0.5
        for index in range(len(sizes)):
            for mask in range(count):
                start = (place_ref[0] ^ mask) * columns + sum(sizes[:index])
                chosen = pl.ds(pl.multiple_of(start, HEAD_DIM), sizes[index])
                piece = refs[index * count + mask][...]
                out_ref[:, chosen] = jnp.where(good, piece, jnp.bfloat16(0.0))

    return pl.pallas_call(
        body,
        grid_spec=pltpu.PrefetchScalarGridSpec(
            num_scalar_prefetch=2,
            grid=(1,),
            in_specs=[full_spec((1, rows))]
            + [full_spec((rows, size)) for size in sizes for mask in range(count)],
            out_specs=full_spec((rows, count * columns)),
        ),
        out_shape=jax.ShapeDtypeStruct((rows, count * columns), jnp.bfloat16),
        compiler_params=params(16),
        cost_estimate=pl.CostEstimate(
            flops=0, bytes_accessed=4 * rows * count * columns, transcendentals=0
        ),
        name="assemble",
    )(place, block_counts, row_mask, *[piece for chunk in chunks for piece in chunk])


def local(queries, keys, values, out_weight, block_counts, row_mask):
    rows = queries.shape[1]
    count = lax.axis_size("cam")
    total = count * rows
    place_array = jnp.full((1,), lax.axis_index("cam"), jnp.int32)
    columns = out_weight.shape[1] // count
    sizes = [columns - columns // 5, columns // 5]

    payloads, weights = pack(
        place_array, block_counts, row_mask, queries, keys, values, out_weight, sizes, count
    )
    weights = [lax.all_gather(part, "fsdp", axis=0, tiled=True) for part in weights]
    received = [payloads[0]] + [None] * (count - 1)
    for mask in order(count):
        received[mask] = xor_permute(payloads[mask], mask, count)
    attended, counts = attend(place_array, received, rows)

    always = total * 3 // 5
    rest = attended[always:]
    shape = jax.ShapeDtypeStruct((2 * count, rest.shape[0] // 2, rest.shape[1]), rest.dtype)
    more = lax.cond(
        jnp.sum(counts) * BLOCK > always,
        lambda part: jnp.stack([piece for pair in gather_features(part, count) for piece in pair]),
        lambda part: unfilled(shape),
        rest,
    )
    features = gather_features(attended[:always], count)
    chunks = []
    for weight in weights:
        pieces = project(place_array, counts, features, more, weight, rows)
        chunk = [pieces[0]] + [None] * (count - 1)
        for mask in order(count):
            chunk[mask] = xor_permute(pieces[mask], mask, count)
        chunks.append(chunk)
    return assemble(place_array, block_counts, row_mask, chunks, sizes, count)[None]


def solution(mesh):
    in_specs = (
        P("fsdp", "cam", None),
        P("fsdp", "cam", None),
        P("fsdp", "cam", None),
        P("fsdp", None),
        P("fsdp", "cam"),
        P("fsdp", "cam"),
    )
    out_specs = P("fsdp", "cam", None)
    return jax.shard_map(local, mesh=mesh, in_specs=in_specs, out_specs=out_specs, check_vma=False)
```

```python
import math

import jax
import jax.numpy as jnp
from jax import lax
from jax.experimental import pallas as pl
from jax.experimental.pallas import tpu as pltpu
from jax.sharding import PartitionSpec as P

HEAD_DIM = 128
BLOCK = 32
SENTINEL = 32.0
LIMIT = 24.0
UNIT = 128


def params(mebibytes):
    return pltpu.CompilerParams(vmem_limit_bytes=mebibytes * 1024 * 1024)


def order(count):
    return sorted(range(1, count), key=lambda mask: (mask == 1, mask & 1, -bin(mask).count("1")))


def variants(total):
    return sorted({-(-total * tenths // (10 * UNIT)) * UNIT for tenths in (4, 5, 6, 8, 10)})


def full_spec(shape):
    return pl.BlockSpec(shape, lambda i, *_: (0,) * len(shape))


def column_of(row):
    n = row.shape[1]
    diagonal = lax.broadcasted_iota(jnp.int32, (n, n), 0) == lax.broadcasted_iota(
        jnp.int32, (n, n), 1
    )
    return jnp.sum(jnp.where(diagonal, row, 0.0), axis=1, keepdims=True)


def valid_column(mask_ref, blocks):
    rows = mask_ref.shape[1]
    inside = lax.broadcasted_iota(jnp.int32, (1, rows), 1) < blocks * BLOCK
    return column_of(jnp.where((mask_ref[...] == 1) & inside, 1.0, 0.0))


def xor_permute(array, mask, count):
    return lax.ppermute(array, "cam", [(place, place ^ mask) for place in range(count)])


def pack(place, block_counts, row_mask, queries, keys, values, out_weight, count):
    _, rows, features = queries.shape
    width = features // count
    depth = out_weight.shape[0]
    columns = out_weight.shape[1] // count
    slicing = columns % HEAD_DIM == 0
    chunks = 1 if slicing else 0
    staged = columns if slicing else HEAD_DIM

    def body(place_ref, blocks_ref, mask_ref, q_ref, k_ref, v_ref, w_ref, *refs):
        out_refs = refs[:count]
        weight_refs = refs[count : count + chunks]
        held, key_out, w_held, load_sems, sems, weight_sems = refs[count + chunks :]
        loads = []
        for slot, ref in enumerate((k_ref, q_ref, v_ref)):
            load = pltpu.make_async_copy(ref.at[0], held.at[slot], load_sems.at[slot])
            load.start()
            loads.append(load)
        if chunks:
            start = pl.multiple_of(place_ref[0] * columns, HEAD_DIM)
            load = pltpu.make_async_copy(
                w_ref.at[:, pl.ds(start, columns)], w_held, load_sems.at[3]
            )
            load.start()
            loads.append(load)
        starts = [pl.multiple_of((place_ref[0] ^ m) * width, HEAD_DIM) for m in range(count)]
        good = valid_column(mask_ref, blocks_ref[0, 0]) > 0.5
        copies = []

        def send(source, target, sem):
            copy = pltpu.make_async_copy(source, target, sem)
            copy.start()
            copies.append(copy)

        loads[0].wait()
        for mask in range(count):
            part = held[0, :, pl.ds(starts[mask], width)]
            key_out[mask] = jnp.where(good, part, jnp.bfloat16(SENTINEL))
            send(key_out.at[mask], out_refs[mask].at[1], sems.at[mask, 1])
        for slot, target in ((1, 0), (2, 2)):
            loads[slot].wait()
            for mask in range(count):
                source = held.at[slot, :, pl.ds(starts[mask], width)]
                send(source, out_refs[mask].at[target], sems.at[mask, target])
        if chunks:
            loads[3].wait()
            send(w_held, weight_refs[0], weight_sems.at[0])
        for copy in copies:
            copy.wait()

    any_spec = pl.BlockSpec(memory_space=pl.ANY)
    weight_shapes = [jax.ShapeDtypeStruct((depth, columns), jnp.bfloat16)] * chunks
    outputs = pl.pallas_call(
        body,
        grid_spec=pltpu.PrefetchScalarGridSpec(
            num_scalar_prefetch=2,
            grid=(1,),
            in_specs=[full_spec((1, rows))] + [any_spec] * 4,
            out_specs=[any_spec] * (count + chunks),
            scratch_shapes=[
                pltpu.VMEM((3, rows, features), jnp.bfloat16),
                pltpu.VMEM((count, rows, width), jnp.bfloat16),
                pltpu.VMEM((depth, staged), jnp.bfloat16),
                pltpu.SemaphoreType.DMA((4,)),
                pltpu.SemaphoreType.DMA((count, 3)),
                pltpu.SemaphoreType.DMA((1,)),
            ],
        ),
        out_shape=[jax.ShapeDtypeStruct((3, rows, width), jnp.bfloat16)] * count + weight_shapes,
        compiler_params=params(56),
        cost_estimate=pl.CostEstimate(
            flops=0, bytes_accessed=12 * rows * features, transcendentals=0
        ),
        name="pack",
    )(place, block_counts, row_mask, queries, keys, values, out_weight)
    if slicing:
        return list(outputs[:count]), outputs[count]
    start = place[0] * columns
    return list(outputs[:count]), lax.dynamic_slice_in_dim(out_weight, start, columns, axis=1)


def pass_weight(shards, distance):
    groups = lax.axis_size("fsdp")
    for sign in (1, -1):
        pairs = []
        for source in range(groups):
            origin, target = source - sign * (distance - 1), source + sign
            if 0 <= origin < groups and 0 <= target < groups:
                pairs.append((source, target))
        shards[sign * distance] = lax.ppermute(shards[sign * (distance - 1)], "fsdp", pairs)


def packed_offsets(place_ref, counts_ref, table, count):
    by_mask, running = [], 0
    for mask in range(count):
        by_mask.append(running)
        table[mask] = running
        running = running + counts_ref[mask] * BLOCK
    by_view, position = [], 0
    for view in range(count):
        by_view.append(position)
        position = position + counts_ref[place_ref[0] ^ view] * BLOCK
    return by_mask, by_view, running


def rows_at(start, size):
    return pl.ds(start if isinstance(start, int) else pl.multiple_of(start, BLOCK), size)


def tile_of(size):
    return max(rows for rows in range(UNIT, 6 * UNIT + 1, UNIT) if size % rows == 0)


def attend(place, received, rows):
    count = len(received)
    width = received[0].shape[2]
    total = count * rows
    span = 2 * HEAD_DIM
    factor = math.log2(math.e) / math.sqrt(HEAD_DIM)

    def body(place_ref, *refs):
        parts = refs[:count]
        out_ref, counts_ref = refs[count : count + 2]
        query_all, key_all, value_all, result, table = refs[count + 2 :]

        @pl.when(pl.program_id(0) == 0)
        def _():
            value_all[...] = jnp.zeros_like(value_all)
            for mask in range(count):
                blocks = jnp.zeros((1, HEAD_DIM), jnp.float32)
                for first in range(0, rows, BLOCK):
                    row = parts[mask][1, first : first + 16, :HEAD_DIM].astype(jnp.float32)[:1]
                    blocks = blocks + jnp.where(row < LIMIT, 1.0, 0.0)
                counts_ref[mask] = jnp.max(blocks).astype(jnp.int32)

        by_mask, by_view, used = packed_offsets(place_ref, counts_ref, table, count)
        for mask in range(count):
            where = rows_at(by_mask[mask], rows)
            query_all[where, :] = parts[mask][0]
            key_all[where, :] = parts[mask][1]
            value_all[where, :] = parts[mask][2]
        key_all[rows_at(used, total // 5), :] = jnp.full((total // 5, span), SENTINEL, jnp.bfloat16)
        below = 0
        for size in variants(total):

            @pl.when((used > below) & (used <= size))
            def _(size=size):
                step = tile_of(size)
                key_mask = key_all[:size, :HEAD_DIM].astype(jnp.float32) > LIMIT
                bias = jnp.where(key_mask, jnp.float32(-1e30), 0.0)
                bias = jnp.concatenate([bias] * (step // HEAD_DIM), axis=1)
                values_t = [
                    value_all[:size, first : first + HEAD_DIM].T
                    for first in range(0, span, HEAD_DIM)
                ]

                def tile(index, carry):
                    if isinstance(index, int):
                        where = pl.ds(index * step, step)
                    else:
                        where = pl.ds(pl.multiple_of(index * step, UNIT), step)
                    for head in range(span // HEAD_DIM):
                        lanes = slice(head * HEAD_DIM, (head + 1) * HEAD_DIM)
                        scores = lax.dot_general(
                            key_all[:size, lanes],
                            query_all[where, lanes],
                            (((1,), (1,)), ((), ())),
                            preferred_element_type=jnp.float32,
                        )
                        scores = scores + bias
                        top = jnp.max(scores, axis=0, keepdims=True)
                        raised = jnp.exp2((scores - top) * factor)
                        norm = jnp.sum(raised, axis=0, keepdims=True)
                        summed = jnp.dot(
                            values_t[head],
                            raised.astype(jnp.bfloat16),
                            preferred_element_type=jnp.float32,
                        )
                        result[where, lanes] = (summed / norm).T.astype(jnp.bfloat16)
                    return carry

                if size == step:
                    tile(0, 0)
                else:
                    lax.fori_loop(0, size // step, tile, 0)

            below = size
        for view in range(count):
            moved = result[rows_at(table[place_ref[0] ^ view], rows), :]
            out_ref[rows_at(by_view[view], rows), :] = moved

    flops = 4 * total * total * width // 4
    return pl.pallas_call(
        body,
        grid_spec=pltpu.PrefetchScalarGridSpec(
            num_scalar_prefetch=1,
            grid=(width // span,),
            in_specs=[pl.BlockSpec((3, rows, span), lambda h, *_: (0, 0, h))] * count,
            out_specs=[
                pl.BlockSpec((total, span), lambda h, *_: (0, h)),
                pl.BlockSpec(memory_space=pltpu.SMEM),
            ],
            scratch_shapes=[
                pltpu.VMEM((total, span), jnp.bfloat16),
                pltpu.VMEM((total + total // 5, span), jnp.bfloat16),
                pltpu.VMEM((total, span), jnp.bfloat16),
                pltpu.VMEM((total, span), jnp.bfloat16),
                pltpu.SMEM((count,), jnp.int32),
            ],
        ),
        out_shape=[
            jax.ShapeDtypeStruct((total, width), jnp.bfloat16),
            jax.ShapeDtypeStruct((count,), jnp.int32),
        ],
        compiler_params=params(40),
        cost_estimate=pl.CostEstimate(
            flops=flops, bytes_accessed=8 * total * width, transcendentals=flops // 512
        ),
        name="attend",
    )(place, *received)


def gather_features(own, count):
    half = own.shape[0] // 2
    held = {0: [own[:half], own[half:]]}
    if count == 8:
        over_x_0 = xor_permute(held[0][0], 2, count)
        over_y_1 = xor_permute(held[0][1], 4, count)
        over_x_1 = xor_permute(held[0][1], 2, count)
        over_y_0 = xor_permute(held[0][0], 4, count)
        diagonal_0 = xor_permute(over_x_0, 4, count)
        diagonal_1 = xor_permute(over_y_1, 2, count)
        held[2] = [over_x_0, over_x_1]
        held[4] = [over_y_0, over_y_1]
        held[6] = [diagonal_0, diagonal_1]
    else:
        for mask in range(2, count, 2):
            held[mask] = [xor_permute(piece, mask, count) for piece in held[0]]
    for mask in range(0, count, 2):
        held[mask + 1] = [xor_permute(piece, 1, count) for piece in held[mask]]
    return [held[mask] for mask in range(count)]


def unfilled(shape):
    def body(out_ref):
        pass

    return pl.pallas_call(
        body,
        out_specs=pl.BlockSpec(memory_space=pl.ANY),
        out_shape=shape,
        name="unfilled",
    )()


def project(place, group, counts, features, more, shards, first_column, columns, rows):
    count = len(features)
    half, width = features[0][0].shape
    extra = more.shape[1]
    total = count * rows
    distances = sorted(shards)
    each = shards[0].shape[0] // width
    bounds = [size for size in variants(total) if size <= 2 * half] + [total]
    lanes = pl.ds(first_column, columns)

    def body(place_ref, group_ref, counts_ref, *refs):
        flat = refs[: 2 * count]
        more_ref = refs[2 * count]
        shard_refs = refs[2 * count + 1 : 2 * count + 1 + len(distances)]
        out_refs = refs[2 * count + 1 + len(distances) : 3 * count + 1 + len(distances)]
        landed, weight_all, sums, sems, more_sems, weight_sems = refs[
            3 * count + 1 + len(distances) :
        ]
        used = sum(counts_ref[mask] for mask in range(count)) * BLOCK

        def weight_copy(mask, shard_ref):
            owner = place_ref[0] ^ mask
            start = pl.multiple_of((owner % each) * width, width)
            return pltpu.make_async_copy(
                shard_ref.at[pl.ds(start, width), lanes], weight_all.at[mask], weight_sems.at[mask]
            )

        for mask in range(count):
            apart = group_ref[0] - (place_ref[0] ^ mask) // each
            for distance, shard_ref in zip(distances, shard_refs):

                @pl.when(apart == distance)
                def _(mask=mask, shard_ref=shard_ref):
                    weight_copy(mask, shard_ref).start()

        below = 0
        for size in bounds:

            @pl.when((used > below) & (used <= size))
            def _(size=size):
                pieces = [(side * half, min(half, size - side * half)) for side in range(2)]
                copies = []
                for mask in range(count):
                    group_copies = []
                    for side, (first, length) in enumerate(pieces):
                        group_copies.append(
                            pltpu.make_async_copy(
                                flat[2 * mask + side].at[:length, :],
                                landed.at[mask, first : first + length, :],
                                sems.at[mask, side],
                            )
                        )
                    if size > 2 * half:
                        for side in range(2):
                            first = 2 * half + side * extra
                            group_copies.append(
                                pltpu.make_async_copy(
                                    more_ref.at[2 * mask + side],
                                    landed.at[mask, first : first + extra, :],
                                    more_sems.at[mask, side],
                                )
                            )
                    for copy in group_copies:
                        copy.start()
                    copies.append(group_copies)
                for mask in range(count):
                    weight_copy(mask, shard_refs[0]).wait()
                    for copy in copies[mask]:
                        copy.wait()
                    part = jnp.dot(
                        landed[mask, :size, :],
                        weight_all[mask],
                        preferred_element_type=jnp.float32,
                    )
                    if mask == 0:
                        sums[:size, :] = part
                    else:
                        sums[:size, :] += part

            below = size
        for mask in range(count):
            position = 0
            for view in range(count):
                position = position + jnp.where(
                    view < (place_ref[0] ^ mask), counts_ref[place_ref[0] ^ view], 0
                )
            moved = sums[rows_at(position * BLOCK, rows), :]
            out_refs[mask][...] = moved.astype(jnp.bfloat16)

    any_spec = pl.BlockSpec(memory_space=pl.ANY)
    inputs = [piece for pair in features for piece in pair] + [more]
    inputs += [shards[distance] for distance in distances]
    inputs = [pltpu.with_memory_space_constraint(array, pltpu.HBM) for array in inputs]
    return pl.pallas_call(
        body,
        grid_spec=pltpu.PrefetchScalarGridSpec(
            num_scalar_prefetch=3,
            grid=(1,),
            in_specs=[any_spec] * len(inputs),
            out_specs=[full_spec((rows, columns))] * count,
            scratch_shapes=[
                pltpu.VMEM((count, total, width), jnp.bfloat16),
                pltpu.VMEM((count, width, columns), jnp.bfloat16),
                pltpu.VMEM((total, columns), jnp.float32),
                pltpu.SemaphoreType.DMA((count, 2)),
                pltpu.SemaphoreType.DMA((count, 2)),
                pltpu.SemaphoreType.DMA((count,)),
            ],
        ),
        out_shape=[jax.ShapeDtypeStruct((rows, columns), jnp.bfloat16)] * count,
        compiler_params=params(56),
        cost_estimate=pl.CostEstimate(
            flops=total * count * width * columns,
            bytes_accessed=total * count * width,
            transcendentals=0,
        ),
        name="project",
    )(place, group, counts, *inputs)


def assemble(place, block_counts, row_mask, chunks, sizes, count):
    rows = row_mask.shape[1]
    columns = sum(sizes)
    if any(size % HEAD_DIM for size in sizes):
        joined = [
            jnp.concatenate([chunk[mask] for chunk in chunks], axis=1) for mask in range(count)
        ]
        stacked = jnp.stack(joined)[jnp.arange(count) ^ place[0]]
        result = jnp.moveaxis(stacked, 0, 1).reshape(rows, count * columns)
        offsets = jnp.arange(rows, dtype=jnp.int32)
        good = (row_mask[0] == 1) & (offsets // BLOCK < block_counts[0, 0])
        return jnp.where(good[:, None], result, jnp.bfloat16(0.0))

    def body(place_ref, blocks_ref, mask_ref, *refs):
        out_ref = refs[-1]
        good = valid_column(mask_ref, blocks_ref[0, 0]) > 0.5
        for index in range(len(sizes)):
            for mask in range(count):
                start = (place_ref[0] ^ mask) * columns + sum(sizes[:index])
                chosen = pl.ds(pl.multiple_of(start, HEAD_DIM), sizes[index])
                piece = refs[index * count + mask][...]
                out_ref[:, chosen] = jnp.where(good, piece, jnp.bfloat16(0.0))

    return pl.pallas_call(
        body,
        grid_spec=pltpu.PrefetchScalarGridSpec(
            num_scalar_prefetch=2,
            grid=(1,),
            in_specs=[full_spec((1, rows))]
            + [full_spec((rows, size)) for size in sizes for mask in range(count)],
            out_specs=full_spec((rows, count * columns)),
        ),
        out_shape=jax.ShapeDtypeStruct((rows, count * columns), jnp.bfloat16),
        compiler_params=params(16),
        cost_estimate=pl.CostEstimate(
            flops=0, bytes_accessed=4 * rows * count * columns, transcendentals=0
        ),
        name="assemble",
    )(place, block_counts, row_mask, *[piece for chunk in chunks for piece in chunk])


def local(queries, keys, values, out_weight, block_counts, row_mask):
    rows = queries.shape[1]
    count = lax.axis_size("cam")
    total = count * rows
    place_array = jnp.full((1,), lax.axis_index("cam"), jnp.int32)
    group_array = jnp.full((1,), lax.axis_index("fsdp"), jnp.int32)
    columns = out_weight.shape[1] // count
    first = max(HEAD_DIM, columns * 3 // 5 // HEAD_DIM * HEAD_DIM)
    sizes = [first, columns - first]

    payloads, weight_part = pack(
        place_array, block_counts, row_mask, queries, keys, values, out_weight, count
    )
    shards = {0: weight_part}
    pass_weight(shards, 1)
    received = [payloads[0]] + [None] * (count - 1)
    for mask in order(count):
        if mask == 1:
            payloads[1], shards[1], shards[-1] = lax.optimization_barrier(
                (payloads[1], shards[1], shards[-1])
            )
            pass_weight(shards, 2)
        received[mask] = xor_permute(payloads[mask], mask, count)
    attended, counts = attend(place_array, received, rows)
    attended, shards[2], shards[-2] = lax.optimization_barrier((attended, shards[2], shards[-2]))
    for distance in range(3, lax.axis_size("fsdp")):
        pass_weight(shards, distance)

    always = total * 3 // 5
    rest = attended[always:]
    shape = jax.ShapeDtypeStruct((2 * count, rest.shape[0] // 2, rest.shape[1]), rest.dtype)
    more = lax.cond(
        jnp.sum(counts) * BLOCK > always,
        lambda part: jnp.stack([piece for pair in gather_features(part, count) for piece in pair]),
        lambda part: unfilled(shape),
        rest,
    )
    features = gather_features(attended[:always], count)
    chunks = []
    for index, size in enumerate(sizes):
        start = sum(sizes[:index])
        pieces = project(
            place_array, group_array, counts, features, more, shards, start, size, rows
        )
        chunk = [pieces[0]] + [None] * (count - 1)
        for mask in order(count):
            chunk[mask] = xor_permute(pieces[mask], mask, count)
        chunks.append(chunk)
    return assemble(place_array, block_counts, row_mask, chunks, sizes, count)[None]


def solution(mesh):
    in_specs = (
        P("fsdp", "cam", None),
        P("fsdp", "cam", None),
        P("fsdp", "cam", None),
        P("fsdp", None),
        P("fsdp", "cam"),
        P("fsdp", "cam"),
    )
    out_specs = P("fsdp", "cam", None)
    return jax.shard_map(local, mesh=mesh, in_specs=in_specs, out_specs=out_specs, check_vma=False)
```

```python
import math

import jax
import jax.numpy as jnp
from jax import lax
from jax.experimental import pallas as pl
from jax.experimental.pallas import tpu as pltpu
from jax.sharding import PartitionSpec as P

HEAD_DIM = 128
BLOCK = 32
SENTINEL = 32.0
LIMIT = 24.0
UNIT = 128


def params(mebibytes):
    return pltpu.CompilerParams(vmem_limit_bytes=mebibytes * 1024 * 1024)


def order(count):
    return sorted(range(1, count), key=lambda mask: (mask == 1, mask & 1, -bin(mask).count("1")))


def variants(total):
    return sorted({-(-total * tenths // (10 * UNIT)) * UNIT for tenths in (4, 5, 6, 8, 10)})


def full_spec(shape):
    return pl.BlockSpec(shape, lambda i, *_: (0,) * len(shape))


def column_of(row):
    n = row.shape[1]
    diagonal = lax.broadcasted_iota(jnp.int32, (n, n), 0) == lax.broadcasted_iota(
        jnp.int32, (n, n), 1
    )
    return jnp.sum(jnp.where(diagonal, row, 0.0), axis=1, keepdims=True)


def valid_column(mask_ref, blocks):
    rows = mask_ref.shape[1]
    inside = lax.broadcasted_iota(jnp.int32, (1, rows), 1) < blocks * BLOCK
    return column_of(jnp.where((mask_ref[...] == 1) & inside, 1.0, 0.0))


def xor_permute(array, mask, count):
    return lax.ppermute(array, "cam", [(place, place ^ mask) for place in range(count)])


def pack(place, block_counts, row_mask, queries, keys, values, out_weight, count):
    _, rows, features = queries.shape
    width = features // count
    depth = out_weight.shape[0]
    columns = out_weight.shape[1] // count
    slicing = columns % HEAD_DIM == 0
    chunks = 1 if slicing else 0
    staged = columns if slicing else HEAD_DIM

    def body(place_ref, blocks_ref, mask_ref, q_ref, k_ref, v_ref, w_ref, *refs):
        out_refs = refs[:count]
        weight_refs = refs[count : count + chunks]
        held, key_out, w_held, load_sems, sems, weight_sems = refs[count + chunks :]
        loads = []
        for slot, ref in enumerate((k_ref, q_ref, v_ref)):
            load = pltpu.make_async_copy(ref.at[0], held.at[slot], load_sems.at[slot])
            load.start()
            loads.append(load)
        if chunks:
            start = pl.multiple_of(place_ref[0] * columns, HEAD_DIM)
            load = pltpu.make_async_copy(
                w_ref.at[:, pl.ds(start, columns)], w_held, load_sems.at[3]
            )
            load.start()
            loads.append(load)
        starts = [pl.multiple_of((place_ref[0] ^ m) * width, HEAD_DIM) for m in range(count)]
        good = valid_column(mask_ref, blocks_ref[0, 0]) > 0.5
        copies = []

        def send(source, target, sem):
            copy = pltpu.make_async_copy(source, target, sem)
            copy.start()
            copies.append(copy)

        loads[0].wait()
        for mask in range(count):
            part = held[0, :, pl.ds(starts[mask], width)]
            key_out[mask] = jnp.where(good, part, jnp.bfloat16(SENTINEL))
            send(key_out.at[mask], out_refs[mask].at[1], sems.at[mask, 1])
        for slot, target in ((1, 0), (2, 2)):
            loads[slot].wait()
            for mask in range(count):
                source = held.at[slot, :, pl.ds(starts[mask], width)]
                send(source, out_refs[mask].at[target], sems.at[mask, target])
        if chunks:
            loads[3].wait()
            send(w_held, weight_refs[0], weight_sems.at[0])
        for copy in copies:
            copy.wait()

    any_spec = pl.BlockSpec(memory_space=pl.ANY)
    weight_shapes = [jax.ShapeDtypeStruct((depth, columns), jnp.bfloat16)] * chunks
    outputs = pl.pallas_call(
        body,
        grid_spec=pltpu.PrefetchScalarGridSpec(
            num_scalar_prefetch=2,
            grid=(1,),
            in_specs=[full_spec((1, rows))] + [any_spec] * 4,
            out_specs=[any_spec] * (count + chunks),
            scratch_shapes=[
                pltpu.VMEM((3, rows, features), jnp.bfloat16),
                pltpu.VMEM((count, rows, width), jnp.bfloat16),
                pltpu.VMEM((depth, staged), jnp.bfloat16),
                pltpu.SemaphoreType.DMA((4,)),
                pltpu.SemaphoreType.DMA((count, 3)),
                pltpu.SemaphoreType.DMA((1,)),
            ],
        ),
        out_shape=[jax.ShapeDtypeStruct((3, rows, width), jnp.bfloat16)] * count + weight_shapes,
        compiler_params=params(56),
        cost_estimate=pl.CostEstimate(
            flops=0, bytes_accessed=12 * rows * features, transcendentals=0
        ),
        name="pack",
    )(place, block_counts, row_mask, queries, keys, values, out_weight)
    if slicing:
        return list(outputs[:count]), outputs[count]
    start = place[0] * columns
    return list(outputs[:count]), lax.dynamic_slice_in_dim(out_weight, start, columns, axis=1)


def pass_weight(shards, distance):
    groups = lax.axis_size("fsdp")
    for sign in (1, -1):
        pairs = []
        for source in range(groups):
            origin, target = source - sign * (distance - 1), source + sign
            if 0 <= origin < groups and 0 <= target < groups:
                pairs.append((source, target))
        shards[sign * distance] = lax.ppermute(shards[sign * (distance - 1)], "fsdp", pairs)


def packed_offsets(place_ref, counts_ref, table, count):
    by_mask, running = [], 0
    for mask in range(count):
        by_mask.append(running)
        table[mask] = running
        running = running + counts_ref[mask] * BLOCK
    by_view, position = [], 0
    for view in range(count):
        by_view.append(position)
        position = position + counts_ref[place_ref[0] ^ view] * BLOCK
    return by_mask, by_view, running


def rows_at(start, size):
    return pl.ds(start if isinstance(start, int) else pl.multiple_of(start, BLOCK), size)


def tile_of(size):
    return max(rows for rows in range(UNIT, 6 * UNIT + 1, UNIT) if size % rows == 0)


def attend(place, received, rows):
    count = len(received)
    width = received[0].shape[2]
    total = count * rows
    span = 2 * HEAD_DIM
    factor = math.log2(math.e) / math.sqrt(HEAD_DIM)

    def body(place_ref, *refs):
        parts = refs[:count]
        out_ref, counts_ref = refs[count : count + 2]
        query_all, key_all, value_all, result, table = refs[count + 2 :]

        @pl.when(pl.program_id(0) == 0)
        def _():
            value_all[...] = jnp.zeros_like(value_all)
            for mask in range(count):
                blocks = jnp.zeros((1, HEAD_DIM), jnp.float32)
                for first in range(0, rows, BLOCK):
                    row = parts[mask][1, first : first + 16, :HEAD_DIM].astype(jnp.float32)[:1]
                    blocks = blocks + jnp.where(row < LIMIT, 1.0, 0.0)
                counts_ref[mask] = jnp.max(blocks).astype(jnp.int32)

        by_mask, by_view, used = packed_offsets(place_ref, counts_ref, table, count)
        for mask in range(count):
            where = rows_at(by_mask[mask], rows)
            query_all[where, :] = parts[mask][0]
            key_all[where, :] = parts[mask][1]
            value_all[where, :] = parts[mask][2]
        key_all[rows_at(used, total // 5), :] = jnp.full((total // 5, span), SENTINEL, jnp.bfloat16)
        below = 0
        for size in variants(total):

            @pl.when((used > below) & (used <= size))
            def _(size=size):
                step = tile_of(size)
                key_mask = key_all[:size, :HEAD_DIM].astype(jnp.float32) > LIMIT
                bias = jnp.where(key_mask, jnp.float32(-1e30), 0.0)
                bias = jnp.concatenate([bias] * (step // HEAD_DIM), axis=1)
                values_t = [
                    value_all[:size, first : first + HEAD_DIM].T
                    for first in range(0, span, HEAD_DIM)
                ]

                def tile(index, carry):
                    if isinstance(index, int):
                        where = pl.ds(index * step, step)
                    else:
                        where = pl.ds(pl.multiple_of(index * step, UNIT), step)
                    for head in range(span // HEAD_DIM):
                        lanes = slice(head * HEAD_DIM, (head + 1) * HEAD_DIM)
                        scores = lax.dot_general(
                            key_all[:size, lanes],
                            query_all[where, lanes],
                            (((1,), (1,)), ((), ())),
                            preferred_element_type=jnp.float32,
                        )
                        scores = scores + bias
                        top = jnp.max(scores, axis=0, keepdims=True)
                        raised = jnp.exp2((scores - top) * factor)
                        norm = jnp.sum(raised, axis=0, keepdims=True)
                        summed = jnp.dot(
                            values_t[head],
                            raised.astype(jnp.bfloat16),
                            preferred_element_type=jnp.float32,
                        )
                        result[where, lanes] = (summed / norm).T.astype(jnp.bfloat16)
                    return carry

                if size == step:
                    tile(0, 0)
                else:
                    lax.fori_loop(0, size // step, tile, 0)

            below = size
        for view in range(count):
            moved = result[rows_at(table[place_ref[0] ^ view], rows), :]
            out_ref[rows_at(by_view[view], rows), :] = moved

    flops = 4 * total * total * width // 4
    return pl.pallas_call(
        body,
        grid_spec=pltpu.PrefetchScalarGridSpec(
            num_scalar_prefetch=1,
            grid=(width // span,),
            in_specs=[pl.BlockSpec((3, rows, span), lambda h, *_: (0, 0, h))] * count,
            out_specs=[
                pl.BlockSpec((total, span), lambda h, *_: (0, h)),
                pl.BlockSpec(memory_space=pltpu.SMEM),
            ],
            scratch_shapes=[
                pltpu.VMEM((total, span), jnp.bfloat16),
                pltpu.VMEM((total + total // 5, span), jnp.bfloat16),
                pltpu.VMEM((total, span), jnp.bfloat16),
                pltpu.VMEM((total, span), jnp.bfloat16),
                pltpu.SMEM((count,), jnp.int32),
            ],
        ),
        out_shape=[
            jax.ShapeDtypeStruct((total, width), jnp.bfloat16),
            jax.ShapeDtypeStruct((count,), jnp.int32),
        ],
        compiler_params=params(40),
        cost_estimate=pl.CostEstimate(
            flops=flops, bytes_accessed=8 * total * width, transcendentals=flops // 512
        ),
        name="attend",
    )(place, *received)


def gather_features(own, count, beside=()):
    half = own.shape[0] // 2
    held = {0: [own[:half], own[half:]]}
    if count == 8:
        over_x_0 = xor_permute(held[0][0], 2, count)
        over_y_1 = xor_permute(held[0][1], 4, count)
        over_x_1 = xor_permute(held[0][1], 2, count)
        over_y_0 = xor_permute(held[0][0], 4, count)
        diagonal_0 = xor_permute(over_x_0, 4, count)
        diagonal_1 = xor_permute(over_y_1, 2, count)
        held[2] = [over_x_0, over_x_1]
        held[4] = [over_y_0, over_y_1]
        held[6] = [diagonal_0, diagonal_1]
    else:
        for mask in range(2, count, 2):
            held[mask] = [xor_permute(piece, mask, count) for piece in held[0]]
    if beside:
        held[count - 2], beside = lax.optimization_barrier((held[count - 2], beside))
    for mask in range(0, count, 2):
        held[mask + 1] = [xor_permute(piece, 1, count) for piece in held[mask]]
    return [held[mask] for mask in range(count)], beside


def unfilled(shape):
    def body(out_ref):
        pass

    return pl.pallas_call(
        body,
        out_specs=pl.BlockSpec(memory_space=pl.ANY),
        out_shape=shape,
        name="unfilled",
    )()


def project(place, group, counts, features, more, shards, rows):
    count = len(features)
    half, width = features[0][0].shape
    extra = more.shape[1]
    total = count * rows
    distances = sorted(shards)
    columns = shards[0].shape[1]
    each = shards[0].shape[0] // width
    bounds = [size for size in variants(total) if size <= 2 * half] + [total]

    def body(place_ref, group_ref, counts_ref, *refs):
        flat = refs[: 2 * count]
        more_ref = refs[2 * count]
        shard_refs = refs[2 * count + 1 : 2 * count + 1 + len(distances)]
        out_refs = refs[2 * count + 1 + len(distances) : 3 * count + 1 + len(distances)]
        landed, weight_all, sums, sems, more_sems, weight_sems = refs[
            3 * count + 1 + len(distances) :
        ]
        used = sum(counts_ref[mask] for mask in range(count)) * BLOCK

        def weight_copy(mask, shard_ref):
            owner = place_ref[0] ^ mask
            start = pl.multiple_of((owner % each) * width, width)
            return pltpu.make_async_copy(
                shard_ref.at[pl.ds(start, width), :], weight_all.at[mask], weight_sems.at[mask]
            )

        for mask in range(count):
            apart = group_ref[0] - (place_ref[0] ^ mask) // each
            for distance, shard_ref in zip(distances, shard_refs):

                @pl.when(apart == distance)
                def _(mask=mask, shard_ref=shard_ref):
                    weight_copy(mask, shard_ref).start()

        below = 0
        for size in bounds:

            @pl.when((used > below) & (used <= size))
            def _(size=size):
                pieces = [(side * half, min(half, size - side * half)) for side in range(2)]
                copies = []
                for mask in range(count):
                    group_copies = []
                    for side, (first, length) in enumerate(pieces):
                        group_copies.append(
                            pltpu.make_async_copy(
                                flat[2 * mask + side].at[:length, :],
                                landed.at[mask, first : first + length, :],
                                sems.at[mask, side],
                            )
                        )
                    if size > 2 * half:
                        for side in range(2):
                            first = 2 * half + side * extra
                            group_copies.append(
                                pltpu.make_async_copy(
                                    more_ref.at[2 * mask + side],
                                    landed.at[mask, first : first + extra, :],
                                    more_sems.at[mask, side],
                                )
                            )
                    for copy in group_copies:
                        copy.start()
                    copies.append(group_copies)
                for mask in range(count):
                    weight_copy(mask, shard_refs[0]).wait()
                    for copy in copies[mask]:
                        copy.wait()
                    part = jnp.dot(
                        landed[mask, :size, :],
                        weight_all[mask],
                        preferred_element_type=jnp.float32,
                    )
                    if mask == 0:
                        sums[:size, :] = part
                    else:
                        sums[:size, :] += part

            below = size
        for mask in range(count):
            position = 0
            for view in range(count):
                position = position + jnp.where(
                    view < (place_ref[0] ^ mask), counts_ref[place_ref[0] ^ view], 0
                )
            moved = sums[rows_at(position * BLOCK, rows), :]
            out_refs[mask][...] = moved.astype(jnp.bfloat16)

    any_spec = pl.BlockSpec(memory_space=pl.ANY)
    inputs = [piece for pair in features for piece in pair] + [more]
    inputs += [shards[distance] for distance in distances]
    inputs = [pltpu.with_memory_space_constraint(array, pltpu.HBM) for array in inputs]
    return pl.pallas_call(
        body,
        grid_spec=pltpu.PrefetchScalarGridSpec(
            num_scalar_prefetch=3,
            grid=(1,),
            in_specs=[any_spec] * len(inputs),
            out_specs=[full_spec((rows, columns))] * count,
            scratch_shapes=[
                pltpu.VMEM((count, total, width), jnp.bfloat16),
                pltpu.VMEM((count, width, columns), jnp.bfloat16),
                pltpu.VMEM((total, columns), jnp.float32),
                pltpu.SemaphoreType.DMA((count, 2)),
                pltpu.SemaphoreType.DMA((count, 2)),
                pltpu.SemaphoreType.DMA((count,)),
            ],
        ),
        out_shape=[jax.ShapeDtypeStruct((rows, columns), jnp.bfloat16)] * count,
        compiler_params=params(56),
        cost_estimate=pl.CostEstimate(
            flops=total * count * width * columns,
            bytes_accessed=total * count * width,
            transcendentals=0,
        ),
        name="project",
    )(place, group, counts, *inputs)


def assemble(place, block_counts, row_mask, pieces, count):
    rows, columns = pieces[0].shape
    if columns % HEAD_DIM:
        stacked = jnp.stack(pieces)[jnp.arange(count) ^ place[0]]
        result = jnp.moveaxis(stacked, 0, 1).reshape(rows, count * columns)
        offsets = jnp.arange(rows, dtype=jnp.int32)
        good = (row_mask[0] == 1) & (offsets // BLOCK < block_counts[0, 0])
        return jnp.where(good[:, None], result, jnp.bfloat16(0.0))

    def body(place_ref, blocks_ref, mask_ref, *refs):
        out_ref = refs[-1]
        good = valid_column(mask_ref, blocks_ref[0, 0]) > 0.5
        for mask in range(count):
            start = pl.multiple_of((place_ref[0] ^ mask) * columns, HEAD_DIM)
            out_ref[:, pl.ds(start, columns)] = jnp.where(
                good, refs[mask][...], jnp.bfloat16(0.0)
            )

    return pl.pallas_call(
        body,
        grid_spec=pltpu.PrefetchScalarGridSpec(
            num_scalar_prefetch=2,
            grid=(1,),
            in_specs=[full_spec((1, rows))] + [full_spec((rows, columns))] * count,
            out_specs=full_spec((rows, count * columns)),
        ),
        out_shape=jax.ShapeDtypeStruct((rows, count * columns), jnp.bfloat16),
        compiler_params=params(16),
        cost_estimate=pl.CostEstimate(
            flops=0, bytes_accessed=4 * rows * count * columns, transcendentals=0
        ),
        name="assemble",
    )(place, block_counts, row_mask, *pieces)


def local(queries, keys, values, out_weight, block_counts, row_mask):
    rows = queries.shape[1]
    count = lax.axis_size("cam")
    total = count * rows
    place_array = jnp.full((1,), lax.axis_index("cam"), jnp.int32)
    group_array = jnp.full((1,), lax.axis_index("fsdp"), jnp.int32)

    payloads, weight_part = pack(
        place_array, block_counts, row_mask, queries, keys, values, out_weight, count
    )
    shards = {0: weight_part}
    groups = lax.axis_size("fsdp")

    received = [payloads[0]] + [None] * (count - 1)
    early = [mask for mask in order(count) if mask & 1 == 0]
    late = [mask for mask in order(count) if mask & 1]
    pass_weight(shards, 1)
    for mask in early:
        received[mask] = xor_permute(payloads[mask], mask, count)
    received, payloads, shards[1], shards[-1] = lax.optimization_barrier(
        (received, payloads, shards[1], shards[-1])
    )
    pass_weight(shards, 2)
    for mask in late:
        received[mask] = xor_permute(payloads[mask], mask, count)
    attended, counts = attend(place_array, received, rows)
    attended, shards[2], shards[-2] = lax.optimization_barrier((attended, shards[2], shards[-2]))
    pass_weight(shards, 3)

    always = total * 3 // 5
    rest = attended[always:]
    shape = jax.ShapeDtypeStruct((2 * count, rest.shape[0] // 2, rest.shape[1]), rest.dtype)
    more = lax.cond(
        jnp.sum(counts) * BLOCK > always,
        lambda part: jnp.stack([p for pair in gather_features(part, count)[0] for p in pair]),
        lambda part: unfilled(shape),
        rest,
    )
    features, (shards[3], shards[-3]) = gather_features(
        attended[:always], count, (shards[3], shards[-3])
    )
    for distance in range(4, groups):
        pass_weight(shards, distance)
    pieces = project(place_array, group_array, counts, features, more, shards, rows)
    landed = [pieces[0]] + [None] * (count - 1)
    for mask in order(count):
        landed[mask] = xor_permute(pieces[mask], mask, count)
    return assemble(place_array, block_counts, row_mask, landed, count)[None]


def solution(mesh):
    in_specs = (
        P("fsdp", "cam", None),
        P("fsdp", "cam", None),
        P("fsdp", "cam", None),
        P("fsdp", None),
        P("fsdp", "cam"),
        P("fsdp", "cam"),
    )
    out_specs = P("fsdp", "cam", None)
    return jax.shard_map(local, mesh=mesh, in_specs=in_specs, out_specs=out_specs, check_vma=False)
```

```python
import math

import jax
import jax.numpy as jnp
from jax import lax
from jax.experimental import pallas as pl
from jax.experimental.pallas import tpu as pltpu
from jax.sharding import PartitionSpec as P

HEAD_DIM = 128
BLOCK = 32
SENTINEL = 32.0
LIMIT = 24.0
UNIT = 128


def params(mebibytes):
    return pltpu.CompilerParams(vmem_limit_bytes=mebibytes * 1024 * 1024)


def order(count):
    return sorted(range(1, count), key=lambda mask: (mask == 1, mask & 1, -bin(mask).count("1")))


def variants(total):
    return sorted({-(-total * tenths // (10 * UNIT)) * UNIT for tenths in (4, 5, 6, 8, 10)})


def full_spec(shape):
    return pl.BlockSpec(shape, lambda i, *_: (0,) * len(shape))


def column_of(row):
    n = row.shape[1]
    diagonal = lax.broadcasted_iota(jnp.int32, (n, n), 0) == lax.broadcasted_iota(
        jnp.int32, (n, n), 1
    )
    return jnp.sum(jnp.where(diagonal, row, 0.0), axis=1, keepdims=True)


def valid_column(mask_ref, blocks):
    rows = mask_ref.shape[1]
    inside = lax.broadcasted_iota(jnp.int32, (1, rows), 1) < blocks * BLOCK
    return column_of(jnp.where((mask_ref[...] == 1) & inside, 1.0, 0.0))


def xor_permute(array, mask, count):
    return lax.ppermute(array, "cam", [(place, place ^ mask) for place in range(count)])


def pack(place, block_counts, row_mask, queries, keys, values, out_weight, count):
    _, rows, features = queries.shape
    width = features // count
    depth = out_weight.shape[0]
    columns = out_weight.shape[1] // count
    slicing = columns % HEAD_DIM == 0
    chunks = 1 if slicing else 0
    staged = columns if slicing else HEAD_DIM

    def body(place_ref, blocks_ref, mask_ref, q_ref, k_ref, v_ref, w_ref, *refs):
        out_refs = refs[:count]
        weight_refs = refs[count : count + chunks]
        held, key_out, w_held, load_sems, sems, weight_sems = refs[count + chunks :]
        loads = []
        for slot, ref in enumerate((k_ref, q_ref, v_ref)):
            load = pltpu.make_async_copy(ref.at[0], held.at[slot], load_sems.at[slot])
            load.start()
            loads.append(load)
        if chunks:
            start = pl.multiple_of(place_ref[0] * columns, HEAD_DIM)
            load = pltpu.make_async_copy(
                w_ref.at[:, pl.ds(start, columns)], w_held, load_sems.at[3]
            )
            load.start()
            loads.append(load)
        starts = [pl.multiple_of((place_ref[0] ^ m) * width, HEAD_DIM) for m in range(count)]
        good = valid_column(mask_ref, blocks_ref[0, 0]) > 0.5
        copies = []

        def send(source, target, sem):
            copy = pltpu.make_async_copy(source, target, sem)
            copy.start()
            copies.append(copy)

        loads[0].wait()
        for mask in range(count):
            part = held[0, :, pl.ds(starts[mask], width)]
            key_out[mask] = jnp.where(good, part, jnp.bfloat16(SENTINEL))
            send(key_out.at[mask], out_refs[mask].at[1], sems.at[mask, 1])
        for slot, target in ((1, 0), (2, 2)):
            loads[slot].wait()
            for mask in range(count):
                source = held.at[slot, :, pl.ds(starts[mask], width)]
                send(source, out_refs[mask].at[target], sems.at[mask, target])
        if chunks:
            loads[3].wait()
            send(w_held, weight_refs[0], weight_sems.at[0])
        for copy in copies:
            copy.wait()

    any_spec = pl.BlockSpec(memory_space=pl.ANY)
    weight_shapes = [jax.ShapeDtypeStruct((depth, columns), jnp.bfloat16)] * chunks
    outputs = pl.pallas_call(
        body,
        grid_spec=pltpu.PrefetchScalarGridSpec(
            num_scalar_prefetch=2,
            grid=(1,),
            in_specs=[full_spec((1, rows))] + [any_spec] * 4,
            out_specs=[any_spec] * (count + chunks),
            scratch_shapes=[
                pltpu.VMEM((3, rows, features), jnp.bfloat16),
                pltpu.VMEM((count, rows, width), jnp.bfloat16),
                pltpu.VMEM((depth, staged), jnp.bfloat16),
                pltpu.SemaphoreType.DMA((4,)),
                pltpu.SemaphoreType.DMA((count, 3)),
                pltpu.SemaphoreType.DMA((1,)),
            ],
        ),
        out_shape=[jax.ShapeDtypeStruct((3, rows, width), jnp.bfloat16)] * count + weight_shapes,
        compiler_params=params(56),
        cost_estimate=pl.CostEstimate(
            flops=0, bytes_accessed=12 * rows * features, transcendentals=0
        ),
        name="pack",
    )(place, block_counts, row_mask, queries, keys, values, out_weight)
    if slicing:
        return list(outputs[:count]), outputs[count]
    start = place[0] * columns
    return list(outputs[:count]), lax.dynamic_slice_in_dim(out_weight, start, columns, axis=1)


def pass_weight(shards, distance):
    groups = lax.axis_size("fsdp")
    for sign in (1, -1):
        pairs = []
        for source in range(groups):
            origin, target = source - sign * (distance - 1), source + sign
            if 0 <= origin < groups and 0 <= target < groups:
                pairs.append((source, target))
        shards[sign * distance] = lax.ppermute(shards[sign * (distance - 1)], "fsdp", pairs)


def packed_offsets(place_ref, counts_ref, table, count):
    by_mask, running = [], 0
    for mask in range(count):
        by_mask.append(running)
        table[mask] = running
        running = running + counts_ref[mask] * BLOCK
    by_view, position = [], 0
    for view in range(count):
        by_view.append(position)
        position = position + counts_ref[place_ref[0] ^ view] * BLOCK
    return by_mask, by_view, running


def rows_at(start, size):
    return pl.ds(start if isinstance(start, int) else pl.multiple_of(start, BLOCK), size)


def tile_of(size):
    return max(rows for rows in range(UNIT, 6 * UNIT + 1, UNIT) if size % rows == 0)


def attend(place, received, rows, lengths):
    count = len(received)
    width = received[0].shape[2]
    total = count * rows
    span = 2 * HEAD_DIM
    factor = math.log2(math.e) / math.sqrt(HEAD_DIM)

    def body(place_ref, *refs):
        parts = refs[:count]
        out_refs = refs[count : count + len(lengths)]
        counts_ref, used_ref = refs[count + len(lengths) : count + len(lengths) + 2]
        query_all, key_all, value_all, result, ordered, table = refs[count + len(lengths) + 2 :]

        @pl.when(pl.program_id(0) == 0)
        def _():
            value_all[...] = jnp.zeros_like(value_all)
            for mask in range(count):
                blocks = jnp.zeros((1, HEAD_DIM), jnp.float32)
                for first in range(0, rows, BLOCK):
                    row = parts[mask][1, first : first + 16, :HEAD_DIM].astype(jnp.float32)[:1]
                    blocks = blocks + jnp.where(row < LIMIT, 1.0, 0.0)
                counts_ref[mask] = jnp.max(blocks).astype(jnp.int32)

        by_mask, by_view, used = packed_offsets(place_ref, counts_ref, table, count)
        used_ref[0] = used
        for mask in range(count):
            where = rows_at(by_mask[mask], rows)
            query_all[where, :] = parts[mask][0]
            key_all[where, :] = parts[mask][1]
            value_all[where, :] = parts[mask][2]
        key_all[rows_at(used, total // 5), :] = jnp.full((total // 5, span), SENTINEL, jnp.bfloat16)
        below = 0
        for size in variants(total):

            @pl.when((used > below) & (used <= size))
            def _(size=size):
                step = tile_of(size)
                key_mask = key_all[:size, :HEAD_DIM].astype(jnp.float32) > LIMIT
                bias = jnp.where(key_mask, jnp.float32(-1e30), 0.0)
                bias = jnp.concatenate([bias] * (step // HEAD_DIM), axis=1)
                values_t = [
                    value_all[:size, first : first + HEAD_DIM].T
                    for first in range(0, span, HEAD_DIM)
                ]

                def tile(index, carry):
                    if isinstance(index, int):
                        where = pl.ds(index * step, step)
                    else:
                        where = pl.ds(pl.multiple_of(index * step, UNIT), step)
                    for head in range(span // HEAD_DIM):
                        lanes = slice(head * HEAD_DIM, (head + 1) * HEAD_DIM)
                        scores = lax.dot_general(
                            key_all[:size, lanes],
                            query_all[where, lanes],
                            (((1,), (1,)), ((), ())),
                            preferred_element_type=jnp.float32,
                        )
                        scores = scores + bias
                        top = jnp.max(scores, axis=0, keepdims=True)
                        raised = jnp.exp2((scores - top) * factor)
                        norm = jnp.sum(raised, axis=0, keepdims=True)
                        summed = jnp.dot(
                            values_t[head],
                            raised.astype(jnp.bfloat16),
                            preferred_element_type=jnp.float32,
                        )
                        result[where, lanes] = (summed / norm).T.astype(jnp.bfloat16)
                    return carry

                if size == step:
                    tile(0, 0)
                else:
                    lax.fori_loop(0, size // step, tile, 0)

            below = size
        for view in range(count):
            moved = result[rows_at(table[place_ref[0] ^ view], rows), :]
            ordered[rows_at(by_view[view], rows), :] = moved
        first = 0
        for length, out_ref in zip(lengths, out_refs):
            out_ref[...] = ordered[first : first + length, :]
            first += length

    flops = 4 * total * total * width // 4
    return pl.pallas_call(
        body,
        grid_spec=pltpu.PrefetchScalarGridSpec(
            num_scalar_prefetch=1,
            grid=(width // span,),
            in_specs=[pl.BlockSpec((3, rows, span), lambda h, *_: (0, 0, h))] * count,
            out_specs=[pl.BlockSpec((length, span), lambda h, *_: (0, h)) for length in lengths]
            + [pl.BlockSpec(memory_space=pltpu.SMEM)] * 2,
            scratch_shapes=[
                pltpu.VMEM((total, span), jnp.bfloat16),
                pltpu.VMEM((total + total // 5, span), jnp.bfloat16),
                pltpu.VMEM((total, span), jnp.bfloat16),
                pltpu.VMEM((total, span), jnp.bfloat16),
                pltpu.VMEM((total, span), jnp.bfloat16),
                pltpu.SMEM((count,), jnp.int32),
            ],
        ),
        out_shape=[jax.ShapeDtypeStruct((length, width), jnp.bfloat16) for length in lengths]
        + [jax.ShapeDtypeStruct((count,), jnp.int32), jax.ShapeDtypeStruct((1,), jnp.int32)],
        compiler_params=params(40),
        cost_estimate=pl.CostEstimate(
            flops=flops, bytes_accessed=8 * total * width, transcendentals=flops // 512
        ),
        name="attend",
    )(place, pltpu.with_memory_space_constraint(received[0], pltpu.HBM), *received[1:])


def gather_features(own, count, between=lambda arrived: arrived):
    held = {0: list(own)}
    if count == 8:
        over_x_0 = xor_permute(held[0][0], 2, count)
        over_y_1 = xor_permute(held[0][1], 4, count)
        over_x_1 = xor_permute(held[0][1], 2, count)
        over_y_0 = xor_permute(held[0][0], 4, count)
        over_x_0, over_y_1 = between((over_x_0, over_y_1))
        diagonal_0 = xor_permute(over_x_0, 4, count)
        diagonal_1 = xor_permute(over_y_1, 2, count)
        held[2] = [over_x_0, over_x_1]
        held[4] = [over_y_0, over_y_1]
        held[6] = [diagonal_0, diagonal_1]
    else:
        for mask in range(2, count, 2):
            held[mask] = [xor_permute(piece, mask, count) for piece in held[0]]
        held[2] = list(between(tuple(held[2])))
    for mask in range(0, count, 2):
        held[mask + 1] = [xor_permute(piece, 1, count) for piece in held[mask]]
    return [held[mask] for mask in range(count)]


def unfilled(shape):
    def body(out_ref):
        pass

    return pl.pallas_call(
        body,
        out_specs=pl.BlockSpec(memory_space=pl.ANY),
        out_shape=shape,
        name="unfilled",
    )()


def project(place, group, counts, features, more, shards, rows):
    count = len(features)
    half, width = features[0][0].shape
    total = count * rows
    distances = sorted(shards)
    columns = shards[0].shape[1]
    each = shards[0].shape[0] // width
    bounds = [size for size in variants(total) if size <= 2 * half] + [total]

    def body(place_ref, group_ref, counts_ref, *refs):
        flat = refs[: 2 * count]
        more_ref = refs[2 * count]
        shard_refs = refs[2 * count + 1 : 2 * count + 1 + len(distances)]
        out_refs = refs[2 * count + 1 + len(distances) : 3 * count + 1 + len(distances)]
        landed, weight_all, sums, sems, weight_sems = refs[3 * count + 1 + len(distances) :]
        used = sum(counts_ref[mask] for mask in range(count)) * BLOCK

        for mask in range(count):
            owner = place_ref[0] ^ mask
            apart = group_ref[0] - owner // each
            start = pl.multiple_of((owner % each) * width, width)
            lower = mask % 2 * width
            for distance, shard_ref in zip(distances, shard_refs):

                @pl.when(apart == distance)
                def _(mask=mask, start=start, lower=lower, shard_ref=shard_ref):
                    pltpu.make_async_copy(
                        shard_ref.at[pl.ds(start, width), :],
                        weight_all.at[mask // 2, lower : lower + width, :],
                        weight_sems.at[mask // 2],
                    ).start()

        below = 0
        for size in bounds:

            @pl.when((used > below) & (used <= size))
            def _(size=size):
                for mask in range(count):
                    lanes = slice(mask % 2 * width, (mask % 2 + 1) * width)
                    sources = [flat[2 * mask], flat[2 * mask + 1]]
                    if size > 2 * half:
                        sources += [more_ref.at[2 * mask], more_ref.at[2 * mask + 1]]
                    first = 0
                    for source in sources:
                        length = min(source.shape[0], size - first)
                        pltpu.make_async_copy(
                            source.at[:length, :],
                            landed.at[mask // 2, first : first + length, lanes],
                            sems.at[mask // 2],
                        ).start()
                        first += length
                sums[:size, :] = jnp.zeros((size, columns), jnp.float32)

                def pair(index, carry):
                    for buffer, sem in (
                        (weight_all.at[index], weight_sems.at[index]),
                        (landed.at[index, :size, :], sems.at[index]),
                    ):
                        pltpu.make_async_copy(buffer, buffer, sem).wait()
                    sums[:size, :] += jnp.dot(
                        landed[index, :size, :],
                        weight_all[index],
                        preferred_element_type=jnp.float32,
                    )
                    return carry

                lax.fori_loop(0, count // 2, pair, 0)

            below = size
        for mask in range(count):
            position = 0
            for view in range(count):
                position = position + jnp.where(
                    view < (place_ref[0] ^ mask), counts_ref[place_ref[0] ^ view], 0
                )
            moved = sums[rows_at(position * BLOCK, rows), :]
            out_refs[mask][...] = moved.astype(jnp.bfloat16)

    any_spec = pl.BlockSpec(memory_space=pl.ANY)
    inputs = [piece for pair in features for piece in pair] + [more]
    inputs += [shards[distance] for distance in distances]
    inputs = [pltpu.with_memory_space_constraint(array, pltpu.HBM) for array in inputs]
    return pl.pallas_call(
        body,
        grid_spec=pltpu.PrefetchScalarGridSpec(
            num_scalar_prefetch=3,
            grid=(1,),
            in_specs=[any_spec] * len(inputs),
            out_specs=[full_spec((rows, columns))] * count,
            scratch_shapes=[
                pltpu.VMEM((count // 2, total, 2 * width), jnp.bfloat16),
                pltpu.VMEM((count // 2, 2 * width, columns), jnp.bfloat16),
                pltpu.VMEM((total, columns), jnp.float32),
                pltpu.SemaphoreType.DMA((count // 2,)),
                pltpu.SemaphoreType.DMA((count // 2,)),
            ],
        ),
        out_shape=[jax.ShapeDtypeStruct((rows, columns), jnp.bfloat16)] * count,
        compiler_params=params(56),
        cost_estimate=pl.CostEstimate(
            flops=total * count * width * columns,
            bytes_accessed=total * count * width,
            transcendentals=0,
        ),
        name="project",
    )(place, group, counts, *inputs)


def assemble(place, block_counts, row_mask, pieces, count):
    rows, columns = pieces[0].shape
    if columns % HEAD_DIM:
        stacked = jnp.stack(pieces)[jnp.arange(count) ^ place[0]]
        result = jnp.moveaxis(stacked, 0, 1).reshape(rows, count * columns)
        offsets = jnp.arange(rows, dtype=jnp.int32)
        good = (row_mask[0] == 1) & (offsets // BLOCK < block_counts[0, 0])
        return jnp.where(good[:, None], result, jnp.bfloat16(0.0))

    def body(place_ref, blocks_ref, mask_ref, *refs):
        out_ref = refs[-1]
        good = valid_column(mask_ref, blocks_ref[0, 0]) > 0.5
        for mask in range(count):
            start = pl.multiple_of((place_ref[0] ^ mask) * columns, HEAD_DIM)
            out_ref[:, pl.ds(start, columns)] = jnp.where(
                good, refs[mask][...], jnp.bfloat16(0.0)
            )

    return pl.pallas_call(
        body,
        grid_spec=pltpu.PrefetchScalarGridSpec(
            num_scalar_prefetch=2,
            grid=(1,),
            in_specs=[full_spec((1, rows))] + [full_spec((rows, columns))] * count,
            out_specs=full_spec((rows, count * columns)),
        ),
        out_shape=jax.ShapeDtypeStruct((rows, count * columns), jnp.bfloat16),
        compiler_params=params(16),
        cost_estimate=pl.CostEstimate(
            flops=0, bytes_accessed=4 * rows * count * columns, transcendentals=0
        ),
        name="assemble",
    )(
        place,
        block_counts,
        row_mask,
        pltpu.with_memory_space_constraint(pieces[0], pltpu.HBM),
        *pieces[1:],
    )


def local(queries, keys, values, out_weight, block_counts, row_mask):
    rows = queries.shape[1]
    count = lax.axis_size("cam")
    total = count * rows
    place_array = jnp.full((1,), lax.axis_index("cam"), jnp.int32)
    group_array = jnp.full((1,), lax.axis_index("fsdp"), jnp.int32)

    payloads, weight_part = pack(
        place_array, block_counts, row_mask, queries, keys, values, out_weight, count
    )
    shards = {0: weight_part}
    groups = lax.axis_size("fsdp")

    received = [payloads[0]] + [None] * (count - 1)
    early = [mask for mask in order(count) if mask & 1 == 0]
    late = [mask for mask in order(count) if mask & 1]
    pass_weight(shards, 1)
    for mask in early:
        received[mask] = xor_permute(payloads[mask], mask, count)
    received, payloads = lax.optimization_barrier((received, payloads))
    for mask in (late[0], 1):
        received[mask] = xor_permute(payloads[mask], mask, count)
    received, payloads, shards[1], shards[-1] = lax.optimization_barrier(
        (received, payloads, shards[1], shards[-1])
    )
    pass_weight(shards, 2)
    for mask in late[1:-1]:
        received[mask] = xor_permute(payloads[mask], mask, count)
    half = total * 3 // 10
    first, second, rest, counts, used = attend(
        place_array, received, rows, (half, half, total - 2 * half)
    )

    quarter = rest.shape[0] // 2
    shape = jax.ShapeDtypeStruct((2 * count, quarter, rest.shape[1]), rest.dtype)

    def gather_rest(part):
        pieces = gather_features((part[:quarter], part[quarter:]), count)
        return jnp.stack([piece for pair in pieces for piece in pair])

    def weight_step(arrived):
        arrived, shards[2], shards[-2] = lax.optimization_barrier((arrived, shards[2], shards[-2]))
        pass_weight(shards, 3)
        return arrived

    features = gather_features((first, second), count, weight_step)
    for distance in range(4, groups):
        pass_weight(shards, distance)
    rest, features, shards = lax.optimization_barrier((rest, features, shards))
    more = lax.cond(used[0] > 2 * half, gather_rest, lambda part: unfilled(shape), rest)
    pieces = project(place_array, group_array, counts, features, more, shards, rows)
    landed = [pieces[0]] + [None] * (count - 1)
    for mask in order(count):
        landed[mask] = xor_permute(pieces[mask], mask, count)
    return assemble(place_array, block_counts, row_mask, landed, count)[None]


def solution(mesh):
    in_specs = (
        P("fsdp", "cam", None),
        P("fsdp", "cam", None),
        P("fsdp", "cam", None),
        P("fsdp", None),
        P("fsdp", "cam"),
        P("fsdp", "cam"),
    )
    out_specs = P("fsdp", "cam", None)
    return jax.shard_map(local, mesh=mesh, in_specs=in_specs, out_specs=out_specs, check_vma=False)
```

```python
import math

import jax
import jax.numpy as jnp
from jax import lax
from jax.experimental import pallas as pl
from jax.experimental.pallas import tpu as pltpu
from jax.sharding import PartitionSpec as P

HEAD_DIM = 128
BLOCK = 32
SENTINEL = 32.0
LIMIT = 24.0
UNIT = 128


def params(mebibytes):
    return pltpu.CompilerParams(vmem_limit_bytes=mebibytes * 1024 * 1024)


def order(count):
    return sorted(range(1, count), key=lambda mask: (mask == 1, mask & 1, -bin(mask).count("1")))


def variants(total):
    return sorted({-(-total * tenths // (10 * UNIT)) * UNIT for tenths in (4, 5, 6, 8, 10)})


def full_spec(shape):
    return pl.BlockSpec(shape, lambda i, *_: (0,) * len(shape))


def column_of(row):
    n = row.shape[1]
    diagonal = lax.broadcasted_iota(jnp.int32, (n, n), 0) == lax.broadcasted_iota(
        jnp.int32, (n, n), 1
    )
    return jnp.sum(jnp.where(diagonal, row, 0.0), axis=1, keepdims=True)


def valid_column(mask_ref, blocks):
    rows = mask_ref.shape[1]
    inside = lax.broadcasted_iota(jnp.int32, (1, rows), 1) < blocks * BLOCK
    return column_of(jnp.where((mask_ref[...] == 1) & inside, 1.0, 0.0))


def xor_permute(array, mask, count):
    return lax.ppermute(array, "cam", [(place, place ^ mask) for place in range(count)])


def pack(place, block_counts, row_mask, queries, keys, values, out_weight, count):
    _, rows, features = queries.shape
    width = features // count
    depth = out_weight.shape[0]
    columns = out_weight.shape[1] // count
    slicing = columns % HEAD_DIM == 0
    chunks = 1 if slicing else 0
    staged = columns if slicing else HEAD_DIM

    def body(place_ref, blocks_ref, mask_ref, q_ref, k_ref, v_ref, w_ref, *refs):
        out_refs = refs[:count]
        weight_refs = refs[count : count + chunks]
        held, key_out, w_held, load_sems, sems, weight_sems = refs[count + chunks :]
        loads = []
        for slot, ref in enumerate((k_ref, q_ref, v_ref)):
            load = pltpu.make_async_copy(ref.at[0], held.at[slot], load_sems.at[slot])
            load.start()
            loads.append(load)
        if chunks:
            start = pl.multiple_of(place_ref[0] * columns, HEAD_DIM)
            load = pltpu.make_async_copy(
                w_ref.at[:, pl.ds(start, columns)], w_held, load_sems.at[3]
            )
            load.start()
            loads.append(load)
        starts = [pl.multiple_of((place_ref[0] ^ m) * width, HEAD_DIM) for m in range(count)]
        good = valid_column(mask_ref, blocks_ref[0, 0]) > 0.5
        copies = []

        def send(source, target, sem):
            copy = pltpu.make_async_copy(source, target, sem)
            copy.start()
            copies.append(copy)

        loads[0].wait()
        for mask in range(count):
            part = held[0, :, pl.ds(starts[mask], width)]
            key_out[mask] = jnp.where(good, part, jnp.bfloat16(SENTINEL))
            send(key_out.at[mask], out_refs[mask].at[1], sems.at[mask, 1])
        for slot, target in ((1, 0), (2, 2)):
            loads[slot].wait()
            for mask in range(count):
                source = held.at[slot, :, pl.ds(starts[mask], width)]
                send(source, out_refs[mask].at[target], sems.at[mask, target])
        if chunks:
            loads[3].wait()
            send(w_held, weight_refs[0], weight_sems.at[0])
        for copy in copies:
            copy.wait()

    any_spec = pl.BlockSpec(memory_space=pl.ANY)
    weight_shapes = [jax.ShapeDtypeStruct((depth, columns), jnp.bfloat16)] * chunks
    outputs = pl.pallas_call(
        body,
        grid_spec=pltpu.PrefetchScalarGridSpec(
            num_scalar_prefetch=2,
            grid=(1,),
            in_specs=[full_spec((1, rows))] + [any_spec] * 4,
            out_specs=[any_spec] * (count + chunks),
            scratch_shapes=[
                pltpu.VMEM((3, rows, features), jnp.bfloat16),
                pltpu.VMEM((count, rows, width), jnp.bfloat16),
                pltpu.VMEM((depth, staged), jnp.bfloat16),
                pltpu.SemaphoreType.DMA((4,)),
                pltpu.SemaphoreType.DMA((count, 3)),
                pltpu.SemaphoreType.DMA((1,)),
            ],
        ),
        out_shape=[jax.ShapeDtypeStruct((3, rows, width), jnp.bfloat16)] * count + weight_shapes,
        compiler_params=params(56),
        cost_estimate=pl.CostEstimate(
            flops=0, bytes_accessed=12 * rows * features, transcendentals=0
        ),
        name="pack",
    )(place, block_counts, row_mask, queries, keys, values, out_weight)
    if slicing:
        return list(outputs[:count]), outputs[count]
    start = place[0] * columns
    return list(outputs[:count]), lax.dynamic_slice_in_dim(out_weight, start, columns, axis=1)


def pass_weight(shards, distance):
    groups = lax.axis_size("fsdp")
    for sign in (1, -1):
        pairs = []
        for source in range(groups):
            origin, target = source - sign * (distance - 1), source + sign
            if 0 <= origin < groups and 0 <= target < groups:
                pairs.append((source, target))
        shards[sign * distance] = lax.ppermute(shards[sign * (distance - 1)], "fsdp", pairs)


def packed_offsets(place_ref, counts_ref, table, count):
    by_mask, running = [], 0
    for mask in range(count):
        by_mask.append(running)
        table[mask] = running
        running = running + counts_ref[mask] * BLOCK
    by_view, position = [], 0
    for view in range(count):
        by_view.append(position)
        position = position + counts_ref[place_ref[0] ^ view] * BLOCK
    return by_mask, by_view, running


def rows_at(start, size):
    return pl.ds(start if isinstance(start, int) else pl.multiple_of(start, BLOCK), size)


def tile_of(size):
    return max(rows for rows in range(UNIT, 6 * UNIT + 1, UNIT) if size % rows == 0)


def attend(place, received, rows, lengths):
    count = len(received)
    width = received[0].shape[2]
    total = count * rows
    span = 2 * HEAD_DIM
    factor = math.log2(math.e) / math.sqrt(HEAD_DIM)

    def body(place_ref, *refs):
        parts = refs[:count]
        out_refs = refs[count : count + len(lengths)]
        counts_ref, used_ref = refs[count + len(lengths) : count + len(lengths) + 2]
        query_all, key_all, value_all, result, ordered, table = refs[count + len(lengths) + 2 :]

        @pl.when(pl.program_id(0) == 0)
        def _():
            value_all[...] = jnp.zeros_like(value_all)
            for mask in range(count):
                blocks = jnp.zeros((1, HEAD_DIM), jnp.float32)
                for first in range(0, rows, BLOCK):
                    row = parts[mask][1, first : first + 16, :HEAD_DIM].astype(jnp.float32)[:1]
                    blocks = blocks + jnp.where(row < LIMIT, 1.0, 0.0)
                counts_ref[mask] = jnp.max(blocks).astype(jnp.int32)

        by_mask, by_view, used = packed_offsets(place_ref, counts_ref, table, count)
        used_ref[0] = used
        for mask in range(count):
            where = rows_at(by_mask[mask], rows)
            query_all[where, :] = parts[mask][0]
            key_all[where, :] = parts[mask][1]
            value_all[where, :] = parts[mask][2]
        key_all[rows_at(used, total // 5), :] = jnp.full((total // 5, span), SENTINEL, jnp.bfloat16)
        below = 0
        for size in variants(total):

            @pl.when((used > below) & (used <= size))
            def _(size=size):
                step = tile_of(size)
                key_mask = key_all[:size, :HEAD_DIM].astype(jnp.float32) > LIMIT
                bias = jnp.where(key_mask, jnp.float32(-1e30), 0.0)
                bias = jnp.concatenate([bias] * (step // HEAD_DIM), axis=1)
                values_t = [
                    value_all[:size, first : first + HEAD_DIM].T
                    for first in range(0, span, HEAD_DIM)
                ]

                def tile(index, carry):
                    if isinstance(index, int):
                        where = pl.ds(index * step, step)
                    else:
                        where = pl.ds(pl.multiple_of(index * step, UNIT), step)
                    for head in range(span // HEAD_DIM):
                        lanes = slice(head * HEAD_DIM, (head + 1) * HEAD_DIM)
                        scores = lax.dot_general(
                            key_all[:size, lanes],
                            query_all[where, lanes],
                            (((1,), (1,)), ((), ())),
                            preferred_element_type=jnp.float32,
                        )
                        scores = scores + bias
                        top = jnp.max(scores, axis=0, keepdims=True)
                        raised = jnp.exp2((scores - top) * factor)
                        norm = jnp.sum(raised, axis=0, keepdims=True)
                        summed = jnp.dot(
                            values_t[head],
                            raised.astype(jnp.bfloat16),
                            preferred_element_type=jnp.float32,
                        )
                        result[where, lanes] = (summed / norm).T.astype(jnp.bfloat16)
                    return carry

                if size == step:
                    tile(0, 0)
                else:
                    lax.fori_loop(0, size // step, tile, 0)

            below = size
        for view in range(count):
            moved = result[rows_at(table[place_ref[0] ^ view], rows), :]
            ordered[rows_at(by_view[view], rows), :] = moved
        first = 0
        for length, out_ref in zip(lengths, out_refs):
            out_ref[...] = ordered[first : first + length, :]
            first += length

    flops = 4 * total * total * width // 4
    return pl.pallas_call(
        body,
        grid_spec=pltpu.PrefetchScalarGridSpec(
            num_scalar_prefetch=1,
            grid=(width // span,),
            in_specs=[pl.BlockSpec((3, rows, span), lambda h, *_: (0, 0, h))] * count,
            out_specs=[pl.BlockSpec((length, span), lambda h, *_: (0, h)) for length in lengths]
            + [pl.BlockSpec(memory_space=pltpu.SMEM)] * 2,
            scratch_shapes=[
                pltpu.VMEM((total, span), jnp.bfloat16),
                pltpu.VMEM((total + total // 5, span), jnp.bfloat16),
                pltpu.VMEM((total, span), jnp.bfloat16),
                pltpu.VMEM((total, span), jnp.bfloat16),
                pltpu.VMEM((total, span), jnp.bfloat16),
                pltpu.SMEM((count,), jnp.int32),
            ],
        ),
        out_shape=[jax.ShapeDtypeStruct((length, width), jnp.bfloat16) for length in lengths]
        + [jax.ShapeDtypeStruct((count,), jnp.int32), jax.ShapeDtypeStruct((1,), jnp.int32)],
        compiler_params=params(40),
        cost_estimate=pl.CostEstimate(
            flops=flops, bytes_accessed=8 * total * width, transcendentals=flops // 512
        ),
        name="attend",
    )(place, pltpu.with_memory_space_constraint(received[0], pltpu.HBM), *received[1:])


def gather_features(own, count, between=lambda arrived: arrived):
    half = own.shape[0] // 2
    held = {0: [own]}
    if count == 8:
        over_x = xor_permute(own, 2, count)
        over_y = xor_permute(own, 4, count)
        held[1] = [between(xor_permute(own, 1, count))]
        held[2], held[4] = [over_x], [over_y]
        held[6] = [xor_permute(over_x[:half], 4, count), xor_permute(over_y[half:], 2, count)]
    else:
        for mask in range(2, count, 2):
            held[mask] = [xor_permute(own, mask, count)]
        held[1] = [between(xor_permute(own, 1, count))]
    for mask in range(2, count, 2):
        held[mask + 1] = [xor_permute(piece, 1, count) for piece in held[mask]]
    return [held[mask] for mask in range(count)]


def unfilled(shape):
    def body(out_ref):
        pass

    return pl.pallas_call(
        body,
        out_specs=pl.BlockSpec(memory_space=pl.ANY),
        out_shape=shape,
        name="unfilled",
    )()


def project(place, group, counts, features, more, shards, rows):
    count = len(features)
    width = more.shape[2]
    total = count * rows
    always = total - more.shape[1]
    distances = sorted(shards)
    columns = shards[0].shape[1]
    each = shards[0].shape[0] // width
    bounds = [size for size in variants(total) if size <= always] + [total]
    flat = [piece for pieces in features for piece in pieces]

    def body(place_ref, group_ref, counts_ref, *refs):
        flat_refs = list(refs[: len(flat)])
        more_ref = refs[len(flat)]
        shard_refs = refs[len(flat) + 1 : len(flat) + 1 + len(distances)]
        out_refs = refs[len(flat) + 1 + len(distances) :][:count]
        landed, weight_all, sums, sems, weight_sems = refs[len(flat) + 1 + len(distances) + count :]
        used = sum(counts_ref[mask] for mask in range(count)) * BLOCK

        for mask in range(count):
            owner = place_ref[0] ^ mask
            apart = group_ref[0] - owner // each
            start = pl.multiple_of((owner % each) * width, width)
            lower = mask % 2 * width
            for distance, shard_ref in zip(distances, shard_refs):

                @pl.when(apart == distance)
                def _(mask=mask, start=start, lower=lower, shard_ref=shard_ref):
                    pltpu.make_async_copy(
                        shard_ref.at[pl.ds(start, width), :],
                        weight_all.at[mask // 2, lower : lower + width, :],
                        weight_sems.at[mask // 2],
                    ).start()

        below = 0
        for size in bounds:

            @pl.when((used > below) & (used <= size))
            def _(size=size):
                taken = 0
                for mask in range(count):
                    lanes = slice(mask % 2 * width, (mask % 2 + 1) * width)
                    sources = flat_refs[taken : taken + len(features[mask])]
                    taken += len(sources)
                    if size > always:
                        sources.append(more_ref.at[mask])
                    first = 0
                    for source in sources:
                        length = min(source.shape[0], size - first)
                        pltpu.make_async_copy(
                            source.at[:length, :],
                            landed.at[mask // 2, first : first + length, lanes],
                            sems.at[mask // 2],
                        ).start()
                        first += length
                sums[:size, :] = jnp.zeros((size, columns), jnp.float32)

                def pair(index, carry):
                    for buffer, sem in (
                        (weight_all.at[index], weight_sems.at[index]),
                        (landed.at[index, :size, :], sems.at[index]),
                    ):
                        pltpu.make_async_copy(buffer, buffer, sem).wait()
                    sums[:size, :] += jnp.dot(
                        landed[index, :size, :],
                        weight_all[index],
                        preferred_element_type=jnp.float32,
                    )
                    return carry

                lax.fori_loop(0, count // 2, pair, 0)

            below = size
        for mask in range(count):
            position = 0
            for view in range(count):
                position = position + jnp.where(
                    view < (place_ref[0] ^ mask), counts_ref[place_ref[0] ^ view], 0
                )
            moved = sums[rows_at(position * BLOCK, rows), :]
            out_refs[mask][...] = moved.astype(jnp.bfloat16)

    any_spec = pl.BlockSpec(memory_space=pl.ANY)
    inputs = flat + [more]
    inputs += [shards[distance] for distance in distances]
    inputs = [pltpu.with_memory_space_constraint(array, pltpu.HBM) for array in inputs]
    return pl.pallas_call(
        body,
        grid_spec=pltpu.PrefetchScalarGridSpec(
            num_scalar_prefetch=3,
            grid=(1,),
            in_specs=[any_spec] * len(inputs),
            out_specs=[full_spec((rows, columns))] * count,
            scratch_shapes=[
                pltpu.VMEM((count // 2, total, 2 * width), jnp.bfloat16),
                pltpu.VMEM((count // 2, 2 * width, columns), jnp.bfloat16),
                pltpu.VMEM((total, columns), jnp.float32),
                pltpu.SemaphoreType.DMA((count // 2,)),
                pltpu.SemaphoreType.DMA((count // 2,)),
            ],
        ),
        out_shape=[jax.ShapeDtypeStruct((rows, columns), jnp.bfloat16)] * count,
        compiler_params=params(56),
        cost_estimate=pl.CostEstimate(
            flops=total * count * width * columns,
            bytes_accessed=total * count * width,
            transcendentals=0,
        ),
        name="project",
    )(place, group, counts, *inputs)


def assemble(place, block_counts, row_mask, pieces, count):
    rows, columns = pieces[0].shape
    if columns % HEAD_DIM:
        stacked = jnp.stack(pieces)[jnp.arange(count) ^ place[0]]
        result = jnp.moveaxis(stacked, 0, 1).reshape(rows, count * columns)
        offsets = jnp.arange(rows, dtype=jnp.int32)
        good = (row_mask[0] == 1) & (offsets // BLOCK < block_counts[0, 0])
        return jnp.where(good[:, None], result, jnp.bfloat16(0.0))

    def body(place_ref, blocks_ref, mask_ref, *refs):
        out_ref = refs[-1]
        good = valid_column(mask_ref, blocks_ref[0, 0]) > 0.5
        for mask in range(count):
            start = pl.multiple_of((place_ref[0] ^ mask) * columns, HEAD_DIM)
            out_ref[:, pl.ds(start, columns)] = jnp.where(
                good, refs[mask][...], jnp.bfloat16(0.0)
            )

    return pl.pallas_call(
        body,
        grid_spec=pltpu.PrefetchScalarGridSpec(
            num_scalar_prefetch=2,
            grid=(1,),
            in_specs=[full_spec((1, rows))] + [full_spec((rows, columns))] * count,
            out_specs=full_spec((rows, count * columns)),
        ),
        out_shape=jax.ShapeDtypeStruct((rows, count * columns), jnp.bfloat16),
        compiler_params=params(16),
        cost_estimate=pl.CostEstimate(
            flops=0, bytes_accessed=4 * rows * count * columns, transcendentals=0
        ),
        name="assemble",
    )(
        place,
        block_counts,
        row_mask,
        pltpu.with_memory_space_constraint(pieces[0], pltpu.HBM),
        *pieces[1:],
    )


def local(queries, keys, values, out_weight, block_counts, row_mask):
    rows = queries.shape[1]
    count = lax.axis_size("cam")
    total = count * rows
    place_array = jnp.full((1,), lax.axis_index("cam"), jnp.int32)
    group_array = jnp.full((1,), lax.axis_index("fsdp"), jnp.int32)

    payloads, weight_part = pack(
        place_array, block_counts, row_mask, queries, keys, values, out_weight, count
    )
    shards = {0: weight_part}
    groups = lax.axis_size("fsdp")

    received = [payloads[0]] + [None] * (count - 1)
    early = [mask for mask in order(count) if mask & 1 == 0]
    late = [mask for mask in order(count) if mask & 1]
    pass_weight(shards, 1)
    for mask in early:
        received[mask] = xor_permute(payloads[mask], mask, count)
    received, payloads = lax.optimization_barrier((received, payloads))
    for mask in (late[0], 1):
        received[mask] = xor_permute(payloads[mask], mask, count)
    received, payloads, shards[1], shards[-1] = lax.optimization_barrier(
        (received, payloads, shards[1], shards[-1])
    )
    pass_weight(shards, 2)
    for mask in late[1:-1]:
        received[mask] = xor_permute(payloads[mask], mask, count)
    always = total * 3 // 5
    attended, rest, counts, used = attend(
        place_array, received, rows, (always, total - always)
    )
    shape = jax.ShapeDtypeStruct((count,) + rest.shape, rest.dtype)

    def gather_rest(part):
        return jnp.stack([jnp.concatenate(pieces) for pieces in gather_features(part, count)])

    def weight_step(arrived):
        arrived, shards[2], shards[-2] = lax.optimization_barrier((arrived, shards[2], shards[-2]))
        pass_weight(shards, 3)
        return arrived

    features = gather_features(attended, count, weight_step)
    for distance in range(4, groups):
        pass_weight(shards, distance)
    rest, features, shards = lax.optimization_barrier((rest, features, shards))
    more = lax.cond(used[0] > always, gather_rest, lambda part: unfilled(shape), rest)
    pieces = project(place_array, group_array, counts, features, more, shards, rows)
    landed = [pieces[0]] + [None] * (count - 1)
    for mask in order(count):
        landed[mask] = xor_permute(pieces[mask], mask, count)
    return assemble(place_array, block_counts, row_mask, landed, count)[None]


def solution(mesh):
    in_specs = (
        P("fsdp", "cam", None),
        P("fsdp", "cam", None),
        P("fsdp", "cam", None),
        P("fsdp", None),
        P("fsdp", "cam"),
        P("fsdp", "cam"),
    )
    out_specs = P("fsdp", "cam", None)
    return jax.shard_map(local, mesh=mesh, in_specs=in_specs, out_specs=out_specs, check_vma=False)
```

```python
import math

import jax
import jax.numpy as jnp
from jax import lax
from jax.experimental import pallas as pl
from jax.experimental.pallas import tpu as pltpu
from jax.sharding import PartitionSpec as P

HEAD_DIM = 128
BLOCK = 32
SENTINEL = 32.0
LIMIT = 24.0
UNIT = 128


def params(mebibytes):
    return pltpu.CompilerParams(vmem_limit_bytes=mebibytes * 1024 * 1024)


def order(count):
    return sorted(range(1, count), key=lambda mask: (mask == 1, mask & 1, -bin(mask).count("1")))


def variants(total):
    return sorted({-(-total * tenths // (10 * UNIT)) * UNIT for tenths in (4, 5, 6, 8, 10)})


def full_spec(shape):
    return pl.BlockSpec(shape, lambda i, *_: (0,) * len(shape))


def column_of(row):
    n = row.shape[1]
    diagonal = lax.broadcasted_iota(jnp.int32, (n, n), 0) == lax.broadcasted_iota(
        jnp.int32, (n, n), 1
    )
    return jnp.sum(jnp.where(diagonal, row, 0.0), axis=1, keepdims=True)


def valid_column(mask_ref, blocks):
    rows = mask_ref.shape[1]
    inside = lax.broadcasted_iota(jnp.int32, (1, rows), 1) < blocks * BLOCK
    return column_of(jnp.where((mask_ref[...] == 1) & inside, 1.0, 0.0))


def xor_permute(array, mask, count):
    return lax.ppermute(array, "cam", [(place, place ^ mask) for place in range(count)])


def cut_weight(place, out_weight, count):
    depth = out_weight.shape[0]
    columns = out_weight.shape[1] // count
    if columns % HEAD_DIM:
        return lax.dynamic_slice_in_dim(out_weight, place[0] * columns, columns, axis=1)
    step = depth // 4

    def body(place_ref, w_ref, out_ref):
        out_ref[...] = w_ref[...]

    return pl.pallas_call(
        body,
        grid_spec=pltpu.PrefetchScalarGridSpec(
            num_scalar_prefetch=1,
            grid=(depth // step,),
            in_specs=[pl.BlockSpec((step, columns), lambda i, place_ref: (i, place_ref[0]))],
            out_specs=pl.BlockSpec((step, columns), lambda i, place_ref: (i, 0)),
        ),
        out_shape=jax.ShapeDtypeStruct((depth, columns), jnp.bfloat16),
        compiler_params=params(56),
        cost_estimate=pl.CostEstimate(
            flops=0, bytes_accessed=4 * depth * columns, transcendentals=0
        ),
        name="cut_weight",
    )(place, out_weight)


def pack(place, block_counts, row_mask, queries, keys, values, count):
    _, rows, features = queries.shape
    width = features // count

    def body(place_ref, blocks_ref, mask_ref, q_ref, k_ref, v_ref, *refs):
        out_refs = refs[:count]
        held, key_out, load_sems, sems = refs[count:]
        loads = []
        for slot, ref in enumerate((k_ref, q_ref, v_ref)):
            load = pltpu.make_async_copy(ref.at[0], held.at[slot], load_sems.at[slot])
            load.start()
            loads.append(load)
        starts = [pl.multiple_of((place_ref[0] ^ m) * width, HEAD_DIM) for m in range(count)]
        good = valid_column(mask_ref, blocks_ref[0, 0]) > 0.5
        copies = []

        def send(source, target, sem):
            copy = pltpu.make_async_copy(source, target, sem)
            copy.start()
            copies.append(copy)

        loads[0].wait()
        for mask in range(count):
            part = held[0, :, pl.ds(starts[mask], width)]
            key_out[mask] = jnp.where(good, part, jnp.bfloat16(SENTINEL))
            send(key_out.at[mask], out_refs[mask].at[1], sems.at[mask, 1])
        for slot, target in ((1, 0), (2, 2)):
            loads[slot].wait()
            for mask in range(count):
                source = held.at[slot, :, pl.ds(starts[mask], width)]
                send(source, out_refs[mask].at[target], sems.at[mask, target])
        for copy in copies:
            copy.wait()

    any_spec = pl.BlockSpec(memory_space=pl.ANY)
    return pl.pallas_call(
        body,
        grid_spec=pltpu.PrefetchScalarGridSpec(
            num_scalar_prefetch=2,
            grid=(1,),
            in_specs=[full_spec((1, rows))] + [any_spec] * 3,
            out_specs=[any_spec] * count,
            scratch_shapes=[
                pltpu.VMEM((3, rows, features), jnp.bfloat16),
                pltpu.VMEM((count, rows, width), jnp.bfloat16),
                pltpu.SemaphoreType.DMA((3,)),
                pltpu.SemaphoreType.DMA((count, 3)),
            ],
        ),
        out_shape=[jax.ShapeDtypeStruct((3, rows, width), jnp.bfloat16)] * count,
        compiler_params=params(56),
        cost_estimate=pl.CostEstimate(
            flops=0, bytes_accessed=12 * rows * features, transcendentals=0
        ),
        name="pack",
    )(place, block_counts, row_mask, queries, keys, values)


def pass_weight(shards, distance):
    groups = lax.axis_size("fsdp")
    for sign in (1, -1):
        pairs = []
        for source in range(groups):
            origin, target = source - sign * (distance - 1), source + sign
            if 0 <= origin < groups and 0 <= target < groups:
                pairs.append((source, target))
        shards[sign * distance] = lax.ppermute(shards[sign * (distance - 1)], "fsdp", pairs)


def packed_offsets(place_ref, counts_ref, table, count):
    by_mask, running = [], 0
    for mask in range(count):
        by_mask.append(running)
        table[mask] = running
        running = running + counts_ref[mask] * BLOCK
    by_view, position = [], 0
    for view in range(count):
        by_view.append(position)
        position = position + counts_ref[place_ref[0] ^ view] * BLOCK
    return by_mask, by_view, running


def rows_at(start, size):
    return pl.ds(start if isinstance(start, int) else pl.multiple_of(start, BLOCK), size)


def tile_of(size):
    return max(rows for rows in range(UNIT, 6 * UNIT + 1, UNIT) if size % rows == 0)


def attend(place, received, rows, lengths):
    count = len(received)
    width = received[0].shape[2]
    total = count * rows
    span = 2 * HEAD_DIM
    factor = math.log2(math.e) / math.sqrt(HEAD_DIM)

    def body(place_ref, *refs):
        parts = refs[:count]
        out_refs = refs[count : count + len(lengths)]
        counts_ref, used_ref = refs[count + len(lengths) : count + len(lengths) + 2]
        query_all, key_all, value_all, result, ordered, table = refs[count + len(lengths) + 2 :]

        @pl.when(pl.program_id(0) == 0)
        def _():
            value_all[...] = jnp.zeros_like(value_all)
            for mask in range(count):
                blocks = jnp.zeros((1, HEAD_DIM), jnp.float32)
                for first in range(0, rows, BLOCK):
                    row = parts[mask][1, first : first + 16, :HEAD_DIM].astype(jnp.float32)[:1]
                    blocks = blocks + jnp.where(row < LIMIT, 1.0, 0.0)
                counts_ref[mask] = jnp.max(blocks).astype(jnp.int32)

        by_mask, by_view, used = packed_offsets(place_ref, counts_ref, table, count)
        used_ref[0] = used
        for mask in range(count):
            where = rows_at(by_mask[mask], rows)
            query_all[where, :] = parts[mask][0]
            key_all[where, :] = parts[mask][1]
            value_all[where, :] = parts[mask][2]
        key_all[rows_at(used, total // 5), :] = jnp.full((total // 5, span), SENTINEL, jnp.bfloat16)
        below = 0
        for size in variants(total):

            @pl.when((used > below) & (used <= size))
            def _(size=size):
                step = tile_of(size)
                key_mask = key_all[:size, :HEAD_DIM].astype(jnp.float32) > LIMIT
                bias = jnp.where(key_mask, jnp.float32(-1e30), 0.0)
                bias = jnp.concatenate([bias] * (step // HEAD_DIM), axis=1)
                values_t = [
                    value_all[:size, first : first + HEAD_DIM].T
                    for first in range(0, span, HEAD_DIM)
                ]

                def tile(index, carry):
                    if isinstance(index, int):
                        where = pl.ds(index * step, step)
                    else:
                        where = pl.ds(pl.multiple_of(index * step, UNIT), step)
                    for head in range(span // HEAD_DIM):
                        lanes = slice(head * HEAD_DIM, (head + 1) * HEAD_DIM)
                        scores = lax.dot_general(
                            key_all[:size, lanes],
                            query_all[where, lanes],
                            (((1,), (1,)), ((), ())),
                            preferred_element_type=jnp.float32,
                        )
                        scores = scores + bias
                        top = jnp.max(scores, axis=0, keepdims=True)
                        raised = jnp.exp2((scores - top) * factor)
                        norm = jnp.sum(raised, axis=0, keepdims=True)
                        summed = jnp.dot(
                            values_t[head],
                            raised.astype(jnp.bfloat16),
                            preferred_element_type=jnp.float32,
                        )
                        result[where, lanes] = (summed / norm).T.astype(jnp.bfloat16)
                    return carry

                if size == step:
                    tile(0, 0)
                else:
                    lax.fori_loop(0, size // step, tile, 0)

            below = size
        for view in range(count):
            moved = result[rows_at(table[place_ref[0] ^ view], rows), :]
            ordered[rows_at(by_view[view], rows), :] = moved
        first = 0
        for length, out_ref in zip(lengths, out_refs):
            out_ref[...] = ordered[first : first + length, :]
            first += length

    flops = 4 * total * total * width // 4
    return pl.pallas_call(
        body,
        grid_spec=pltpu.PrefetchScalarGridSpec(
            num_scalar_prefetch=1,
            grid=(width // span,),
            in_specs=[pl.BlockSpec((3, rows, span), lambda h, *_: (0, 0, h))] * count,
            out_specs=[pl.BlockSpec((length, span), lambda h, *_: (0, h)) for length in lengths]
            + [pl.BlockSpec(memory_space=pltpu.SMEM)] * 2,
            scratch_shapes=[
                pltpu.VMEM((total, span), jnp.bfloat16),
                pltpu.VMEM((total + total // 5, span), jnp.bfloat16),
                pltpu.VMEM((total, span), jnp.bfloat16),
                pltpu.VMEM((total, span), jnp.bfloat16),
                pltpu.VMEM((total, span), jnp.bfloat16),
                pltpu.SMEM((count,), jnp.int32),
            ],
        ),
        out_shape=[jax.ShapeDtypeStruct((length, width), jnp.bfloat16) for length in lengths]
        + [jax.ShapeDtypeStruct((count,), jnp.int32), jax.ShapeDtypeStruct((1,), jnp.int32)],
        compiler_params=params(40),
        cost_estimate=pl.CostEstimate(
            flops=flops, bytes_accessed=8 * total * width, transcendentals=flops // 512
        ),
        name="attend",
    )(place, pltpu.with_memory_space_constraint(received[0], pltpu.HBM), *received[1:])


def gather_features(own, count, between=lambda arrived: arrived):
    half = own.shape[0] // 2
    held = {0: [own]}
    if count == 8:
        over_x = xor_permute(own, 2, count)
        over_y = xor_permute(own, 4, count)
        held[1] = [between(xor_permute(own, 1, count))]
        held[2], held[4] = [over_x], [over_y]
        held[6] = [xor_permute(over_x[:half], 4, count), xor_permute(over_y[half:], 2, count)]
    else:
        for mask in range(2, count, 2):
            held[mask] = [xor_permute(own, mask, count)]
        held[1] = [between(xor_permute(own, 1, count))]
    for mask in range(2, count, 2):
        held[mask + 1] = [xor_permute(piece, 1, count) for piece in held[mask]]
    return [held[mask] for mask in range(count)]


def unfilled(shape):
    def body(out_ref):
        pass

    return pl.pallas_call(
        body,
        out_specs=pl.BlockSpec(memory_space=pl.ANY),
        out_shape=shape,
        name="unfilled",
    )()


def project(place, group, counts, features, more, shards, rows):
    count = len(features)
    width = more.shape[2]
    total = count * rows
    always = total - more.shape[1]
    distances = sorted(shards)
    columns = shards[0].shape[1]
    each = shards[0].shape[0] // width
    bounds = [size for size in variants(total) if size <= always] + [total]
    flat = [piece for pieces in features for piece in pieces]

    def body(place_ref, group_ref, counts_ref, *refs):
        flat_refs = list(refs[: len(flat)])
        more_ref = refs[len(flat)]
        shard_refs = refs[len(flat) + 1 : len(flat) + 1 + len(distances)]
        out_refs = refs[len(flat) + 1 + len(distances) :][:count]
        landed, weight_all, sums, sems, weight_sems = refs[len(flat) + 1 + len(distances) + count :]
        used = sum(counts_ref[mask] for mask in range(count)) * BLOCK

        for mask in range(count):
            owner = place_ref[0] ^ mask
            apart = group_ref[0] - owner // each
            start = pl.multiple_of((owner % each) * width, width)
            lower = mask % 2 * width
            for distance, shard_ref in zip(distances, shard_refs):

                @pl.when(apart == distance)
                def _(mask=mask, start=start, lower=lower, shard_ref=shard_ref):
                    pltpu.make_async_copy(
                        shard_ref.at[pl.ds(start, width), :],
                        weight_all.at[mask // 2, lower : lower + width, :],
                        weight_sems.at[mask // 2],
                    ).start()

        below = 0
        for size in bounds:

            @pl.when((used > below) & (used <= size))
            def _(size=size):
                taken = 0
                for mask in range(count):
                    lanes = slice(mask % 2 * width, (mask % 2 + 1) * width)
                    sources = flat_refs[taken : taken + len(features[mask])]
                    taken += len(sources)
                    if size > always:
                        sources.append(more_ref.at[mask])
                    first = 0
                    for source in sources:
                        length = min(source.shape[0], size - first)
                        pltpu.make_async_copy(
                            source.at[:length, :],
                            landed.at[mask // 2, first : first + length, lanes],
                            sems.at[mask // 2],
                        ).start()
                        first += length
                sums[:size, :] = jnp.zeros((size, columns), jnp.float32)

                def pair(index, carry):
                    for buffer, sem in (
                        (weight_all.at[index], weight_sems.at[index]),
                        (landed.at[index, :size, :], sems.at[index]),
                    ):
                        pltpu.make_async_copy(buffer, buffer, sem).wait()
                    sums[:size, :] += jnp.dot(
                        landed[index, :size, :],
                        weight_all[index],
                        preferred_element_type=jnp.float32,
                    )
                    return carry

                lax.fori_loop(0, count // 2, pair, 0)

            below = size
        for mask in range(count):
            position = 0
            for view in range(count):
                position = position + jnp.where(
                    view < (place_ref[0] ^ mask), counts_ref[place_ref[0] ^ view], 0
                )
            moved = sums[rows_at(position * BLOCK, rows), :]
            out_refs[mask][...] = moved.astype(jnp.bfloat16)

    any_spec = pl.BlockSpec(memory_space=pl.ANY)
    inputs = flat + [more]
    inputs += [shards[distance] for distance in distances]
    inputs = [pltpu.with_memory_space_constraint(array, pltpu.HBM) for array in inputs]
    return pl.pallas_call(
        body,
        grid_spec=pltpu.PrefetchScalarGridSpec(
            num_scalar_prefetch=3,
            grid=(1,),
            in_specs=[any_spec] * len(inputs),
            out_specs=[full_spec((rows, columns))] * count,
            scratch_shapes=[
                pltpu.VMEM((count // 2, total, 2 * width), jnp.bfloat16),
                pltpu.VMEM((count // 2, 2 * width, columns), jnp.bfloat16),
                pltpu.VMEM((total, columns), jnp.float32),
                pltpu.SemaphoreType.DMA((count // 2,)),
                pltpu.SemaphoreType.DMA((count // 2,)),
            ],
        ),
        out_shape=[jax.ShapeDtypeStruct((rows, columns), jnp.bfloat16)] * count,
        compiler_params=params(56),
        cost_estimate=pl.CostEstimate(
            flops=total * count * width * columns,
            bytes_accessed=total * count * width,
            transcendentals=0,
        ),
        name="project",
    )(place, group, counts, *inputs)


def assemble(place, block_counts, row_mask, pieces, count):
    rows, columns = pieces[0].shape
    if columns % HEAD_DIM:
        stacked = jnp.stack(pieces)[jnp.arange(count) ^ place[0]]
        result = jnp.moveaxis(stacked, 0, 1).reshape(rows, count * columns)
        offsets = jnp.arange(rows, dtype=jnp.int32)
        good = (row_mask[0] == 1) & (offsets // BLOCK < block_counts[0, 0])
        return jnp.where(good[:, None], result, jnp.bfloat16(0.0))

    def body(place_ref, blocks_ref, mask_ref, *refs):
        out_ref = refs[-1]
        good = valid_column(mask_ref, blocks_ref[0, 0]) > 0.5
        for mask in range(count):
            start = pl.multiple_of((place_ref[0] ^ mask) * columns, HEAD_DIM)
            out_ref[:, pl.ds(start, columns)] = jnp.where(
                good, refs[mask][...], jnp.bfloat16(0.0)
            )

    return pl.pallas_call(
        body,
        grid_spec=pltpu.PrefetchScalarGridSpec(
            num_scalar_prefetch=2,
            grid=(1,),
            in_specs=[full_spec((1, rows))] + [full_spec((rows, columns))] * count,
            out_specs=full_spec((rows, count * columns)),
        ),
        out_shape=jax.ShapeDtypeStruct((rows, count * columns), jnp.bfloat16),
        compiler_params=params(16),
        cost_estimate=pl.CostEstimate(
            flops=0, bytes_accessed=4 * rows * count * columns, transcendentals=0
        ),
        name="assemble",
    )(
        place,
        block_counts,
        row_mask,
        pltpu.with_memory_space_constraint(pieces[0], pltpu.HBM),
        *pieces[1:],
    )


def local(queries, keys, values, out_weight, block_counts, row_mask):
    rows = queries.shape[1]
    count = lax.axis_size("cam")
    total = count * rows
    place_array = jnp.full((1,), lax.axis_index("cam"), jnp.int32)
    group_array = jnp.full((1,), lax.axis_index("fsdp"), jnp.int32)

    shards = {0: cut_weight(place_array, out_weight, count)}
    queries, shards[0] = lax.optimization_barrier((queries, shards[0]))
    payloads = pack(place_array, block_counts, row_mask, queries, keys, values, count)
    groups = lax.axis_size("fsdp")

    received = [payloads[0]] + [None] * (count - 1)
    early = [mask for mask in order(count) if mask & 1 == 0]
    late = [mask for mask in order(count) if mask & 1]
    pass_weight(shards, 1)
    for mask in early:
        received[mask] = xor_permute(payloads[mask], mask, count)
    received, payloads, shards[1], shards[-1] = lax.optimization_barrier(
        (received, payloads, shards[1], shards[-1])
    )
    pass_weight(shards, 2)
    for mask in late:
        received[mask] = xor_permute(payloads[mask], mask, count)
    always = total * 3 // 5
    attended, rest, counts, used = attend(
        place_array, received, rows, (always, total - always)
    )
    shape = jax.ShapeDtypeStruct((count,) + rest.shape, rest.dtype)

    def gather_rest(part):
        return jnp.stack([jnp.concatenate(pieces) for pieces in gather_features(part, count)])

    def weight_step(arrived):
        arrived, shards[2], shards[-2] = lax.optimization_barrier((arrived, shards[2], shards[-2]))
        pass_weight(shards, 3)
        return arrived

    features = gather_features(attended, count, weight_step)
    for distance in range(4, groups):
        pass_weight(shards, distance)
    rest, features, shards = lax.optimization_barrier((rest, features, shards))
    more = lax.cond(used[0] > always, gather_rest, lambda part: unfilled(shape), rest)
    pieces = project(place_array, group_array, counts, features, more, shards, rows)
    landed = [pieces[0]] + [None] * (count - 1)
    for mask in order(count):
        landed[mask] = xor_permute(pieces[mask], mask, count)
    return assemble(place_array, block_counts, row_mask, landed, count)[None]


def solution(mesh):
    in_specs = (
        P("fsdp", "cam", None),
        P("fsdp", "cam", None),
        P("fsdp", "cam", None),
        P("fsdp", None),
        P("fsdp", "cam"),
        P("fsdp", "cam"),
    )
    out_specs = P("fsdp", "cam", None)
    return jax.shard_map(local, mesh=mesh, in_specs=in_specs, out_specs=out_specs, check_vma=False)
```

```python
import math

import jax
import jax.numpy as jnp
from jax import lax
from jax.experimental import pallas as pl
from jax.experimental.pallas import tpu as pltpu
from jax.sharding import PartitionSpec as P

HEAD_DIM = 128
BLOCK = 32
SENTINEL = 32.0
LIMIT = 24.0
UNIT = 128


def params(mebibytes):
    return pltpu.CompilerParams(vmem_limit_bytes=mebibytes * 1024 * 1024)


def order(count):
    return sorted(range(1, count), key=lambda mask: (mask == 1, mask & 1, -bin(mask).count("1")))


def variants(total):
    return sorted({-(-total * tenths // (10 * UNIT)) * UNIT for tenths in (4, 5, 6, 8, 10)})


def full_spec(shape):
    return pl.BlockSpec(shape, lambda i, *_: (0,) * len(shape))


def column_of(row):
    n = row.shape[1]
    diagonal = lax.broadcasted_iota(jnp.int32, (n, n), 0) == lax.broadcasted_iota(
        jnp.int32, (n, n), 1
    )
    return jnp.sum(jnp.where(diagonal, row, 0.0), axis=1, keepdims=True)


def valid_column(mask_ref, blocks):
    rows = mask_ref.shape[1]
    inside = lax.broadcasted_iota(jnp.int32, (1, rows), 1) < blocks * BLOCK
    return column_of(jnp.where((mask_ref[...] == 1) & inside, 1.0, 0.0))


def xor_permute(array, mask, count):
    return lax.ppermute(array, "cam", [(place, place ^ mask) for place in range(count)])


def cut_weight(place, out_weight, count):
    depth = out_weight.shape[0]
    columns = out_weight.shape[1] // count
    if columns % HEAD_DIM:
        return lax.dynamic_slice_in_dim(out_weight, place[0] * columns, columns, axis=1)
    parts = 4
    step = depth // parts

    def body(place_ref, w_ref, out_ref, held, load_sems, store_sems):
        start = pl.multiple_of(place_ref[0] * columns, HEAD_DIM)
        loads, stores = [], []
        for part in range(parts):
            inside = pl.ds(part * step, step)
            load = pltpu.make_async_copy(
                w_ref.at[inside, pl.ds(start, columns)], held.at[part], load_sems.at[part]
            )
            load.start()
            loads.append(load)
        for part in range(parts):
            inside = pl.ds(part * step, step)
            loads[part].wait()
            store = pltpu.make_async_copy(held.at[part], out_ref.at[inside, :], store_sems.at[part])
            store.start()
            stores.append(store)
        for store in stores:
            store.wait()

    return pl.pallas_call(
        body,
        grid_spec=pltpu.PrefetchScalarGridSpec(
            num_scalar_prefetch=1,
            grid=(1,),
            in_specs=[pl.BlockSpec(memory_space=pl.ANY)],
            out_specs=pl.BlockSpec(memory_space=pl.ANY),
            scratch_shapes=[
                pltpu.VMEM((parts, step, columns), jnp.bfloat16),
                pltpu.SemaphoreType.DMA((parts,)),
                pltpu.SemaphoreType.DMA((parts,)),
            ],
        ),
        out_shape=jax.ShapeDtypeStruct((depth, columns), jnp.bfloat16),
        compiler_params=params(56),
        cost_estimate=pl.CostEstimate(
            flops=0, bytes_accessed=4 * depth * columns, transcendentals=0
        ),
        name="cut_weight",
    )(place, out_weight)


def pack(place, block_counts, row_mask, queries, keys, values, count):
    _, rows, features = queries.shape
    width = features // count

    def body(place_ref, blocks_ref, mask_ref, q_ref, k_ref, v_ref, *refs):
        out_refs = refs[:count]
        held, key_out, load_sems, sems = refs[count:]
        loads = []
        for slot, ref in enumerate((k_ref, q_ref, v_ref)):
            load = pltpu.make_async_copy(ref.at[0], held.at[slot], load_sems.at[slot])
            load.start()
            loads.append(load)
        starts = [pl.multiple_of((place_ref[0] ^ m) * width, HEAD_DIM) for m in range(count)]
        good = valid_column(mask_ref, blocks_ref[0, 0]) > 0.5
        copies = []

        def send(source, target, sem):
            copy = pltpu.make_async_copy(source, target, sem)
            copy.start()
            copies.append(copy)

        loads[0].wait()
        for mask in range(count):
            part = held[0, :, pl.ds(starts[mask], width)]
            key_out[mask] = jnp.where(good, part, jnp.bfloat16(SENTINEL))
            send(key_out.at[mask], out_refs[mask].at[1], sems.at[mask, 1])
        for slot, target in ((1, 0), (2, 2)):
            loads[slot].wait()
            for mask in range(count):
                source = held.at[slot, :, pl.ds(starts[mask], width)]
                send(source, out_refs[mask].at[target], sems.at[mask, target])
        for copy in copies:
            copy.wait()

    any_spec = pl.BlockSpec(memory_space=pl.ANY)
    return pl.pallas_call(
        body,
        grid_spec=pltpu.PrefetchScalarGridSpec(
            num_scalar_prefetch=2,
            grid=(1,),
            in_specs=[full_spec((1, rows))] + [any_spec] * 3,
            out_specs=[any_spec] * count,
            scratch_shapes=[
                pltpu.VMEM((3, rows, features), jnp.bfloat16),
                pltpu.VMEM((count, rows, width), jnp.bfloat16),
                pltpu.SemaphoreType.DMA((3,)),
                pltpu.SemaphoreType.DMA((count, 3)),
            ],
        ),
        out_shape=[jax.ShapeDtypeStruct((3, rows, width), jnp.bfloat16)] * count,
        compiler_params=params(56),
        cost_estimate=pl.CostEstimate(
            flops=0, bytes_accessed=12 * rows * features, transcendentals=0
        ),
        name="pack",
    )(place, block_counts, row_mask, queries, keys, values)


def pass_weight(shards, distance):
    groups = lax.axis_size("fsdp")
    for sign in (1, -1):
        pairs = []
        for source in range(groups):
            origin, target = source - sign * (distance - 1), source + sign
            if 0 <= origin < groups and 0 <= target < groups:
                pairs.append((source, target))
        shards[sign * distance] = lax.ppermute(shards[sign * (distance - 1)], "fsdp", pairs)


def packed_offsets(place_ref, counts_ref, table, count):
    by_mask, running = [], 0
    for mask in range(count):
        by_mask.append(running)
        table[mask] = running
        running = running + counts_ref[mask] * BLOCK
    by_view, position = [], 0
    for view in range(count):
        by_view.append(position)
        position = position + counts_ref[place_ref[0] ^ view] * BLOCK
    return by_mask, by_view, running


def rows_at(start, size):
    return pl.ds(start if isinstance(start, int) else pl.multiple_of(start, BLOCK), size)


def tile_of(size):
    return max(rows for rows in range(UNIT, 6 * UNIT + 1, UNIT) if size % rows == 0)


def attend(place, received, rows, lengths):
    count = len(received)
    width = received[0].shape[2]
    total = count * rows
    span = 2 * HEAD_DIM
    factor = math.log2(math.e) / math.sqrt(HEAD_DIM)

    def body(place_ref, *refs):
        parts = refs[:count]
        out_refs = refs[count : count + len(lengths)]
        counts_ref, used_ref = refs[count + len(lengths) : count + len(lengths) + 2]
        query_all, key_all, value_all, result, ordered, table = refs[count + len(lengths) + 2 :]

        @pl.when(pl.program_id(0) == 0)
        def _():
            value_all[...] = jnp.zeros_like(value_all)
            for mask in range(count):
                blocks = jnp.zeros((1, HEAD_DIM), jnp.float32)
                for first in range(0, rows, BLOCK):
                    row = parts[mask][1, first : first + 16, :HEAD_DIM].astype(jnp.float32)[:1]
                    blocks = blocks + jnp.where(row < LIMIT, 1.0, 0.0)
                counts_ref[mask] = jnp.max(blocks).astype(jnp.int32)

        by_mask, by_view, used = packed_offsets(place_ref, counts_ref, table, count)
        used_ref[0] = used
        for mask in range(count):
            where = rows_at(by_mask[mask], rows)
            query_all[where, :] = parts[mask][0]
            key_all[where, :] = parts[mask][1]
            value_all[where, :] = parts[mask][2]
        key_all[rows_at(used, total // 5), :] = jnp.full((total // 5, span), SENTINEL, jnp.bfloat16)
        below = 0
        for size in variants(total):

            @pl.when((used > below) & (used <= size))
            def _(size=size):
                step = tile_of(size)
                key_mask = key_all[:size, :HEAD_DIM].astype(jnp.float32) > LIMIT
                bias = jnp.where(key_mask, jnp.float32(-1e30), 0.0)
                bias = jnp.concatenate([bias] * (step // HEAD_DIM), axis=1)
                values_t = [
                    value_all[:size, first : first + HEAD_DIM].T
                    for first in range(0, span, HEAD_DIM)
                ]

                def tile(index, carry):
                    if isinstance(index, int):
                        where = pl.ds(index * step, step)
                    else:
                        where = pl.ds(pl.multiple_of(index * step, UNIT), step)
                    for head in range(span // HEAD_DIM):
                        lanes = slice(head * HEAD_DIM, (head + 1) * HEAD_DIM)
                        scores = lax.dot_general(
                            key_all[:size, lanes],
                            query_all[where, lanes],
                            (((1,), (1,)), ((), ())),
                            preferred_element_type=jnp.float32,
                        )
                        scores = scores + bias
                        top = jnp.max(scores, axis=0, keepdims=True)
                        raised = jnp.exp2((scores - top) * factor)
                        norm = jnp.sum(raised, axis=0, keepdims=True)
                        summed = jnp.dot(
                            values_t[head],
                            raised.astype(jnp.bfloat16),
                            preferred_element_type=jnp.float32,
                        )
                        result[where, lanes] = (summed / norm).T.astype(jnp.bfloat16)
                    return carry

                if size == step:
                    tile(0, 0)
                else:
                    lax.fori_loop(0, size // step, tile, 0)

            below = size
        for view in range(count):
            moved = result[rows_at(table[place_ref[0] ^ view], rows), :]
            ordered[rows_at(by_view[view], rows), :] = moved
        first = 0
        for length, out_ref in zip(lengths, out_refs):
            out_ref[...] = ordered[first : first + length, :]
            first += length

    flops = 4 * total * total * width // 25
    return pl.pallas_call(
        body,
        grid_spec=pltpu.PrefetchScalarGridSpec(
            num_scalar_prefetch=1,
            grid=(width // span,),
            in_specs=[pl.BlockSpec((3, rows, span), lambda h, *_: (0, 0, h))] * count,
            out_specs=[pl.BlockSpec((length, span), lambda h, *_: (0, h)) for length in lengths]
            + [pl.BlockSpec(memory_space=pltpu.SMEM)] * 2,
            scratch_shapes=[
                pltpu.VMEM((total, span), jnp.bfloat16),
                pltpu.VMEM((total + total // 5, span), jnp.bfloat16),
                pltpu.VMEM((total, span), jnp.bfloat16),
                pltpu.VMEM((total, span), jnp.bfloat16),
                pltpu.VMEM((total, span), jnp.bfloat16),
                pltpu.SMEM((count,), jnp.int32),
            ],
        ),
        out_shape=[jax.ShapeDtypeStruct((length, width), jnp.bfloat16) for length in lengths]
        + [jax.ShapeDtypeStruct((count,), jnp.int32), jax.ShapeDtypeStruct((1,), jnp.int32)],
        compiler_params=params(40),
        cost_estimate=pl.CostEstimate(
            flops=flops, bytes_accessed=total * width, transcendentals=flops // 512
        ),
        name="attend",
    )(place, pltpu.with_memory_space_constraint(received[0], pltpu.HBM), *received[1:])


def gather_features(own, count, between=lambda arrived: arrived):
    half = own.shape[0] // 2
    held = {0: [own]}
    if count == 8:
        over_x = xor_permute(own, 2, count)
        over_y = xor_permute(own, 4, count)
        held[1] = [between(xor_permute(own, 1, count))]
        held[2], held[4] = [over_x], [over_y]
        held[6] = [xor_permute(over_x[:half], 4, count), xor_permute(over_y[half:], 2, count)]
    else:
        for mask in range(2, count, 2):
            held[mask] = [xor_permute(own, mask, count)]
        held[1] = [between(xor_permute(own, 1, count))]
    for mask in range(2, count, 2):
        held[mask + 1] = [xor_permute(piece, 1, count) for piece in held[mask]]
    return [held[mask] for mask in range(count)]


def unfilled(shape):
    def body(out_ref):
        pass

    return pl.pallas_call(
        body,
        out_specs=pl.BlockSpec(memory_space=pl.ANY),
        out_shape=shape,
        name="unfilled",
    )()


def project(place, group, counts, features, more, shards, rows):
    count = len(features)
    width = more.shape[2]
    total = count * rows
    always = total - more.shape[1]
    distances = sorted(shards)
    columns = shards[0].shape[1]
    each = shards[0].shape[0] // width
    bounds = [size for size in variants(total) if size <= always] + [total]
    flat = [piece for pieces in features for piece in pieces]

    def body(place_ref, group_ref, counts_ref, *refs):
        flat_refs = list(refs[: len(flat)])
        more_ref = refs[len(flat)]
        shard_refs = refs[len(flat) + 1 : len(flat) + 1 + len(distances)]
        out_refs = refs[len(flat) + 1 + len(distances) :][:count]
        landed, weight_all, sums, sems, weight_sems = refs[len(flat) + 1 + len(distances) + count :]
        used = sum(counts_ref[mask] for mask in range(count)) * BLOCK

        def send_weight(mask):
            owner = place_ref[0] ^ mask
            apart = group_ref[0] - owner // each
            start = pl.multiple_of((owner % each) * width, width)
            lower = mask % 2 * width
            for distance, shard_ref in zip(distances, shard_refs):

                @pl.when(apart == distance)
                def _():
                    pltpu.make_async_copy(
                        shard_ref.at[pl.ds(start, width), :],
                        weight_all.at[mask // 2, lower : lower + width, :],
                        weight_sems.at[mask // 2],
                    ).start()

        below = 0
        for size in bounds:

            @pl.when((used > below) & (used <= size))
            def _(size=size):
                taken = 0
                for mask in range(count):
                    send_weight(mask)
                    lanes = slice(mask % 2 * width, (mask % 2 + 1) * width)
                    sources = flat_refs[taken : taken + len(features[mask])]
                    taken += len(sources)
                    if size > always:
                        sources.append(more_ref.at[mask])
                    first = 0
                    for source in sources:
                        length = min(source.shape[0], size - first)
                        pltpu.make_async_copy(
                            source.at[:length, :],
                            landed.at[mask // 2, first : first + length, lanes],
                            sems.at[mask // 2],
                        ).start()
                        first += length
                sums[:size, :] = jnp.zeros((size, columns), jnp.float32)

                def pair(index, carry):
                    for buffer, sem in (
                        (weight_all.at[index], weight_sems.at[index]),
                        (landed.at[index, :size, :], sems.at[index]),
                    ):
                        pltpu.make_async_copy(buffer, buffer, sem).wait()
                    sums[:size, :] += jnp.dot(
                        landed[index, :size, :],
                        weight_all[index],
                        preferred_element_type=jnp.float32,
                    )
                    return carry

                lax.fori_loop(0, count // 2, pair, 0)

            below = size
        for mask in range(count):
            position = 0
            for view in range(count):
                position = position + jnp.where(
                    view < (place_ref[0] ^ mask), counts_ref[place_ref[0] ^ view], 0
                )
            moved = sums[rows_at(position * BLOCK, rows), :]
            out_refs[mask][...] = moved.astype(jnp.bfloat16)

    any_spec = pl.BlockSpec(memory_space=pl.ANY)
    inputs = flat + [more]
    inputs += [shards[distance] for distance in distances]
    inputs = [pltpu.with_memory_space_constraint(array, pltpu.HBM) for array in inputs]
    return pl.pallas_call(
        body,
        grid_spec=pltpu.PrefetchScalarGridSpec(
            num_scalar_prefetch=3,
            grid=(1,),
            in_specs=[any_spec] * len(inputs),
            out_specs=[full_spec((rows, columns))] * count,
            scratch_shapes=[
                pltpu.VMEM((count // 2, total, 2 * width), jnp.bfloat16),
                pltpu.VMEM((count // 2, 2 * width, columns), jnp.bfloat16),
                pltpu.VMEM((total, columns), jnp.float32),
                pltpu.SemaphoreType.DMA((count // 2,)),
                pltpu.SemaphoreType.DMA((count // 2,)),
            ],
        ),
        out_shape=[jax.ShapeDtypeStruct((rows, columns), jnp.bfloat16)] * count,
        compiler_params=params(56),
        cost_estimate=pl.CostEstimate(
            flops=total * count * width * columns,
            bytes_accessed=total * count * width,
            transcendentals=0,
        ),
        name="project",
    )(place, group, counts, *inputs)


def assemble(place, block_counts, row_mask, pieces, count):
    rows, columns = pieces[0].shape
    if columns % HEAD_DIM:
        stacked = jnp.stack(pieces)[jnp.arange(count) ^ place[0]]
        result = jnp.moveaxis(stacked, 0, 1).reshape(rows, count * columns)
        offsets = jnp.arange(rows, dtype=jnp.int32)
        good = (row_mask[0] == 1) & (offsets // BLOCK < block_counts[0, 0])
        return jnp.where(good[:, None], result, jnp.bfloat16(0.0))

    def body(place_ref, blocks_ref, mask_ref, *refs):
        piece_refs, out_ref = refs[:count], refs[count]
        held, masked, load_sems, store_sems = refs[count + 1 :]
        loads, stores = [], []
        for mask in range(count):
            load = pltpu.make_async_copy(piece_refs[mask], held.at[mask], load_sems.at[mask])
            load.start()
            loads.append(load)
        good = valid_column(mask_ref, blocks_ref[0, 0]) > 0.5
        for mask in range(count):
            loads[mask].wait()
            masked[mask] = jnp.where(good, held[mask], jnp.bfloat16(0.0))
            start = pl.multiple_of((place_ref[0] ^ mask) * columns, HEAD_DIM)
            store = pltpu.make_async_copy(
                masked.at[mask], out_ref.at[:, pl.ds(start, columns)], store_sems.at[mask]
            )
            store.start()
            stores.append(store)
        for store in stores:
            store.wait()

    any_spec = pl.BlockSpec(memory_space=pl.ANY)
    return pl.pallas_call(
        body,
        grid_spec=pltpu.PrefetchScalarGridSpec(
            num_scalar_prefetch=2,
            grid=(1,),
            in_specs=[full_spec((1, rows))] + [any_spec] * count,
            out_specs=any_spec,
            scratch_shapes=[
                pltpu.VMEM((count, rows, columns), jnp.bfloat16),
                pltpu.VMEM((count, rows, columns), jnp.bfloat16),
                pltpu.SemaphoreType.DMA((count,)),
                pltpu.SemaphoreType.DMA((count,)),
            ],
        ),
        out_shape=jax.ShapeDtypeStruct((rows, count * columns), jnp.bfloat16),
        compiler_params=params(16),
        cost_estimate=pl.CostEstimate(
            flops=0, bytes_accessed=4 * rows * count * columns, transcendentals=0
        ),
        name="assemble",
    )(
        place,
        block_counts,
        row_mask,
        pltpu.with_memory_space_constraint(pieces[0], pltpu.HBM),
        *pieces[1:],
    )


def local(queries, keys, values, out_weight, block_counts, row_mask):
    rows = queries.shape[1]
    count = lax.axis_size("cam")
    total = count * rows
    place_array = jnp.full((1,), lax.axis_index("cam"), jnp.int32)
    group_array = jnp.full((1,), lax.axis_index("fsdp"), jnp.int32)

    shards = {0: cut_weight(place_array, out_weight, count)}
    queries, shards[0] = lax.optimization_barrier((queries, shards[0]))
    payloads = pack(place_array, block_counts, row_mask, queries, keys, values, count)
    groups = lax.axis_size("fsdp")

    received = [payloads[0]] + [None] * (count - 1)
    early = [mask for mask in order(count) if mask & 1 == 0]
    late = [mask for mask in order(count) if mask & 1]
    pass_weight(shards, 1)
    for mask in early:
        received[mask] = xor_permute(payloads[mask], mask, count)
    received, payloads, shards[1], shards[-1] = lax.optimization_barrier(
        (received, payloads, shards[1], shards[-1])
    )
    pass_weight(shards, 2)
    for mask in late:
        received[mask] = xor_permute(payloads[mask], mask, count)
    always = total * 3 // 5
    attended, rest, counts, used = attend(
        place_array, received, rows, (always, total - always)
    )
    shape = jax.ShapeDtypeStruct((count,) + rest.shape, rest.dtype)

    def gather_rest(part):
        return jnp.stack([jnp.concatenate(pieces) for pieces in gather_features(part, count)])

    def weight_step(arrived):
        arrived, shards[2], shards[-2] = lax.optimization_barrier((arrived, shards[2], shards[-2]))
        pass_weight(shards, 3)
        return arrived

    features = gather_features(attended, count, weight_step)
    for distance in range(4, groups):
        pass_weight(shards, distance)
    rest, features, shards = lax.optimization_barrier((rest, features, shards))
    more = lax.cond(used[0] > always, gather_rest, lambda part: unfilled(shape), rest)
    pieces = project(place_array, group_array, counts, features, more, shards, rows)
    landed = [pieces[0]] + [None] * (count - 1)
    for mask in order(count):
        landed[mask] = xor_permute(pieces[mask], mask, count)
    return assemble(place_array, block_counts, row_mask, landed, count)[None]


def solution(mesh):
    in_specs = (
        P("fsdp", "cam", None),
        P("fsdp", "cam", None),
        P("fsdp", "cam", None),
        P("fsdp", None),
        P("fsdp", "cam"),
        P("fsdp", "cam"),
    )
    out_specs = P("fsdp", "cam", None)
    return jax.shard_map(local, mesh=mesh, in_specs=in_specs, out_specs=out_specs, check_vma=False)
```

```python
import math

import jax
import jax.numpy as jnp
from jax import lax
from jax.experimental import pallas as pl
from jax.experimental.pallas import tpu as pltpu
from jax.sharding import PartitionSpec as P

HEAD_DIM = 128
BLOCK = 32
SENTINEL = 32.0
LIMIT = 24.0
UNIT = 128


def params(mebibytes):
    return pltpu.CompilerParams(vmem_limit_bytes=mebibytes * 1024 * 1024)


def order(count):
    return sorted(range(1, count), key=lambda mask: (mask == 1, mask & 1, -bin(mask).count("1")))


def variants(total):
    return sorted({-(-total * tenths // (10 * UNIT)) * UNIT for tenths in (4, 5, 6, 8, 10)})


def full_spec(shape):
    return pl.BlockSpec(shape, lambda i, *_: (0,) * len(shape))


def column_of(row):
    n = row.shape[1]
    diagonal = lax.broadcasted_iota(jnp.int32, (n, n), 0) == lax.broadcasted_iota(
        jnp.int32, (n, n), 1
    )
    return jnp.sum(jnp.where(diagonal, row, 0.0), axis=1, keepdims=True)


def valid_column(mask_ref, blocks):
    rows = mask_ref.shape[1]
    inside = lax.broadcasted_iota(jnp.int32, (1, rows), 1) < blocks * BLOCK
    return column_of(jnp.where((mask_ref[...] == 1) & inside, 1.0, 0.0))


def xor_permute(array, mask, count):
    return lax.ppermute(array, "cam", [(place, place ^ mask) for place in range(count)])


def cut_weight(place, out_weight, count):
    depth = out_weight.shape[0]
    columns = out_weight.shape[1] // count
    if columns % HEAD_DIM:
        return lax.dynamic_slice_in_dim(out_weight, place[0] * columns, columns, axis=1)
    parts = 4
    step = depth // parts

    def body(place_ref, w_ref, out_ref, held, load_sems, store_sems):
        start = pl.multiple_of(place_ref[0] * columns, HEAD_DIM)
        loads, stores = [], []
        for part in range(parts):
            inside = pl.ds(part * step, step)
            load = pltpu.make_async_copy(
                w_ref.at[inside, pl.ds(start, columns)], held.at[part], load_sems.at[part]
            )
            load.start()
            loads.append(load)
        for part in range(parts):
            inside = pl.ds(part * step, step)
            loads[part].wait()
            store = pltpu.make_async_copy(held.at[part], out_ref.at[inside, :], store_sems.at[part])
            store.start()
            stores.append(store)
        for store in stores:
            store.wait()

    return pl.pallas_call(
        body,
        grid_spec=pltpu.PrefetchScalarGridSpec(
            num_scalar_prefetch=1,
            grid=(1,),
            in_specs=[pl.BlockSpec(memory_space=pl.ANY)],
            out_specs=pl.BlockSpec(memory_space=pl.ANY),
            scratch_shapes=[
                pltpu.VMEM((parts, step, columns), jnp.bfloat16),
                pltpu.SemaphoreType.DMA((parts,)),
                pltpu.SemaphoreType.DMA((parts,)),
            ],
        ),
        out_shape=jax.ShapeDtypeStruct((depth, columns), jnp.bfloat16),
        compiler_params=params(56),
        cost_estimate=pl.CostEstimate(
            flops=0, bytes_accessed=4 * depth * columns, transcendentals=0
        ),
        name="cut_weight",
    )(place, out_weight)


def pack(place, block_counts, row_mask, queries, keys, values, count):
    _, rows, features = queries.shape
    width = features // count

    def body(place_ref, blocks_ref, mask_ref, q_ref, k_ref, v_ref, *refs):
        out_refs = refs[:count]
        held, key_out, load_sems, sems = refs[count:]
        loads = []
        for slot, ref in enumerate((k_ref, q_ref, v_ref)):
            load = pltpu.make_async_copy(ref.at[0], held.at[slot], load_sems.at[slot])
            load.start()
            loads.append(load)
        starts = [pl.multiple_of((place_ref[0] ^ m) * width, HEAD_DIM) for m in range(count)]
        good = valid_column(mask_ref, blocks_ref[0, 0]) > 0.5
        copies = []

        def send(source, target, sem):
            copy = pltpu.make_async_copy(source, target, sem)
            copy.start()
            copies.append(copy)

        loads[0].wait()
        for mask in range(count):
            part = held[0, :, pl.ds(starts[mask], width)]
            key_out[mask] = jnp.where(good, part, jnp.bfloat16(SENTINEL))
            send(key_out.at[mask], out_refs[mask].at[1], sems.at[mask, 1])
        for slot, target in ((1, 0), (2, 2)):
            loads[slot].wait()
            for mask in range(count):
                source = held.at[slot, :, pl.ds(starts[mask], width)]
                send(source, out_refs[mask].at[target], sems.at[mask, target])
        for copy in copies:
            copy.wait()

    any_spec = pl.BlockSpec(memory_space=pl.ANY)
    return pl.pallas_call(
        body,
        grid_spec=pltpu.PrefetchScalarGridSpec(
            num_scalar_prefetch=2,
            grid=(1,),
            in_specs=[full_spec((1, rows))] + [any_spec] * 3,
            out_specs=[any_spec] * count,
            scratch_shapes=[
                pltpu.VMEM((3, rows, features), jnp.bfloat16),
                pltpu.VMEM((count, rows, width), jnp.bfloat16),
                pltpu.SemaphoreType.DMA((3,)),
                pltpu.SemaphoreType.DMA((count, 3)),
            ],
        ),
        out_shape=[jax.ShapeDtypeStruct((3, rows, width), jnp.bfloat16)] * count,
        compiler_params=params(56),
        cost_estimate=pl.CostEstimate(
            flops=0, bytes_accessed=12 * rows * features, transcendentals=0
        ),
        name="pack",
    )(place, block_counts, row_mask, queries, keys, values)


def pass_weight(shards, distance):
    groups = lax.axis_size("fsdp")
    for sign in (1, -1):
        pairs = []
        for source in range(groups):
            origin, target = source - sign * (distance - 1), source + sign
            if 0 <= origin < groups and 0 <= target < groups:
                pairs.append((source, target))
        shards[sign * distance] = lax.ppermute(shards[sign * (distance - 1)], "fsdp", pairs)


def packed_offsets(place_ref, counts_ref, table, count):
    by_mask, running = [], 0
    for mask in range(count):
        by_mask.append(running)
        table[mask] = running
        running = running + counts_ref[mask] * BLOCK
    by_view, position = [], 0
    for view in range(count):
        by_view.append(position)
        position = position + counts_ref[place_ref[0] ^ view] * BLOCK
    return by_mask, by_view, running


def rows_at(start, size):
    return pl.ds(start if isinstance(start, int) else pl.multiple_of(start, BLOCK), size)


def tile_of(size):
    return max(rows for rows in range(UNIT, 6 * UNIT + 1, UNIT) if size % rows == 0)


def attend(place, received, rows, lengths):
    count = len(received)
    width = received[0].shape[2]
    total = count * rows
    span = 2 * HEAD_DIM
    factor = math.log2(math.e) / math.sqrt(HEAD_DIM)

    def body(place_ref, *refs):
        parts = refs[:count]
        out_refs = refs[count : count + len(lengths)]
        counts_ref, used_ref = refs[count + len(lengths) : count + len(lengths) + 2]
        query_all, key_all, value_all, result, ordered, table = refs[count + len(lengths) + 2 :]

        @pl.when(pl.program_id(0) == 0)
        def _():
            value_all[...] = jnp.zeros_like(value_all)
            for mask in range(count):
                blocks = jnp.zeros((1, HEAD_DIM), jnp.float32)
                for first in range(0, rows, BLOCK):
                    row = parts[mask][1, first : first + 16, :HEAD_DIM].astype(jnp.float32)[:1]
                    blocks = blocks + jnp.where(row < LIMIT, 1.0, 0.0)
                counts_ref[mask] = jnp.max(blocks).astype(jnp.int32)

        by_mask, by_view, used = packed_offsets(place_ref, counts_ref, table, count)
        used_ref[0] = used
        for mask in range(count):
            where = rows_at(by_mask[mask], rows)
            query_all[where, :] = parts[mask][0]
            key_all[where, :] = parts[mask][1]
            value_all[where, :] = parts[mask][2]
        key_all[rows_at(used, total // 5), :] = jnp.full((total // 5, span), SENTINEL, jnp.bfloat16)
        below = 0
        for size in variants(total):

            @pl.when((used > below) & (used <= size))
            def _(size=size):
                step = tile_of(size)
                key_mask = key_all[:size, :HEAD_DIM].astype(jnp.float32) > LIMIT
                bias = jnp.where(key_mask, jnp.float32(-1e30), 0.0)
                bias = jnp.concatenate([bias] * (step // HEAD_DIM), axis=1)
                values_t = [
                    value_all[:size, first : first + HEAD_DIM].T
                    for first in range(0, span, HEAD_DIM)
                ]

                def tile(index, carry):
                    if isinstance(index, int):
                        where = pl.ds(index * step, step)
                    else:
                        where = pl.ds(pl.multiple_of(index * step, UNIT), step)
                    for head in range(span // HEAD_DIM):
                        lanes = slice(head * HEAD_DIM, (head + 1) * HEAD_DIM)
                        scores = lax.dot_general(
                            key_all[:size, lanes],
                            query_all[where, lanes],
                            (((1,), (1,)), ((), ())),
                            preferred_element_type=jnp.float32,
                        )
                        scores = scores + bias
                        top = jnp.max(scores, axis=0, keepdims=True)
                        raised = jnp.exp2((scores - top) * factor)
                        norm = jnp.sum(raised, axis=0, keepdims=True)
                        summed = jnp.dot(
                            values_t[head],
                            raised.astype(jnp.bfloat16),
                            preferred_element_type=jnp.float32,
                        )
                        result[where, lanes] = (summed / norm).T.astype(jnp.bfloat16)
                    return carry

                if size == step:
                    tile(0, 0)
                else:
                    lax.fori_loop(0, size // step, tile, 0)

            below = size
        for view in range(count):
            moved = result[rows_at(table[place_ref[0] ^ view], rows), :]
            ordered[rows_at(by_view[view], rows), :] = moved
        first = 0
        for length, out_ref in zip(lengths, out_refs):
            out_ref[...] = ordered[first : first + length, :]
            first += length

    flops = 4 * total * total * width // 25
    return pl.pallas_call(
        body,
        grid_spec=pltpu.PrefetchScalarGridSpec(
            num_scalar_prefetch=1,
            grid=(width // span,),
            in_specs=[pl.BlockSpec((3, rows, span), lambda h, *_: (0, 0, h))] * count,
            out_specs=[pl.BlockSpec((length, span), lambda h, *_: (0, h)) for length in lengths]
            + [pl.BlockSpec(memory_space=pltpu.SMEM)] * 2,
            scratch_shapes=[
                pltpu.VMEM((total, span), jnp.bfloat16),
                pltpu.VMEM((total + total // 5, span), jnp.bfloat16),
                pltpu.VMEM((total, span), jnp.bfloat16),
                pltpu.VMEM((total, span), jnp.bfloat16),
                pltpu.VMEM((total, span), jnp.bfloat16),
                pltpu.SMEM((count,), jnp.int32),
            ],
        ),
        out_shape=[jax.ShapeDtypeStruct((length, width), jnp.bfloat16) for length in lengths]
        + [jax.ShapeDtypeStruct((count,), jnp.int32), jax.ShapeDtypeStruct((1,), jnp.int32)],
        compiler_params=params(40),
        cost_estimate=pl.CostEstimate(
            flops=flops, bytes_accessed=total * width, transcendentals=flops // 512
        ),
        name="attend",
    )(place, pltpu.with_memory_space_constraint(received[0], pltpu.HBM), *received[1:])


def gather_features(own, count, between=lambda arrived: arrived):
    half = own.shape[0] // 2
    held = {0: [own]}
    if count == 8:
        over_x = xor_permute(own, 2, count)
        over_y = xor_permute(own, 4, count)
        held[1] = [between(xor_permute(own, 1, count))]
        held[2], held[4] = [over_x], [over_y]
        held[6] = [xor_permute(over_x[:half], 4, count), xor_permute(over_y[half:], 2, count)]
    else:
        for mask in range(2, count, 2):
            held[mask] = [xor_permute(own, mask, count)]
        held[1] = [between(xor_permute(own, 1, count))]
    for mask in range(2, count, 2):
        held[mask + 1] = [xor_permute(piece, 1, count) for piece in held[mask]]
    return [held[mask] for mask in range(count)]


def unfilled(shape):
    def body(out_ref):
        pass

    return pl.pallas_call(
        body,
        out_specs=pl.BlockSpec(memory_space=pl.ANY),
        out_shape=shape,
        name="unfilled",
    )()


def project(place, group, counts, features, more, shards, rows):
    count = len(features)
    width = more.shape[2]
    total = count * rows
    always = total - more.shape[1]
    distances = sorted(shards)
    columns = shards[0].shape[1]
    each = shards[0].shape[0] // width
    bounds = [size for size in variants(total) if size <= always] + [total]
    flat = [piece for pieces in features for piece in pieces]

    def body(place_ref, group_ref, counts_ref, *refs):
        flat_refs = list(refs[: len(flat)])
        more_ref = refs[len(flat)]
        shard_refs = refs[len(flat) + 1 : len(flat) + 1 + len(distances)]
        out_refs = refs[len(flat) + 1 + len(distances) :][:count]
        landed, weight_all, sums, sems, weight_sems = refs[len(flat) + 1 + len(distances) + count :]
        used = sum(counts_ref[mask] for mask in range(count)) * BLOCK

        def send_weight(mask):
            owner = place_ref[0] ^ mask
            apart = group_ref[0] - owner // each
            start = pl.multiple_of((owner % each) * width, width)
            lower = mask % 2 * width
            for distance, shard_ref in zip(distances, shard_refs):

                @pl.when(apart == distance)
                def _():
                    pltpu.make_async_copy(
                        shard_ref.at[pl.ds(start, width), :],
                        weight_all.at[mask // 2, lower : lower + width, :],
                        weight_sems.at[mask // 2],
                    ).start()

        below = 0
        for size in bounds:

            @pl.when((used > below) & (used <= size))
            def _(size=size):
                taken = 0
                for mask in range(count):
                    send_weight(mask)
                    lanes = slice(mask % 2 * width, (mask % 2 + 1) * width)
                    sources = flat_refs[taken : taken + len(features[mask])]
                    taken += len(sources)
                    if size > always:
                        sources.append(more_ref.at[mask])
                    first = 0
                    for source in sources:
                        length = min(source.shape[0], size - first)
                        pltpu.make_async_copy(
                            source.at[:length, :],
                            landed.at[mask // 2, first : first + length, lanes],
                            sems.at[mask // 2],
                        ).start()
                        first += length
                sums[:size, :] = jnp.zeros((size, columns), jnp.float32)

                def pair(index, carry):
                    for buffer, sem in (
                        (weight_all.at[index], weight_sems.at[index]),
                        (landed.at[index, :size, :], sems.at[index]),
                    ):
                        pltpu.make_async_copy(buffer, buffer, sem).wait()
                    sums[:size, :] += jnp.dot(
                        landed[index, :size, :],
                        weight_all[index],
                        preferred_element_type=jnp.float32,
                    )
                    return carry

                lax.fori_loop(0, count // 2, pair, 0)

            below = size
        for mask in range(count):
            position = 0
            for view in range(count):
                position = position + jnp.where(
                    view < (place_ref[0] ^ mask), counts_ref[place_ref[0] ^ view], 0
                )
            moved = sums[rows_at(position * BLOCK, rows), :]
            out_refs[mask][...] = moved.astype(jnp.bfloat16)

    any_spec = pl.BlockSpec(memory_space=pl.ANY)
    inputs = flat + [more]
    inputs += [shards[distance] for distance in distances]
    inputs = [pltpu.with_memory_space_constraint(array, pltpu.HBM) for array in inputs]
    return pl.pallas_call(
        body,
        grid_spec=pltpu.PrefetchScalarGridSpec(
            num_scalar_prefetch=3,
            grid=(1,),
            in_specs=[any_spec] * len(inputs),
            out_specs=[full_spec((rows, columns))] * count,
            scratch_shapes=[
                pltpu.VMEM((count // 2, total, 2 * width), jnp.bfloat16),
                pltpu.VMEM((count // 2, 2 * width, columns), jnp.bfloat16),
                pltpu.VMEM((total, columns), jnp.float32),
                pltpu.SemaphoreType.DMA((count // 2,)),
                pltpu.SemaphoreType.DMA((count // 2,)),
            ],
        ),
        out_shape=[jax.ShapeDtypeStruct((rows, columns), jnp.bfloat16)] * count,
        compiler_params=params(56),
        cost_estimate=pl.CostEstimate(
            flops=total * count * width * columns,
            bytes_accessed=total * count * width,
            transcendentals=0,
        ),
        name="project",
    )(place, group, counts, *inputs)


def assemble(place, block_counts, row_mask, pieces, count):
    rows, columns = pieces[0].shape
    if columns % HEAD_DIM:
        stacked = jnp.stack(pieces)[jnp.arange(count) ^ place[0]]
        result = jnp.moveaxis(stacked, 0, 1).reshape(rows, count * columns)
        offsets = jnp.arange(rows, dtype=jnp.int32)
        good = (row_mask[0] == 1) & (offsets // BLOCK < block_counts[0, 0])
        return jnp.where(good[:, None], result, jnp.bfloat16(0.0))

    def body(place_ref, blocks_ref, mask_ref, *refs):
        out_ref = refs[-1]
        good = valid_column(mask_ref, blocks_ref[0, 0]) > 0.5
        for mask in range(count):
            start = pl.multiple_of((place_ref[0] ^ mask) * columns, HEAD_DIM)
            out_ref[:, pl.ds(start, columns)] = jnp.where(
                good, refs[mask][...], jnp.bfloat16(0.0)
            )

    return pl.pallas_call(
        body,
        grid_spec=pltpu.PrefetchScalarGridSpec(
            num_scalar_prefetch=2,
            grid=(1,),
            in_specs=[full_spec((1, rows))] + [full_spec((rows, columns))] * count,
            out_specs=full_spec((rows, count * columns)),
        ),
        out_shape=jax.ShapeDtypeStruct((rows, count * columns), jnp.bfloat16),
        compiler_params=params(16),
        cost_estimate=pl.CostEstimate(
            flops=0, bytes_accessed=4 * rows * count * columns, transcendentals=0
        ),
        name="assemble",
    )(
        place,
        block_counts,
        row_mask,
        pltpu.with_memory_space_constraint(pieces[0], pltpu.HBM),
        *pieces[1:],
    )


def local(queries, keys, values, out_weight, block_counts, row_mask):
    rows = queries.shape[1]
    count = lax.axis_size("cam")
    total = count * rows
    place_array = jnp.full((1,), lax.axis_index("cam"), jnp.int32)
    group_array = jnp.full((1,), lax.axis_index("fsdp"), jnp.int32)

    shards = {0: cut_weight(place_array, out_weight, count)}
    queries, shards[0] = lax.optimization_barrier((queries, shards[0]))
    payloads = list(
        pack(place_array, block_counts, row_mask, queries, keys, values, count)
    )
    groups = lax.axis_size("fsdp")

    received = [payloads[0]] + [None] * (count - 1)
    early = [mask for mask in order(count) if mask & 1 == 0]
    late = [mask for mask in order(count) if mask & 1]
    pass_weight(shards, 1)
    for mask in early:
        received[mask] = xor_permute(payloads[mask], mask, count)
    received[early[0]], payloads[late[0]] = lax.optimization_barrier(
        (received[early[0]], payloads[late[0]])
    )
    received[late[0]] = xor_permute(payloads[late[0]], late[0], count)
    gate = [received[mask] for mask in early[1:]]
    gate, shards[1], shards[-1] = lax.optimization_barrier((gate, shards[1], shards[-1]))
    for mask, block in zip(early[1:], gate):
        received[mask] = block
    pass_weight(shards, 2)
    received[late[0]], payloads = lax.optimization_barrier((received[late[0]], payloads))
    for mask in late[1:]:
        received[mask] = xor_permute(payloads[mask], mask, count)
    always = total * 3 // 5
    attended, rest, counts, used = attend(
        place_array, received, rows, (always, total - always)
    )
    shape = jax.ShapeDtypeStruct((count,) + rest.shape, rest.dtype)

    def gather_rest(part):
        return jnp.stack([jnp.concatenate(pieces) for pieces in gather_features(part, count)])

    def weight_step(arrived):
        arrived, shards[2], shards[-2] = lax.optimization_barrier((arrived, shards[2], shards[-2]))
        pass_weight(shards, 3)
        return arrived

    features = gather_features(attended, count, weight_step)
    for distance in range(4, groups):
        pass_weight(shards, distance)
    rest, features, shards = lax.optimization_barrier((rest, features, shards))
    more = lax.cond(used[0] > always, gather_rest, lambda part: unfilled(shape), rest)
    pieces = project(place_array, group_array, counts, features, more, shards, rows)
    landed = [pieces[0]] + [None] * (count - 1)
    for mask in order(count):
        landed[mask] = xor_permute(pieces[mask], mask, count)
    return assemble(place_array, block_counts, row_mask, landed, count)[None]


def solution(mesh):
    in_specs = (
        P("fsdp", "cam", None),
        P("fsdp", "cam", None),
        P("fsdp", "cam", None),
        P("fsdp", None),
        P("fsdp", "cam"),
        P("fsdp", "cam"),
    )
    out_specs = P("fsdp", "cam", None)
    return jax.shard_map(local, mesh=mesh, in_specs=in_specs, out_specs=out_specs, check_vma=False)
```

```python
import math

import jax
import jax.numpy as jnp
from jax import lax
from jax.experimental import pallas as pl
from jax.experimental.pallas import tpu as pltpu
from jax.sharding import PartitionSpec as P

HEAD_DIM = 128
BLOCK = 32
SENTINEL = 32.0
LIMIT = 24.0
UNIT = 128


def params(mebibytes):
    return pltpu.CompilerParams(vmem_limit_bytes=mebibytes * 1024 * 1024)


def order(count):
    return sorted(range(1, count), key=lambda mask: (mask == 1, mask & 1, -bin(mask).count("1")))


def variants(total):
    return sorted({-(-total * tenths // (10 * UNIT)) * UNIT for tenths in (4, 5, 6, 8, 10)})


def full_spec(shape):
    return pl.BlockSpec(shape, lambda i, *_: (0,) * len(shape))


def column_of(row):
    n = row.shape[1]
    diagonal = lax.broadcasted_iota(jnp.int32, (n, n), 0) == lax.broadcasted_iota(
        jnp.int32, (n, n), 1
    )
    return jnp.sum(jnp.where(diagonal, row, 0.0), axis=1, keepdims=True)


def valid_column(mask_ref, blocks):
    rows = mask_ref.shape[1]
    inside = lax.broadcasted_iota(jnp.int32, (1, rows), 1) < blocks * BLOCK
    return column_of(jnp.where((mask_ref[...] == 1) & inside, 1.0, 0.0))


def xor_permute(array, mask, count):
    return lax.ppermute(array, "cam", [(place, place ^ mask) for place in range(count)])


def cut_weight(place, out_weight, count):
    depth = out_weight.shape[0]
    columns = out_weight.shape[1] // count
    if columns % HEAD_DIM:
        return lax.dynamic_slice_in_dim(out_weight, place[0] * columns, columns, axis=1)
    parts = 4
    step = depth // parts

    def body(place_ref, w_ref, out_ref, held, load_sems, store_sems):
        start = pl.multiple_of(place_ref[0] * columns, HEAD_DIM)
        loads, stores = [], []
        for part in range(parts):
            inside = pl.ds(part * step, step)
            load = pltpu.make_async_copy(
                w_ref.at[inside, pl.ds(start, columns)], held.at[part], load_sems.at[part]
            )
            load.start()
            loads.append(load)
        for part in range(parts):
            inside = pl.ds(part * step, step)
            loads[part].wait()
            store = pltpu.make_async_copy(held.at[part], out_ref.at[inside, :], store_sems.at[part])
            store.start()
            stores.append(store)
        for store in stores:
            store.wait()

    return pl.pallas_call(
        body,
        grid_spec=pltpu.PrefetchScalarGridSpec(
            num_scalar_prefetch=1,
            grid=(1,),
            in_specs=[pl.BlockSpec(memory_space=pl.ANY)],
            out_specs=pl.BlockSpec(memory_space=pl.ANY),
            scratch_shapes=[
                pltpu.VMEM((parts, step, columns), jnp.bfloat16),
                pltpu.SemaphoreType.DMA((parts,)),
                pltpu.SemaphoreType.DMA((parts,)),
            ],
        ),
        out_shape=jax.ShapeDtypeStruct((depth, columns), jnp.bfloat16),
        compiler_params=params(56),
        cost_estimate=pl.CostEstimate(
            flops=0, bytes_accessed=4 * depth * columns, transcendentals=0
        ),
        name="cut_weight",
    )(place, out_weight)


def pack(place, block_counts, row_mask, queries, keys, values, count):
    _, rows, features = queries.shape
    width = features // count

    def body(place_ref, blocks_ref, mask_ref, q_ref, k_ref, v_ref, *refs):
        out_refs = refs[:count]
        held, key_out, load_sems, sems = refs[count:]
        loads = []
        for slot, ref in enumerate((k_ref, q_ref, v_ref)):
            load = pltpu.make_async_copy(ref.at[0], held.at[slot], load_sems.at[slot])
            load.start()
            loads.append(load)
        starts = [pl.multiple_of((place_ref[0] ^ m) * width, HEAD_DIM) for m in range(count)]
        good = valid_column(mask_ref, blocks_ref[0, 0]) > 0.5
        copies = []

        def send(source, target, sem):
            copy = pltpu.make_async_copy(source, target, sem)
            copy.start()
            copies.append(copy)

        loads[0].wait()
        for mask in range(count):
            part = held[0, :, pl.ds(starts[mask], width)]
            key_out[mask] = jnp.where(good, part, jnp.bfloat16(SENTINEL))
            send(key_out.at[mask], out_refs[mask].at[1], sems.at[mask, 1])
        for slot, target in ((1, 0), (2, 2)):
            loads[slot].wait()
            for mask in range(count):
                source = held.at[slot, :, pl.ds(starts[mask], width)]
                send(source, out_refs[mask].at[target], sems.at[mask, target])
        for copy in copies:
            copy.wait()

    any_spec = pl.BlockSpec(memory_space=pl.ANY)
    return pl.pallas_call(
        body,
        grid_spec=pltpu.PrefetchScalarGridSpec(
            num_scalar_prefetch=2,
            grid=(1,),
            in_specs=[full_spec((1, rows))] + [any_spec] * 3,
            out_specs=[any_spec] * count,
            scratch_shapes=[
                pltpu.VMEM((3, rows, features), jnp.bfloat16),
                pltpu.VMEM((count, rows, width), jnp.bfloat16),
                pltpu.SemaphoreType.DMA((3,)),
                pltpu.SemaphoreType.DMA((count, 3)),
            ],
        ),
        out_shape=[jax.ShapeDtypeStruct((3, rows, width), jnp.bfloat16)] * count,
        compiler_params=params(56),
        cost_estimate=pl.CostEstimate(
            flops=0, bytes_accessed=12 * rows * features, transcendentals=0
        ),
        name="pack",
    )(place, block_counts, row_mask, queries, keys, values)


def pass_weight(shards, distance):
    groups = lax.axis_size("fsdp")
    for sign in (1, -1):
        pairs = []
        for source in range(groups):
            origin, target = source - sign * (distance - 1), source + sign
            if 0 <= origin < groups and 0 <= target < groups:
                pairs.append((source, target))
        shards[sign * distance] = lax.ppermute(shards[sign * (distance - 1)], "fsdp", pairs)


def packed_offsets(place_ref, counts_ref, table, count):
    by_mask, running = [], 0
    for mask in range(count):
        by_mask.append(running)
        table[mask] = running
        running = running + counts_ref[mask] * BLOCK
    by_view, position = [], 0
    for view in range(count):
        by_view.append(position)
        position = position + counts_ref[place_ref[0] ^ view] * BLOCK
    return by_mask, by_view, running


def rows_at(start, size):
    return pl.ds(start if isinstance(start, int) else pl.multiple_of(start, BLOCK), size)


def tile_of(size):
    return max(rows for rows in range(UNIT, 6 * UNIT + 1, UNIT) if size % rows == 0)


def attend(place, received, rows, lengths):
    count = len(received)
    width = received[0].shape[2]
    total = count * rows
    span = 2 * HEAD_DIM
    factor = math.log2(math.e) / math.sqrt(HEAD_DIM)

    def body(place_ref, *refs):
        parts = refs[:count]
        out_refs = refs[count : count + len(lengths)]
        counts_ref, used_ref = refs[count + len(lengths) : count + len(lengths) + 2]
        query_all, key_all, value_all, result, ordered, table = refs[count + len(lengths) + 2 :]

        @pl.when(pl.program_id(0) == 0)
        def _():
            value_all[...] = jnp.zeros_like(value_all)
            for mask in range(count):
                blocks = jnp.zeros((1, HEAD_DIM), jnp.float32)
                for first in range(0, rows, BLOCK):
                    row = parts[mask][1, first : first + 16, :HEAD_DIM].astype(jnp.float32)[:1]
                    blocks = blocks + jnp.where(row < LIMIT, 1.0, 0.0)
                counts_ref[mask] = jnp.max(blocks).astype(jnp.int32)

        by_mask, by_view, used = packed_offsets(place_ref, counts_ref, table, count)
        used_ref[0] = used
        for mask in range(count):
            where = rows_at(by_mask[mask], rows)
            query_all[where, :] = parts[mask][0]
            key_all[where, :] = parts[mask][1]
            value_all[where, :] = parts[mask][2]
        key_all[rows_at(used, total // 5), :] = jnp.full((total // 5, span), SENTINEL, jnp.bfloat16)
        below = 0
        for size in variants(total):

            @pl.when((used > below) & (used <= size))
            def _(size=size):
                step = tile_of(size)
                key_mask = key_all[:size, :HEAD_DIM].astype(jnp.float32) > LIMIT
                bias = jnp.where(key_mask, jnp.float32(-1e30), 0.0)
                bias = jnp.concatenate([bias] * (step // HEAD_DIM), axis=1)
                values_t = [
                    value_all[:size, first : first + HEAD_DIM].T
                    for first in range(0, span, HEAD_DIM)
                ]

                def tile(index, carry):
                    if isinstance(index, int):
                        where = pl.ds(index * step, step)
                    else:
                        where = pl.ds(pl.multiple_of(index * step, UNIT), step)
                    for head in range(span // HEAD_DIM):
                        lanes = slice(head * HEAD_DIM, (head + 1) * HEAD_DIM)
                        scores = lax.dot_general(
                            key_all[:size, lanes],
                            query_all[where, lanes],
                            (((1,), (1,)), ((), ())),
                            preferred_element_type=jnp.float32,
                        )
                        scores = scores + bias
                        top = jnp.max(scores, axis=0, keepdims=True)
                        raised = jnp.exp2((scores - top) * factor)
                        norm = jnp.sum(raised, axis=0, keepdims=True)
                        summed = jnp.dot(
                            values_t[head],
                            raised.astype(jnp.bfloat16),
                            preferred_element_type=jnp.float32,
                        )
                        result[where, lanes] = (summed / norm).T.astype(jnp.bfloat16)
                    return carry

                if size == step:
                    tile(0, 0)
                else:
                    lax.fori_loop(0, size // step, tile, 0)

            below = size
        for view in range(count):
            moved = result[rows_at(table[place_ref[0] ^ view], rows), :]
            ordered[rows_at(by_view[view], rows), :] = moved
        first = 0
        for length, out_ref in zip(lengths, out_refs):
            out_ref[...] = ordered[first : first + length, :]
            first += length

    flops = 4 * total * total * width // 25
    return pl.pallas_call(
        body,
        grid_spec=pltpu.PrefetchScalarGridSpec(
            num_scalar_prefetch=1,
            grid=(width // span,),
            in_specs=[pl.BlockSpec((3, rows, span), lambda h, *_: (0, 0, h))] * count,
            out_specs=[pl.BlockSpec((length, span), lambda h, *_: (0, h)) for length in lengths]
            + [pl.BlockSpec(memory_space=pltpu.SMEM)] * 2,
            scratch_shapes=[
                pltpu.VMEM((total, span), jnp.bfloat16),
                pltpu.VMEM((total + total // 5, span), jnp.bfloat16),
                pltpu.VMEM((total, span), jnp.bfloat16),
                pltpu.VMEM((total, span), jnp.bfloat16),
                pltpu.VMEM((total, span), jnp.bfloat16),
                pltpu.SMEM((count,), jnp.int32),
            ],
        ),
        out_shape=[jax.ShapeDtypeStruct((length, width), jnp.bfloat16) for length in lengths]
        + [jax.ShapeDtypeStruct((count,), jnp.int32), jax.ShapeDtypeStruct((1,), jnp.int32)],
        compiler_params=params(40),
        cost_estimate=pl.CostEstimate(
            flops=flops, bytes_accessed=total * width, transcendentals=flops // 512
        ),
        name="attend",
    )(place, pltpu.with_memory_space_constraint(received[0], pltpu.HBM), *received[1:])


def gather_features(own, count, between=lambda arrived: arrived):
    half = own.shape[0] // 2
    held = {0: [own]}
    if count == 8:
        over_x = xor_permute(own, 2, count)
        over_y = xor_permute(own, 4, count)
        held[1] = [between(xor_permute(own, 1, count))]
        held[1][0], over_x, over_y = lax.optimization_barrier((held[1][0], over_x, over_y))
        held[2], held[4] = [over_x], [over_y]
        held[6] = [xor_permute(over_x[:half], 4, count), xor_permute(over_y[half:], 2, count)]
    else:
        for mask in range(2, count, 2):
            held[mask] = [xor_permute(own, mask, count)]
        held[1] = [between(xor_permute(own, 1, count))]
    for mask in range(2, count, 2):
        if mask == 4:
            held[6], held[4] = lax.optimization_barrier((held[6], held[4]))
        held[mask + 1] = [xor_permute(piece, 1, count) for piece in held[mask]]
    return [held[mask] for mask in range(count)]


def unfilled(shape):
    def body(out_ref):
        pass

    return pl.pallas_call(
        body,
        out_specs=pl.BlockSpec(memory_space=pl.ANY),
        out_shape=shape,
        name="unfilled",
    )()


NEAR = 2


def near_shards(shards):
    return {distance: shards[distance] for distance in shards if abs(distance) <= NEAR}


def shard_apart(place_ref, group_ref, pair, each):
    return group_ref[0] - (place_ref[0] ^ (2 * pair)) // each


def send_weights(place_ref, group_ref, pair, each, width, distances, shard_refs, target, sem):
    apart = shard_apart(place_ref, group_ref, pair, each)
    for distance, shard_ref in zip(distances, shard_refs):

        @pl.when(apart == distance)
        def _():
            for side in range(2):
                owner = place_ref[0] ^ (2 * pair + side)
                start = pl.multiple_of((owner % each) * width, width)
                pltpu.make_async_copy(
                    shard_ref.at[pl.ds(start, width), :],
                    target.at[side * width : (side + 1) * width, :],
                    sem,
                ).start()


def send_features(piece_refs, size, width, target, sem):
    for side, refs in enumerate(piece_refs):
        first = 0
        for ref in refs:
            length = min(ref.shape[0], size - first)
            pltpu.make_async_copy(
                ref.at[:length, :],
                target.at[first : first + length, side * width : (side + 1) * width],
                sem,
            ).start()
            first += length


def wait_all(*buffers_and_sems):
    for buffer, sem in buffers_and_sems:
        pltpu.make_async_copy(buffer, buffer, sem).wait()


def group_refs(refs, features):
    grouped, taken = [], 0
    for pieces in features:
        grouped.append(refs[taken : taken + len(pieces)])
        taken += len(pieces)
    return grouped


def pinned(arrays):
    return [pltpu.with_memory_space_constraint(array, pltpu.HBM) for array in arrays]


def project_near(place, group, counts, features, shards, rows, always):
    count = len(features)
    pairs = count // 2 - 1
    flat = [piece for pieces in features[: 2 * pairs] for piece in pieces]
    width = flat[0].shape[1]
    shards = near_shards(shards)
    distances = sorted(shards)
    columns = shards[0].shape[1]
    each = shards[0].shape[0] // width
    bounds = [size for size in variants(count * rows) if size <= always]

    def body(place_ref, group_ref, counts_ref, *refs):
        grouped = group_refs(refs[: len(flat)], features[: 2 * pairs])
        shard_refs = refs[len(flat) : len(flat) + len(distances)]
        out_ref, landed, weight_all, sums, sems, weight_sems, out_sem = refs[
            len(flat) + len(distances) :
        ]
        used = sum(counts_ref[mask] for mask in range(count)) * BLOCK

        def taken(pair):
            apart = shard_apart(place_ref, group_ref, pair, each)
            return (apart <= NEAR) & (apart >= -NEAR)

        below = 0
        for size in bounds:

            @pl.when((used > below) & ((used <= size) | (size == always)))
            def _(size=size):
                for pair in range(pairs):

                    @pl.when(taken(pair))
                    def _(pair=pair):
                        send_weights(
                            place_ref, group_ref, pair, each, width, distances, shard_refs,
                            weight_all.at[pair], weight_sems.at[pair],
                        )
                        send_features(
                            grouped[2 * pair : 2 * pair + 2], size, width,
                            landed.at[pair], sems.at[pair],
                        )

                sums[:size, :] = jnp.zeros((size, columns), jnp.float32)

                def add(pair, carry):
                    @pl.when(taken(pair))
                    def _():
                        wait_all(
                            (weight_all.at[pair], weight_sems.at[pair]),
                            (landed.at[pair, :size, :], sems.at[pair]),
                        )
                        sums[:size, :] += jnp.dot(
                            landed[pair, :size, :],
                            weight_all[pair],
                            preferred_element_type=jnp.float32,
                        )

                    return carry

                lax.fori_loop(0, pairs, add, 0)
                copy = pltpu.make_async_copy(
                    sums.at[:size, :], out_ref.at[:size, :], out_sem.at[0]
                )
                copy.start()
                copy.wait()

            below = size

    any_spec = pl.BlockSpec(memory_space=pl.ANY)
    inputs = pinned(flat + [shards[distance] for distance in distances])
    return pl.pallas_call(
        body,
        grid_spec=pltpu.PrefetchScalarGridSpec(
            num_scalar_prefetch=3,
            grid=(1,),
            in_specs=[any_spec] * len(inputs),
            out_specs=any_spec,
            scratch_shapes=[
                pltpu.VMEM((pairs, always, 2 * width), jnp.bfloat16),
                pltpu.VMEM((pairs, 2 * width, columns), jnp.bfloat16),
                pltpu.VMEM((always, columns), jnp.float32),
                pltpu.SemaphoreType.DMA((pairs,)),
                pltpu.SemaphoreType.DMA((pairs,)),
                pltpu.SemaphoreType.DMA((1,)),
            ],
        ),
        out_shape=jax.ShapeDtypeStruct((always, columns), jnp.float32),
        compiler_params=params(56),
        cost_estimate=pl.CostEstimate(
            flops=0, bytes_accessed=always * columns, transcendentals=0
        ),
        name="project_near",
    )(place, group, counts, *inputs)


def project(place, group, counts, features, more, shards, partial, rows):
    count = len(features)
    pairs = count // 2
    width = more.shape[2]
    total = count * rows
    always = total - more.shape[1]
    distances = sorted(shards)
    columns = shards[0].shape[1]
    each = shards[0].shape[0] // width
    bounds = [size for size in variants(total) if size <= always] + [total]
    flat = [piece for pieces in features for piece in pieces]

    def body(place_ref, group_ref, counts_ref, *refs):
        grouped = group_refs(refs[: len(flat)], features)
        more_ref, partial_ref = refs[len(flat) : len(flat) + 2]
        refs = refs[len(flat) + 2 :]
        shard_refs = refs[: len(distances)]
        out_refs = refs[len(distances) : len(distances) + count]
        landed, weight_all, sums, sems, weight_sems, partial_sem = refs[len(distances) + count :]
        used = sum(counts_ref[mask] for mask in range(count)) * BLOCK

        def left(pair):
            apart = shard_apart(place_ref, group_ref, pair, each)
            return (pair == pairs - 1) | (apart > NEAR) | (apart < -NEAR)

        below = 0
        for size in bounds:
            low = min(size, always)

            @pl.when((used > below) & (used <= size))
            def _(size=size, low=low):
                load = pltpu.make_async_copy(
                    partial_ref.at[:low, :], sums.at[:low, :], partial_sem.at[0]
                )
                load.start()
                for pair in range(pairs):
                    sources = [list(grouped[2 * pair + side]) for side in range(2)]
                    if size > always:
                        for side in range(2):
                            sources[side].append(more_ref.at[2 * pair + side])

                    @pl.when(left(pair) | (size > always))
                    def _(pair=pair, sources=sources):
                        send_weights(
                            place_ref, group_ref, pair, each, width, distances, shard_refs,
                            weight_all.at[pair], weight_sems.at[pair],
                        )
                        send_features(sources, size, width, landed.at[pair], sems.at[pair])

                if size > always:
                    sums[always:, :] = jnp.zeros((total - always, columns), jnp.float32)
                load.wait()

                def add_rows(pair, first, end):
                    sums[first:end, :] += jnp.dot(
                        landed[pair, first:end, :],
                        weight_all[pair],
                        preferred_element_type=jnp.float32,
                    )

                def add(pair, carry):
                    @pl.when(left(pair) | (size > always))
                    def _():
                        wait_all(
                            (weight_all.at[pair], weight_sems.at[pair]),
                            (landed.at[pair, :size, :], sems.at[pair]),
                        )

                    @pl.when(left(pair))
                    def _():
                        add_rows(pair, 0, low)

                    if size > always:
                        add_rows(pair, always, size)
                    return carry

                lax.fori_loop(0, pairs, add, 0)

            below = size
        for mask in range(count):
            position = 0
            for view in range(count):
                position = position + jnp.where(
                    view < (place_ref[0] ^ mask), counts_ref[place_ref[0] ^ view], 0
                )
            moved = sums[rows_at(position * BLOCK, rows), :]
            out_refs[mask][...] = moved.astype(jnp.bfloat16)

    any_spec = pl.BlockSpec(memory_space=pl.ANY)
    inputs = pinned(flat + [more, partial] + [shards[distance] for distance in distances])
    return pl.pallas_call(
        body,
        grid_spec=pltpu.PrefetchScalarGridSpec(
            num_scalar_prefetch=3,
            grid=(1,),
            in_specs=[any_spec] * len(inputs),
            out_specs=[full_spec((rows, columns))] * count,
            scratch_shapes=[
                pltpu.VMEM((pairs, total, 2 * width), jnp.bfloat16),
                pltpu.VMEM((pairs, 2 * width, columns), jnp.bfloat16),
                pltpu.VMEM((total, columns), jnp.float32),
                pltpu.SemaphoreType.DMA((pairs,)),
                pltpu.SemaphoreType.DMA((pairs,)),
                pltpu.SemaphoreType.DMA((1,)),
            ],
        ),
        out_shape=[jax.ShapeDtypeStruct((rows, columns), jnp.bfloat16)] * count,
        compiler_params=params(56),
        cost_estimate=pl.CostEstimate(
            flops=total * count * width * columns // 4,
            bytes_accessed=total * count * width,
            transcendentals=0,
        ),
        name="project",
    )(place, group, counts, *inputs)


def assemble(place, block_counts, row_mask, pieces, count):
    rows, columns = pieces[0].shape
    if columns % HEAD_DIM:
        stacked = jnp.stack(pieces)[jnp.arange(count) ^ place[0]]
        result = jnp.moveaxis(stacked, 0, 1).reshape(rows, count * columns)
        offsets = jnp.arange(rows, dtype=jnp.int32)
        good = (row_mask[0] == 1) & (offsets // BLOCK < block_counts[0, 0])
        return jnp.where(good[:, None], result, jnp.bfloat16(0.0))

    def body(place_ref, blocks_ref, mask_ref, *refs):
        out_ref = refs[-1]
        good = valid_column(mask_ref, blocks_ref[0, 0]) > 0.5
        for mask in range(count):
            start = pl.multiple_of((place_ref[0] ^ mask) * columns, HEAD_DIM)
            out_ref[:, pl.ds(start, columns)] = jnp.where(
                good, refs[mask][...], jnp.bfloat16(0.0)
            )

    return pl.pallas_call(
        body,
        grid_spec=pltpu.PrefetchScalarGridSpec(
            num_scalar_prefetch=2,
            grid=(1,),
            in_specs=[full_spec((1, rows))] + [full_spec((rows, columns))] * count,
            out_specs=full_spec((rows, count * columns)),
        ),
        out_shape=jax.ShapeDtypeStruct((rows, count * columns), jnp.bfloat16),
        compiler_params=params(16),
        cost_estimate=pl.CostEstimate(
            flops=0, bytes_accessed=4 * rows * count * columns, transcendentals=0
        ),
        name="assemble",
    )(
        place,
        block_counts,
        row_mask,
        pltpu.with_memory_space_constraint(pieces[0], pltpu.HBM),
        *pieces[1:],
    )


def local(queries, keys, values, out_weight, block_counts, row_mask):
    rows = queries.shape[1]
    count = lax.axis_size("cam")
    total = count * rows
    place_array = jnp.full((1,), lax.axis_index("cam"), jnp.int32)
    group_array = jnp.full((1,), lax.axis_index("fsdp"), jnp.int32)

    shards = {0: cut_weight(place_array, out_weight, count)}
    queries, shards[0] = lax.optimization_barrier((queries, shards[0]))
    payloads = list(
        pack(place_array, block_counts, row_mask, queries, keys, values, count)
    )
    groups = lax.axis_size("fsdp")

    received = [payloads[0]] + [None] * (count - 1)
    early = [mask for mask in order(count) if mask & 1 == 0]
    late = [mask for mask in order(count) if mask & 1]
    pass_weight(shards, 1)
    for mask in early:
        received[mask] = xor_permute(payloads[mask], mask, count)
    received[early[0]], payloads[late[0]] = lax.optimization_barrier(
        (received[early[0]], payloads[late[0]])
    )
    received[late[0]] = xor_permute(payloads[late[0]], late[0], count)
    gate = [received[mask] for mask in early[1:]]
    gate, shards[1], shards[-1] = lax.optimization_barrier((gate, shards[1], shards[-1]))
    for mask, block in zip(early[1:], gate):
        received[mask] = block
    pass_weight(shards, 2)
    received[late[0]], payloads = lax.optimization_barrier((received[late[0]], payloads))
    for mask in late[1:]:
        received[mask] = xor_permute(payloads[mask], mask, count)
    always = total * 3 // 5
    attended, rest, counts, used = attend(
        place_array, received, rows, (always, total - always)
    )
    shape = jax.ShapeDtypeStruct((count,) + rest.shape, rest.dtype)

    def gather_rest(part):
        return jnp.stack([jnp.concatenate(pieces) for pieces in gather_features(part, count)])

    def weight_step(arrived):
        arrived, shards[2], shards[-2] = lax.optimization_barrier((arrived, shards[2], shards[-2]))
        pass_weight(shards, 3)
        return arrived

    features = gather_features(attended, count, weight_step)
    for distance in range(4, groups):
        pass_weight(shards, distance)
    partial = project_near(
        place_array, group_array, counts, features, shards, rows, always
    )
    rest, features, shards, partial = lax.optimization_barrier((rest, features, shards, partial))
    more = lax.cond(used[0] > always, gather_rest, lambda part: unfilled(shape), rest)
    pieces = project(
        place_array, group_array, counts, features, more, shards, partial, rows
    )
    landed = [pieces[0]] + [None] * (count - 1)
    for mask in order(count):
        landed[mask] = xor_permute(pieces[mask], mask, count)
    return assemble(place_array, block_counts, row_mask, landed, count)[None]


def solution(mesh):
    in_specs = (
        P("fsdp", "cam", None),
        P("fsdp", "cam", None),
        P("fsdp", "cam", None),
        P("fsdp", None),
        P("fsdp", "cam"),
        P("fsdp", "cam"),
    )
    out_specs = P("fsdp", "cam", None)
    return jax.shard_map(local, mesh=mesh, in_specs=in_specs, out_specs=out_specs, check_vma=False)
```

```python
import math

import jax
import jax.numpy as jnp
from jax import lax
from jax.experimental import pallas as pl
from jax.experimental.pallas import tpu as pltpu
from jax.sharding import PartitionSpec as P

HEAD_DIM = 128
BLOCK = 32
SENTINEL = 32.0
LIMIT = 24.0
UNIT = 128


def params(mebibytes):
    return pltpu.CompilerParams(vmem_limit_bytes=mebibytes * 1024 * 1024)


def order(count):
    return sorted(range(1, count), key=lambda mask: (mask == 1, mask & 1, -bin(mask).count("1")))


def variants(total):
    return sorted({-(-total * tenths // (10 * UNIT)) * UNIT for tenths in (4, 5, 6, 8, 10)})


def full_spec(shape):
    return pl.BlockSpec(shape, lambda i, *_: (0,) * len(shape))


def column_of(row):
    n = row.shape[1]
    diagonal = lax.broadcasted_iota(jnp.int32, (n, n), 0) == lax.broadcasted_iota(
        jnp.int32, (n, n), 1
    )
    return jnp.sum(jnp.where(diagonal, row, 0.0), axis=1, keepdims=True)


def valid_column(mask_ref, blocks):
    rows = mask_ref.shape[1]
    inside = lax.broadcasted_iota(jnp.int32, (1, rows), 1) < blocks * BLOCK
    return column_of(jnp.where((mask_ref[...] == 1) & inside, 1.0, 0.0))


def xor_permute(array, mask, count):
    return lax.ppermute(array, "cam", [(place, place ^ mask) for place in range(count)])


def cut_weight(place, out_weight, count):
    depth = out_weight.shape[0]
    columns = out_weight.shape[1] // count
    if columns % HEAD_DIM:
        return lax.dynamic_slice_in_dim(out_weight, place[0] * columns, columns, axis=1)
    parts = 4
    step = depth // parts

    def body(place_ref, w_ref, out_ref, held, load_sems, store_sems):
        start = pl.multiple_of(place_ref[0] * columns, HEAD_DIM)
        loads, stores = [], []
        for part in range(parts):
            inside = pl.ds(part * step, step)
            load = pltpu.make_async_copy(
                w_ref.at[inside, pl.ds(start, columns)], held.at[part], load_sems.at[part]
            )
            load.start()
            loads.append(load)
        for part in range(parts):
            inside = pl.ds(part * step, step)
            loads[part].wait()
            store = pltpu.make_async_copy(held.at[part], out_ref.at[inside, :], store_sems.at[part])
            store.start()
            stores.append(store)
        for store in stores:
            store.wait()

    return pl.pallas_call(
        body,
        grid_spec=pltpu.PrefetchScalarGridSpec(
            num_scalar_prefetch=1,
            grid=(1,),
            in_specs=[pl.BlockSpec(memory_space=pl.ANY)],
            out_specs=pl.BlockSpec(memory_space=pl.ANY),
            scratch_shapes=[
                pltpu.VMEM((parts, step, columns), jnp.bfloat16),
                pltpu.SemaphoreType.DMA((parts,)),
                pltpu.SemaphoreType.DMA((parts,)),
            ],
        ),
        out_shape=jax.ShapeDtypeStruct((depth, columns), jnp.bfloat16),
        compiler_params=params(56),
        cost_estimate=pl.CostEstimate(
            flops=0, bytes_accessed=4 * depth * columns, transcendentals=0
        ),
        name="cut_weight",
    )(place, out_weight)


def pack(place, block_counts, row_mask, queries, keys, values, masks, count):
    _, rows, features = queries.shape
    width = features // count
    number = len(masks)

    def body(place_ref, blocks_ref, mask_ref, q_ref, k_ref, v_ref, *refs):
        out_refs = refs[:number]
        held, load_sems, store_sems = refs[number:]

        def copies(index, slot):
            start = pl.multiple_of((place_ref[0] ^ masks[index]) * width, HEAD_DIM)
            source = (q_ref, k_ref, v_ref)[slot].at[0, :, pl.ds(start, width)]
            buffer = held.at[index, slot]
            return (
                pltpu.make_async_copy(source, buffer, load_sems.at[index, slot]),
                pltpu.make_async_copy(
                    buffer, out_refs[index].at[slot], store_sems.at[index, slot]
                ),
            )

        steps = [copies(index, slot) for slot in (1, 0, 2) for index in range(number)]
        for load, _ in steps:
            load.start()
        good = valid_column(mask_ref, blocks_ref[0, 0]) > 0.5
        for step, (load, store) in enumerate(steps):
            load.wait()
            if step < number:
                held[step, 1] = jnp.where(good, held[step, 1], jnp.bfloat16(SENTINEL))
            store.start()
        for _, store in steps:
            store.wait()

    any_spec = pl.BlockSpec(memory_space=pl.ANY)
    return list(
        pl.pallas_call(
            body,
            grid_spec=pltpu.PrefetchScalarGridSpec(
                num_scalar_prefetch=2,
                grid=(1,),
                in_specs=[full_spec((1, rows))] + [any_spec] * 3,
                out_specs=[any_spec] * number,
                scratch_shapes=[
                    pltpu.VMEM((number, 3, rows, width), jnp.bfloat16),
                    pltpu.SemaphoreType.DMA((number, 3)),
                    pltpu.SemaphoreType.DMA((number, 3)),
                ],
            ),
            out_shape=[jax.ShapeDtypeStruct((3, rows, width), jnp.bfloat16)] * number,
            compiler_params=params(56),
            cost_estimate=pl.CostEstimate(
                flops=0, bytes_accessed=12 * rows * width * number, transcendentals=0
            ),
            name="pack",
        )(place, block_counts, row_mask, queries, keys, values)
    )


def pass_weight(shards, distance):
    groups = lax.axis_size("fsdp")
    for sign in (1, -1):
        pairs = []
        for source in range(groups):
            origin, target = source - sign * (distance - 1), source + sign
            if 0 <= origin < groups and 0 <= target < groups:
                pairs.append((source, target))
        shards[sign * distance] = lax.ppermute(shards[sign * (distance - 1)], "fsdp", pairs)


def packed_offsets(place_ref, counts_ref, table, count):
    by_mask, running = [], 0
    for mask in range(count):
        by_mask.append(running)
        table[mask] = running
        running = running + counts_ref[mask] * BLOCK
    by_view, position = [], 0
    for view in range(count):
        by_view.append(position)
        position = position + counts_ref[place_ref[0] ^ view] * BLOCK
    return by_mask, by_view, running


def rows_at(start, size):
    return pl.ds(start if isinstance(start, int) else pl.multiple_of(start, BLOCK), size)


def tile_of(size):
    return max(rows for rows in range(UNIT, 6 * UNIT + 1, UNIT) if size % rows == 0)


def attend(place, received, rows, lengths):
    count = len(received)
    width = received[0].shape[2]
    total = count * rows
    span = 2 * HEAD_DIM
    factor = math.log2(math.e) / math.sqrt(HEAD_DIM)

    def body(place_ref, *refs):
        parts = refs[:count]
        out_refs = refs[count : count + len(lengths)]
        counts_ref, used_ref = refs[count + len(lengths) : count + len(lengths) + 2]
        query_all, key_all, value_all, result, ordered, table = refs[count + len(lengths) + 2 :]

        @pl.when(pl.program_id(0) == 0)
        def _():
            value_all[...] = jnp.zeros_like(value_all)
            for mask in range(count):
                blocks = jnp.zeros((1, HEAD_DIM), jnp.float32)
                for first in range(0, rows, BLOCK):
                    row = parts[mask][1, first : first + 16, :HEAD_DIM].astype(jnp.float32)[:1]
                    blocks = blocks + jnp.where(row < LIMIT, 1.0, 0.0)
                counts_ref[mask] = jnp.max(blocks).astype(jnp.int32)

        by_mask, by_view, used = packed_offsets(place_ref, counts_ref, table, count)
        used_ref[0] = used
        for mask in range(count):
            where = rows_at(by_mask[mask], rows)
            query_all[where, :] = parts[mask][0]
            key_all[where, :] = parts[mask][1]
            value_all[where, :] = parts[mask][2]
        key_all[rows_at(used, total // 5), :] = jnp.full((total // 5, span), SENTINEL, jnp.bfloat16)
        below = 0
        for size in variants(total):

            @pl.when((used > below) & (used <= size))
            def _(size=size):
                step = tile_of(size)
                key_mask = key_all[:size, :HEAD_DIM].astype(jnp.float32) > LIMIT
                bias = jnp.where(key_mask, jnp.float32(-1e30), 0.0)
                bias = jnp.concatenate([bias] * (step // HEAD_DIM), axis=1)
                values_t = [
                    value_all[:size, first : first + HEAD_DIM].T
                    for first in range(0, span, HEAD_DIM)
                ]

                def tile(index, carry):
                    if isinstance(index, int):
                        where = pl.ds(index * step, step)
                    else:
                        where = pl.ds(pl.multiple_of(index * step, UNIT), step)
                    for head in range(span // HEAD_DIM):
                        lanes = slice(head * HEAD_DIM, (head + 1) * HEAD_DIM)
                        scores = lax.dot_general(
                            key_all[:size, lanes],
                            query_all[where, lanes],
                            (((1,), (1,)), ((), ())),
                            preferred_element_type=jnp.float32,
                        )
                        scores = scores + bias
                        top = jnp.max(scores, axis=0, keepdims=True)
                        raised = jnp.exp2((scores - top) * factor)
                        norm = jnp.sum(raised, axis=0, keepdims=True)
                        summed = jnp.dot(
                            values_t[head],
                            raised.astype(jnp.bfloat16),
                            preferred_element_type=jnp.float32,
                        )
                        result[where, lanes] = (summed / norm).T.astype(jnp.bfloat16)
                    return carry

                if size == step:
                    tile(0, 0)
                else:
                    lax.fori_loop(0, size // step, tile, 0)

            below = size
        for view in range(count):
            moved = result[rows_at(table[place_ref[0] ^ view], rows), :]
            ordered[rows_at(by_view[view], rows), :] = moved
        first = 0
        for length, out_ref in zip(lengths, out_refs):
            out_ref[...] = ordered[first : first + length, :]
            first += length

    flops = 4 * total * total * width // 25
    return pl.pallas_call(
        body,
        grid_spec=pltpu.PrefetchScalarGridSpec(
            num_scalar_prefetch=1,
            grid=(width // span,),
            in_specs=[pl.BlockSpec((3, rows, span), lambda h, *_: (0, 0, h))] * count,
            out_specs=[pl.BlockSpec((length, span), lambda h, *_: (0, h)) for length in lengths]
            + [pl.BlockSpec(memory_space=pltpu.SMEM)] * 2,
            scratch_shapes=[
                pltpu.VMEM((total, span), jnp.bfloat16),
                pltpu.VMEM((total + total // 5, span), jnp.bfloat16),
                pltpu.VMEM((total, span), jnp.bfloat16),
                pltpu.VMEM((total, span), jnp.bfloat16),
                pltpu.VMEM((total, span), jnp.bfloat16),
                pltpu.SMEM((count,), jnp.int32),
            ],
        ),
        out_shape=[jax.ShapeDtypeStruct((length, width), jnp.bfloat16) for length in lengths]
        + [jax.ShapeDtypeStruct((count,), jnp.int32), jax.ShapeDtypeStruct((1,), jnp.int32)],
        compiler_params=params(40),
        cost_estimate=pl.CostEstimate(
            flops=flops, bytes_accessed=total * width, transcendentals=flops // 512
        ),
        name="attend",
    )(place, pltpu.with_memory_space_constraint(received[0], pltpu.HBM), *received[1:])


def gather_features(own, count, between=lambda arrived: arrived):
    half = own.shape[0] // 2
    held = {0: [own]}
    if count == 8:
        over_x = xor_permute(own, 2, count)
        over_y = xor_permute(own, 4, count)
        held[1] = [between(xor_permute(own, 1, count))]
        held[1][0], over_x, over_y = lax.optimization_barrier((held[1][0], over_x, over_y))
        held[2], held[4] = [over_x], [over_y]
        held[6] = [xor_permute(over_x[:half], 4, count), xor_permute(over_y[half:], 2, count)]
    else:
        for mask in range(2, count, 2):
            held[mask] = [xor_permute(own, mask, count)]
        held[1] = [between(xor_permute(own, 1, count))]
    for mask in range(2, count, 2):
        if mask == 4:
            held[6], held[4] = lax.optimization_barrier((held[6], held[4]))
        held[mask + 1] = [xor_permute(piece, 1, count) for piece in held[mask]]
    return [held[mask] for mask in range(count)]


def unfilled(shape):
    def body(out_ref):
        pass

    return pl.pallas_call(
        body,
        out_specs=pl.BlockSpec(memory_space=pl.ANY),
        out_shape=shape,
        name="unfilled",
    )()


NEAR = 2


def near_shards(shards):
    return {distance: shards[distance] for distance in shards if abs(distance) <= NEAR}


def shard_apart(place_ref, group_ref, pair, each):
    return group_ref[0] - (place_ref[0] ^ (2 * pair)) // each


def send_weights(place_ref, group_ref, pair, each, width, distances, shard_refs, target, sem):
    apart = shard_apart(place_ref, group_ref, pair, each)
    for distance, shard_ref in zip(distances, shard_refs):

        @pl.when(apart == distance)
        def _():
            for side in range(2):
                owner = place_ref[0] ^ (2 * pair + side)
                start = pl.multiple_of((owner % each) * width, width)
                pltpu.make_async_copy(
                    shard_ref.at[pl.ds(start, width), :],
                    target.at[side * width : (side + 1) * width, :],
                    sem,
                ).start()


def send_features(piece_refs, size, width, target, sem):
    for side, refs in enumerate(piece_refs):
        first = 0
        for ref in refs:
            length = min(ref.shape[0], size - first)
            pltpu.make_async_copy(
                ref.at[:length, :],
                target.at[first : first + length, side * width : (side + 1) * width],
                sem,
            ).start()
            first += length


def wait_all(*buffers_and_sems):
    for buffer, sem in buffers_and_sems:
        pltpu.make_async_copy(buffer, buffer, sem).wait()


def group_refs(refs, features):
    grouped, taken = [], 0
    for pieces in features:
        grouped.append(refs[taken : taken + len(pieces)])
        taken += len(pieces)
    return grouped


def pinned(arrays):
    return [pltpu.with_memory_space_constraint(array, pltpu.HBM) for array in arrays]


def project_near(place, group, counts, features, shards, rows, always):
    count = len(features)
    pairs = count // 2 - 1
    flat = [piece for pieces in features[: 2 * pairs] for piece in pieces]
    width = flat[0].shape[1]
    shards = near_shards(shards)
    distances = sorted(shards)
    columns = shards[0].shape[1]
    each = shards[0].shape[0] // width
    bounds = [size for size in variants(count * rows) if size <= always]

    def body(place_ref, group_ref, counts_ref, *refs):
        grouped = group_refs(refs[: len(flat)], features[: 2 * pairs])
        shard_refs = refs[len(flat) : len(flat) + len(distances)]
        out_ref, landed, weight_all, sums, sems, weight_sems, out_sem = refs[
            len(flat) + len(distances) :
        ]
        used = sum(counts_ref[mask] for mask in range(count)) * BLOCK

        def taken(pair):
            apart = shard_apart(place_ref, group_ref, pair, each)
            return (apart <= NEAR) & (apart >= -NEAR)

        below = 0
        for size in bounds:

            @pl.when((used > below) & ((used <= size) | (size == always)))
            def _(size=size):
                for pair in range(pairs):

                    @pl.when(taken(pair))
                    def _(pair=pair):
                        send_weights(
                            place_ref, group_ref, pair, each, width, distances, shard_refs,
                            weight_all.at[pair], weight_sems.at[pair],
                        )
                        send_features(
                            grouped[2 * pair : 2 * pair + 2], size, width,
                            landed.at[pair], sems.at[pair],
                        )

                sums[:size, :] = jnp.zeros((size, columns), jnp.float32)

                def add(pair, carry):
                    @pl.when(taken(pair))
                    def _():
                        wait_all(
                            (weight_all.at[pair], weight_sems.at[pair]),
                            (landed.at[pair, :size, :], sems.at[pair]),
                        )
                        sums[:size, :] += jnp.dot(
                            landed[pair, :size, :],
                            weight_all[pair],
                            preferred_element_type=jnp.float32,
                        )

                    return carry

                lax.fori_loop(0, pairs, add, 0)
                copy = pltpu.make_async_copy(
                    sums.at[:size, :], out_ref.at[:size, :], out_sem.at[0]
                )
                copy.start()
                copy.wait()

            below = size

    any_spec = pl.BlockSpec(memory_space=pl.ANY)
    inputs = pinned(flat + [shards[distance] for distance in distances])
    return pl.pallas_call(
        body,
        grid_spec=pltpu.PrefetchScalarGridSpec(
            num_scalar_prefetch=3,
            grid=(1,),
            in_specs=[any_spec] * len(inputs),
            out_specs=any_spec,
            scratch_shapes=[
                pltpu.VMEM((pairs, always, 2 * width), jnp.bfloat16),
                pltpu.VMEM((pairs, 2 * width, columns), jnp.bfloat16),
                pltpu.VMEM((always, columns), jnp.float32),
                pltpu.SemaphoreType.DMA((pairs,)),
                pltpu.SemaphoreType.DMA((pairs,)),
                pltpu.SemaphoreType.DMA((1,)),
            ],
        ),
        out_shape=jax.ShapeDtypeStruct((always, columns), jnp.float32),
        compiler_params=params(56),
        cost_estimate=pl.CostEstimate(
            flops=0, bytes_accessed=always * columns, transcendentals=0
        ),
        name="project_near",
    )(place, group, counts, *inputs)


def project(place, group, counts, features, more, shards, partial, rows):
    count = len(features)
    pairs = count // 2
    width = more.shape[2]
    total = count * rows
    always = total - more.shape[1]
    distances = sorted(shards)
    columns = shards[0].shape[1]
    each = shards[0].shape[0] // width
    bounds = [size for size in variants(total) if size <= always] + [total]
    flat = [piece for pieces in features for piece in pieces]

    def body(place_ref, group_ref, counts_ref, *refs):
        grouped = group_refs(refs[: len(flat)], features)
        more_ref, partial_ref = refs[len(flat) : len(flat) + 2]
        refs = refs[len(flat) + 2 :]
        shard_refs = refs[: len(distances)]
        out_refs = refs[len(distances) : len(distances) + count]
        landed, weight_all, sums, sems, weight_sems, partial_sem = refs[len(distances) + count :]
        used = sum(counts_ref[mask] for mask in range(count)) * BLOCK

        def left(pair):
            apart = shard_apart(place_ref, group_ref, pair, each)
            return (pair == pairs - 1) | (apart > NEAR) | (apart < -NEAR)

        below = 0
        for size in bounds:
            low = min(size, always)

            @pl.when((used > below) & (used <= size))
            def _(size=size, low=low):
                load = pltpu.make_async_copy(
                    partial_ref.at[:low, :], sums.at[:low, :], partial_sem.at[0]
                )
                load.start()
                for pair in range(pairs):
                    sources = [list(grouped[2 * pair + side]) for side in range(2)]
                    if size > always:
                        for side in range(2):
                            sources[side].append(more_ref.at[2 * pair + side])

                    @pl.when(left(pair) | (size > always))
                    def _(pair=pair, sources=sources):
                        send_weights(
                            place_ref, group_ref, pair, each, width, distances, shard_refs,
                            weight_all.at[pair], weight_sems.at[pair],
                        )
                        send_features(sources, size, width, landed.at[pair], sems.at[pair])

                if size > always:
                    sums[always:, :] = jnp.zeros((total - always, columns), jnp.float32)
                load.wait()

                def add_rows(pair, first, end):
                    sums[first:end, :] += jnp.dot(
                        landed[pair, first:end, :],
                        weight_all[pair],
                        preferred_element_type=jnp.float32,
                    )

                def add(pair, carry):
                    @pl.when(left(pair) | (size > always))
                    def _():
                        wait_all(
                            (weight_all.at[pair], weight_sems.at[pair]),
                            (landed.at[pair, :size, :], sems.at[pair]),
                        )

                    @pl.when(left(pair))
                    def _():
                        add_rows(pair, 0, low)

                    if size > always:
                        add_rows(pair, always, size)
                    return carry

                lax.fori_loop(0, pairs, add, 0)

            below = size
        for mask in range(count):
            position = 0
            for view in range(count):
                position = position + jnp.where(
                    view < (place_ref[0] ^ mask), counts_ref[place_ref[0] ^ view], 0
                )
            moved = sums[rows_at(position * BLOCK, rows), :]
            out_refs[mask][...] = moved.astype(jnp.bfloat16)

    any_spec = pl.BlockSpec(memory_space=pl.ANY)
    inputs = pinned(flat + [more, partial] + [shards[distance] for distance in distances])
    return pl.pallas_call(
        body,
        grid_spec=pltpu.PrefetchScalarGridSpec(
            num_scalar_prefetch=3,
            grid=(1,),
            in_specs=[any_spec] * len(inputs),
            out_specs=[full_spec((rows, columns))] * count,
            scratch_shapes=[
                pltpu.VMEM((pairs, total, 2 * width), jnp.bfloat16),
                pltpu.VMEM((pairs, 2 * width, columns), jnp.bfloat16),
                pltpu.VMEM((total, columns), jnp.float32),
                pltpu.SemaphoreType.DMA((pairs,)),
                pltpu.SemaphoreType.DMA((pairs,)),
                pltpu.SemaphoreType.DMA((1,)),
            ],
        ),
        out_shape=[jax.ShapeDtypeStruct((rows, columns), jnp.bfloat16)] * count,
        compiler_params=params(56),
        cost_estimate=pl.CostEstimate(
            flops=total * count * width * columns // 4,
            bytes_accessed=total * count * width,
            transcendentals=0,
        ),
        name="project",
    )(place, group, counts, *inputs)


def assemble(place, block_counts, row_mask, pieces, count):
    rows, columns = pieces[0].shape
    if columns % HEAD_DIM:
        stacked = jnp.stack(pieces)[jnp.arange(count) ^ place[0]]
        result = jnp.moveaxis(stacked, 0, 1).reshape(rows, count * columns)
        offsets = jnp.arange(rows, dtype=jnp.int32)
        good = (row_mask[0] == 1) & (offsets // BLOCK < block_counts[0, 0])
        return jnp.where(good[:, None], result, jnp.bfloat16(0.0))

    def body(place_ref, blocks_ref, mask_ref, *refs):
        out_ref = refs[-1]
        good = valid_column(mask_ref, blocks_ref[0, 0]) > 0.5
        for mask in range(count):
            start = pl.multiple_of((place_ref[0] ^ mask) * columns, HEAD_DIM)
            out_ref[:, pl.ds(start, columns)] = jnp.where(
                good, refs[mask][...], jnp.bfloat16(0.0)
            )

    return pl.pallas_call(
        body,
        grid_spec=pltpu.PrefetchScalarGridSpec(
            num_scalar_prefetch=2,
            grid=(1,),
            in_specs=[full_spec((1, rows))] + [full_spec((rows, columns))] * count,
            out_specs=full_spec((rows, count * columns)),
        ),
        out_shape=jax.ShapeDtypeStruct((rows, count * columns), jnp.bfloat16),
        compiler_params=params(16),
        cost_estimate=pl.CostEstimate(
            flops=0, bytes_accessed=4 * rows * count * columns, transcendentals=0
        ),
        name="assemble",
    )(
        place,
        block_counts,
        row_mask,
        pltpu.with_memory_space_constraint(pieces[0], pltpu.HBM),
        *pieces[1:],
    )


def local(queries, keys, values, out_weight, block_counts, row_mask):
    rows = queries.shape[1]
    count = lax.axis_size("cam")
    total = count * rows
    place_array = jnp.full((1,), lax.axis_index("cam"), jnp.int32)
    group_array = jnp.full((1,), lax.axis_index("fsdp"), jnp.int32)

    shards = {0: cut_weight(place_array, out_weight, count)}
    queries, shards[0] = lax.optimization_barrier((queries, shards[0]))
    groups = lax.axis_size("fsdp")

    received = [None] * count
    early = [mask for mask in order(count) if mask & 1 == 0]
    late = [mask for mask in order(count) if mask & 1]
    pass_weight(shards, 1)

    def payloads_for(masks):
        packed = pack(place_array, block_counts, row_mask, queries, keys, values, masks, count)
        return dict(zip(masks, packed))

    for mask, block in payloads_for(early).items():
        received[mask] = xor_permute(block, mask, count)
    received[early[0]], queries = lax.optimization_barrier((received[early[0]], queries))
    payloads = payloads_for(late + [0])
    received[0] = payloads[0]
    received[late[0]] = xor_permute(payloads[late[0]], late[0], count)
    gate = [received[mask] for mask in early[1:]]
    gate, shards[1], shards[-1] = lax.optimization_barrier((gate, shards[1], shards[-1]))
    for mask, block in zip(early[1:], gate):
        received[mask] = block
    pass_weight(shards, 2)
    received[late[0]], payloads = lax.optimization_barrier((received[late[0]], payloads))
    for mask in late[1:]:
        received[mask] = xor_permute(payloads[mask], mask, count)
    always = total * 3 // 5
    attended, rest, counts, used = attend(
        place_array, received, rows, (always, total - always)
    )
    shape = jax.ShapeDtypeStruct((count,) + rest.shape, rest.dtype)

    def gather_rest(part):
        return jnp.stack([jnp.concatenate(pieces) for pieces in gather_features(part, count)])

    def weight_step(arrived):
        arrived, shards[2], shards[-2] = lax.optimization_barrier((arrived, shards[2], shards[-2]))
        pass_weight(shards, 3)
        return arrived

    features = gather_features(attended, count, weight_step)
    for distance in range(4, groups):
        pass_weight(shards, distance)
    partial = project_near(
        place_array, group_array, counts, features, shards, rows, always
    )
    rest, features, shards, partial = lax.optimization_barrier((rest, features, shards, partial))
    more = lax.cond(used[0] > always, gather_rest, lambda part: unfilled(shape), rest)
    pieces = project(
        place_array, group_array, counts, features, more, shards, partial, rows
    )
    landed = [pieces[0]] + [None] * (count - 1)
    for mask in order(count):
        landed[mask] = xor_permute(pieces[mask], mask, count)
    return assemble(place_array, block_counts, row_mask, landed, count)[None]


def solution(mesh):
    in_specs = (
        P("fsdp", "cam", None),
        P("fsdp", "cam", None),
        P("fsdp", "cam", None),
        P("fsdp", None),
        P("fsdp", "cam"),
        P("fsdp", "cam"),
    )
    out_specs = P("fsdp", "cam", None)
    return jax.shard_map(local, mesh=mesh, in_specs=in_specs, out_specs=out_specs, check_vma=False)
```

```python
import math

import jax
import jax.numpy as jnp
from jax import lax
from jax.experimental import pallas as pl
from jax.experimental.pallas import tpu as pltpu
from jax.sharding import PartitionSpec as P

HEAD_DIM = 128
BLOCK = 32
SENTINEL = 32.0
LIMIT = 24.0
UNIT = 128


def params(mebibytes):
    return pltpu.CompilerParams(vmem_limit_bytes=mebibytes * 1024 * 1024)


def order(count):
    return sorted(range(1, count), key=lambda mask: (mask == 1, mask & 1, -bin(mask).count("1")))


def variants(total):
    return sorted({-(-total * tenths // (10 * UNIT)) * UNIT for tenths in (4, 5, 6, 8, 10)})


def full_spec(shape):
    return pl.BlockSpec(shape, lambda i, *_: (0,) * len(shape))


def column_of(row):
    n = row.shape[1]
    diagonal = lax.broadcasted_iota(jnp.int32, (n, n), 0) == lax.broadcasted_iota(
        jnp.int32, (n, n), 1
    )
    return jnp.sum(jnp.where(diagonal, row, 0.0), axis=1, keepdims=True)


def valid_column(mask_ref, blocks):
    rows = mask_ref.shape[1]
    inside = lax.broadcasted_iota(jnp.int32, (1, rows), 1) < blocks * BLOCK
    return column_of(jnp.where((mask_ref[...] == 1) & inside, 1.0, 0.0))


def xor_permute(array, mask, count):
    return lax.ppermute(array, "cam", [(place, place ^ mask) for place in range(count)])


def cut_weight(place, out_weight, count):
    depth = out_weight.shape[0]
    columns = out_weight.shape[1] // count
    if columns % HEAD_DIM:
        return lax.dynamic_slice_in_dim(out_weight, place[0] * columns, columns, axis=1)
    parts = 4
    step = depth // parts

    def body(place_ref, w_ref, out_ref, held, load_sems, store_sems):
        start = pl.multiple_of(place_ref[0] * columns, HEAD_DIM)
        loads, stores = [], []
        for part in range(parts):
            inside = pl.ds(part * step, step)
            load = pltpu.make_async_copy(
                w_ref.at[inside, pl.ds(start, columns)], held.at[part], load_sems.at[part]
            )
            load.start()
            loads.append(load)
        for part in range(parts):
            inside = pl.ds(part * step, step)
            loads[part].wait()
            store = pltpu.make_async_copy(held.at[part], out_ref.at[inside, :], store_sems.at[part])
            store.start()
            stores.append(store)
        for store in stores:
            store.wait()

    return pl.pallas_call(
        body,
        grid_spec=pltpu.PrefetchScalarGridSpec(
            num_scalar_prefetch=1,
            grid=(1,),
            in_specs=[pl.BlockSpec(memory_space=pl.ANY)],
            out_specs=pl.BlockSpec(memory_space=pl.ANY),
            scratch_shapes=[
                pltpu.VMEM((parts, step, columns), jnp.bfloat16),
                pltpu.SemaphoreType.DMA((parts,)),
                pltpu.SemaphoreType.DMA((parts,)),
            ],
        ),
        out_shape=jax.ShapeDtypeStruct((depth, columns), jnp.bfloat16),
        compiler_params=params(56),
        cost_estimate=pl.CostEstimate(
            flops=0, bytes_accessed=4 * depth * columns, transcendentals=0
        ),
        name="cut_weight",
    )(place, out_weight)


def pack(place, block_counts, row_mask, queries, keys, values, masks, count):
    _, rows, features = queries.shape
    width = features // count
    number = len(masks)

    def body(place_ref, blocks_ref, mask_ref, q_ref, k_ref, v_ref, *refs):
        out_refs = refs[:number]
        held, load_sems, store_sems = refs[number:]

        def copies(index, slot):
            start = pl.multiple_of((place_ref[0] ^ masks[index]) * width, HEAD_DIM)
            source = (q_ref, k_ref, v_ref)[slot].at[0, :, pl.ds(start, width)]
            buffer = held.at[index, slot]
            return (
                pltpu.make_async_copy(source, buffer, load_sems.at[index, slot]),
                pltpu.make_async_copy(
                    buffer, out_refs[index].at[slot], store_sems.at[index, slot]
                ),
            )

        steps = [copies(index, slot) for slot in (1, 0, 2) for index in range(number)]
        for load, _ in steps:
            load.start()
        good = valid_column(mask_ref, blocks_ref[0, 0]) > 0.5
        for step, (load, store) in enumerate(steps):
            load.wait()
            if step < number:
                held[step, 1] = jnp.where(good, held[step, 1], jnp.bfloat16(SENTINEL))
            store.start()
        for _, store in steps:
            store.wait()

    any_spec = pl.BlockSpec(memory_space=pl.ANY)
    return list(
        pl.pallas_call(
            body,
            grid_spec=pltpu.PrefetchScalarGridSpec(
                num_scalar_prefetch=2,
                grid=(1,),
                in_specs=[full_spec((1, rows))] + [any_spec] * 3,
                out_specs=[any_spec] * number,
                scratch_shapes=[
                    pltpu.VMEM((number, 3, rows, width), jnp.bfloat16),
                    pltpu.SemaphoreType.DMA((number, 3)),
                    pltpu.SemaphoreType.DMA((number, 3)),
                ],
            ),
            out_shape=[jax.ShapeDtypeStruct((3, rows, width), jnp.bfloat16)] * number,
            compiler_params=params(56),
            cost_estimate=pl.CostEstimate(
                flops=0, bytes_accessed=12 * rows * width * number, transcendentals=0
            ),
            name="pack",
        )(place, block_counts, row_mask, queries, keys, values)
    )


def pass_weight(shards, distance):
    groups = lax.axis_size("fsdp")
    for sign in (1, -1):
        pairs = []
        for source in range(groups):
            origin, target = source - sign * (distance - 1), source + sign
            if 0 <= origin < groups and 0 <= target < groups:
                pairs.append((source, target))
        shards[sign * distance] = lax.ppermute(shards[sign * (distance - 1)], "fsdp", pairs)


def packed_offsets(place_ref, counts_ref, table, count):
    by_mask, running = [], 0
    for mask in range(count):
        by_mask.append(running)
        table[mask] = running
        running = running + counts_ref[mask] * BLOCK
    by_view, position = [], 0
    for view in range(count):
        by_view.append(position)
        position = position + counts_ref[place_ref[0] ^ view] * BLOCK
    return by_mask, by_view, running


def rows_at(start, size):
    return pl.ds(start if isinstance(start, int) else pl.multiple_of(start, BLOCK), size)


def tile_of(size):
    return max(rows for rows in range(UNIT, 6 * UNIT + 1, UNIT) if size % rows == 0)


def attend(place, received, rows, lengths):
    count = len(received)
    width = received[0].shape[2]
    total = count * rows
    span = 2 * HEAD_DIM
    factor = math.log2(math.e) / math.sqrt(HEAD_DIM)

    def body(place_ref, *refs):
        parts = refs[:count]
        out_refs = refs[count : count + len(lengths)]
        counts_ref, used_ref = refs[count + len(lengths) : count + len(lengths) + 2]
        query_all, key_all, value_all, result, ordered, table = refs[count + len(lengths) + 2 :]

        @pl.when(pl.program_id(0) == 0)
        def _():
            value_all[...] = jnp.zeros_like(value_all)
            for mask in range(count):
                blocks = jnp.zeros((1, HEAD_DIM), jnp.float32)
                for first in range(0, rows, BLOCK):
                    row = parts[mask][1, first : first + 16, :HEAD_DIM].astype(jnp.float32)[:1]
                    blocks = blocks + jnp.where(row < LIMIT, 1.0, 0.0)
                counts_ref[mask] = jnp.max(blocks).astype(jnp.int32)

        by_mask, by_view, used = packed_offsets(place_ref, counts_ref, table, count)
        used_ref[0] = used
        for mask in range(count):
            where = rows_at(by_mask[mask], rows)
            query_all[where, :] = parts[mask][0]
            key_all[where, :] = parts[mask][1]
            value_all[where, :] = parts[mask][2]
        key_all[rows_at(used, total // 5), :] = jnp.full((total // 5, span), SENTINEL, jnp.bfloat16)
        below = 0
        for size in variants(total):

            @pl.when((used > below) & (used <= size))
            def _(size=size):
                step = tile_of(size)
                key_mask = key_all[:size, :HEAD_DIM].astype(jnp.float32) > LIMIT
                bias = jnp.where(key_mask, jnp.float32(-1e30), 0.0)
                bias = jnp.concatenate([bias] * (step // HEAD_DIM), axis=1)
                values_t = [
                    value_all[:size, first : first + HEAD_DIM].T
                    for first in range(0, span, HEAD_DIM)
                ]

                def tile(index, carry):
                    if isinstance(index, int):
                        where = pl.ds(index * step, step)
                    else:
                        where = pl.ds(pl.multiple_of(index * step, UNIT), step)
                    for head in range(span // HEAD_DIM):
                        lanes = slice(head * HEAD_DIM, (head + 1) * HEAD_DIM)
                        scores = lax.dot_general(
                            key_all[:size, lanes],
                            query_all[where, lanes],
                            (((1,), (1,)), ((), ())),
                            preferred_element_type=jnp.float32,
                        )
                        scores = scores + bias
                        top = jnp.max(scores, axis=0, keepdims=True)
                        raised = jnp.exp2((scores - top) * factor)
                        norm = jnp.sum(raised, axis=0, keepdims=True)
                        summed = jnp.dot(
                            values_t[head],
                            raised.astype(jnp.bfloat16),
                            preferred_element_type=jnp.float32,
                        )
                        result[where, lanes] = (summed / norm).T.astype(jnp.bfloat16)
                    return carry

                if size == step:
                    tile(0, 0)
                else:
                    lax.fori_loop(0, size // step, tile, 0)

            below = size
        for view in range(count):
            moved = result[rows_at(table[place_ref[0] ^ view], rows), :]
            ordered[rows_at(by_view[view], rows), :] = moved
        first = 0
        for length, out_ref in zip(lengths, out_refs):
            out_ref[...] = ordered[first : first + length, :]
            first += length

    flops = 4 * total * total * width // 25
    return pl.pallas_call(
        body,
        grid_spec=pltpu.PrefetchScalarGridSpec(
            num_scalar_prefetch=1,
            grid=(width // span,),
            in_specs=[pl.BlockSpec((3, rows, span), lambda h, *_: (0, 0, h))] * count,
            out_specs=[pl.BlockSpec((length, span), lambda h, *_: (0, h)) for length in lengths]
            + [pl.BlockSpec(memory_space=pltpu.SMEM)] * 2,
            scratch_shapes=[
                pltpu.VMEM((total, span), jnp.bfloat16),
                pltpu.VMEM((total + total // 5, span), jnp.bfloat16),
                pltpu.VMEM((total, span), jnp.bfloat16),
                pltpu.VMEM((total, span), jnp.bfloat16),
                pltpu.VMEM((total, span), jnp.bfloat16),
                pltpu.SMEM((count,), jnp.int32),
            ],
        ),
        out_shape=[jax.ShapeDtypeStruct((length, width), jnp.bfloat16) for length in lengths]
        + [jax.ShapeDtypeStruct((count,), jnp.int32), jax.ShapeDtypeStruct((1,), jnp.int32)],
        compiler_params=params(40),
        cost_estimate=pl.CostEstimate(
            flops=flops, bytes_accessed=total * width, transcendentals=flops // 512
        ),
        name="attend",
    )(place, pltpu.with_memory_space_constraint(received[0], pltpu.HBM), *received[1:])


def gather_features(own, count, between=lambda arrived: arrived):
    half = own.shape[0] // 2
    held = {0: [own]}
    if count == 8:
        over_x = xor_permute(own, 2, count)
        over_y = xor_permute(own, 4, count)
        held[1] = [between(xor_permute(own, 1, count))]
        held[1][0], over_x, over_y = lax.optimization_barrier((held[1][0], over_x, over_y))
        held[2], held[4] = [over_x], [over_y]
        held[6] = [xor_permute(over_x[:half], 4, count), xor_permute(over_y[half:], 2, count)]
    else:
        for mask in range(2, count, 2):
            held[mask] = [xor_permute(own, mask, count)]
        held[1] = [between(xor_permute(own, 1, count))]
    for mask in range(2, count, 2):
        if mask == 4:
            held[6], held[4] = lax.optimization_barrier((held[6], held[4]))
        held[mask + 1] = [xor_permute(piece, 1, count) for piece in held[mask]]
    return [held[mask] for mask in range(count)]


def unfilled(shape):
    def body(out_ref):
        pass

    return pl.pallas_call(
        body,
        out_specs=pl.BlockSpec(memory_space=pl.ANY),
        out_shape=shape,
        name="unfilled",
    )()


NEAR = 2


def near_shards(shards):
    return {distance: shards[distance] for distance in shards if abs(distance) <= NEAR}


def shard_apart(place_ref, group_ref, pair, each):
    return group_ref[0] - (place_ref[0] ^ (2 * pair)) // each


def send_weights(place_ref, group_ref, pair, each, width, distances, shard_refs, target, sem):
    apart = shard_apart(place_ref, group_ref, pair, each)
    for distance, shard_ref in zip(distances, shard_refs):

        @pl.when(apart == distance)
        def _():
            for side in range(2):
                owner = place_ref[0] ^ (2 * pair + side)
                start = pl.multiple_of((owner % each) * width, width)
                pltpu.make_async_copy(
                    shard_ref.at[pl.ds(start, width), :],
                    target.at[side * width : (side + 1) * width, :],
                    sem,
                ).start()


def send_features(piece_refs, size, width, target, sem):
    for side, refs in enumerate(piece_refs):
        first = 0
        for ref in refs:
            length = min(ref.shape[0], size - first)
            pltpu.make_async_copy(
                ref.at[:length, :],
                target.at[first : first + length, side * width : (side + 1) * width],
                sem,
            ).start()
            first += length


def wait_all(*buffers_and_sems):
    for buffer, sem in buffers_and_sems:
        pltpu.make_async_copy(buffer, buffer, sem).wait()


def group_refs(refs, features):
    grouped, taken = [], 0
    for pieces in features:
        grouped.append(refs[taken : taken + len(pieces)])
        taken += len(pieces)
    return grouped


def pinned(arrays):
    return [pltpu.with_memory_space_constraint(array, pltpu.HBM) for array in arrays]


def project_near(place, group, counts, features, shards, rows, always):
    count = len(features)
    pairs = count // 2 - 1
    flat = [piece for pieces in features[: 2 * pairs] for piece in pieces]
    width = flat[0].shape[1]
    shards = near_shards(shards)
    distances = sorted(shards)
    columns = shards[0].shape[1]
    each = shards[0].shape[0] // width
    bounds = [size for size in variants(count * rows) if size <= always]

    def body(place_ref, group_ref, counts_ref, *refs):
        grouped = group_refs(refs[: len(flat)], features[: 2 * pairs])
        shard_refs = refs[len(flat) : len(flat) + len(distances)]
        out_ref, landed, weight_all, sums, sems, weight_sems, out_sem = refs[
            len(flat) + len(distances) :
        ]
        used = sum(counts_ref[mask] for mask in range(count)) * BLOCK

        def taken(pair):
            apart = shard_apart(place_ref, group_ref, pair, each)
            return (apart <= NEAR) & (apart >= -NEAR)

        below = 0
        for size in bounds:

            @pl.when((used > below) & ((used <= size) | (size == always)))
            def _(size=size):
                for pair in range(pairs):

                    @pl.when(taken(pair))
                    def _(pair=pair):
                        send_weights(
                            place_ref, group_ref, pair, each, width, distances, shard_refs,
                            weight_all.at[pair], weight_sems.at[pair],
                        )
                        send_features(
                            grouped[2 * pair : 2 * pair + 2], size, width,
                            landed.at[pair], sems.at[pair],
                        )

                sums[:size, :] = jnp.zeros((size, columns), jnp.float32)

                def add(pair, carry):
                    @pl.when(taken(pair))
                    def _():
                        wait_all(
                            (weight_all.at[pair], weight_sems.at[pair]),
                            (landed.at[pair, :size, :], sems.at[pair]),
                        )
                        sums[:size, :] += jnp.dot(
                            landed[pair, :size, :],
                            weight_all[pair],
                            preferred_element_type=jnp.float32,
                        )

                    return carry

                lax.fori_loop(0, pairs, add, 0)
                copy = pltpu.make_async_copy(
                    sums.at[:size, :], out_ref.at[:size, :], out_sem.at[0]
                )
                copy.start()
                copy.wait()

            below = size

    any_spec = pl.BlockSpec(memory_space=pl.ANY)
    inputs = pinned(flat + [shards[distance] for distance in distances])
    return pl.pallas_call(
        body,
        grid_spec=pltpu.PrefetchScalarGridSpec(
            num_scalar_prefetch=3,
            grid=(1,),
            in_specs=[any_spec] * len(inputs),
            out_specs=any_spec,
            scratch_shapes=[
                pltpu.VMEM((pairs, always, 2 * width), jnp.bfloat16),
                pltpu.VMEM((pairs, 2 * width, columns), jnp.bfloat16),
                pltpu.VMEM((always, columns), jnp.float32),
                pltpu.SemaphoreType.DMA((pairs,)),
                pltpu.SemaphoreType.DMA((pairs,)),
                pltpu.SemaphoreType.DMA((1,)),
            ],
        ),
        out_shape=jax.ShapeDtypeStruct((always, columns), jnp.float32),
        compiler_params=params(56),
        cost_estimate=pl.CostEstimate(
            flops=0, bytes_accessed=always * columns, transcendentals=0
        ),
        name="project_near",
    )(place, group, counts, *inputs)


def project(place, group, counts, features, more, shards, partial, rows):
    count = len(features)
    pairs = count // 2
    width = more.shape[2]
    total = count * rows
    always = total - more.shape[1]
    distances = sorted(shards)
    columns = shards[0].shape[1]
    each = shards[0].shape[0] // width
    bounds = variants(total)
    flat = [piece for pieces in features for piece in pieces]

    def body(place_ref, group_ref, counts_ref, *refs):
        grouped = group_refs(refs[: len(flat)], features)
        more_ref, partial_ref = refs[len(flat) : len(flat) + 2]
        refs = refs[len(flat) + 2 :]
        shard_refs = refs[: len(distances)]
        out_refs = refs[len(distances) : len(distances) + count]
        landed, weight_all, sums, sems, weight_sems, partial_sem = refs[len(distances) + count :]
        used = sum(counts_ref[mask] for mask in range(count)) * BLOCK

        def left(pair):
            apart = shard_apart(place_ref, group_ref, pair, each)
            return (pair == pairs - 1) | (apart > NEAR) | (apart < -NEAR)

        below = 0
        for size in bounds:
            low = min(size, always)

            @pl.when((used > below) & (used <= size))
            def _(size=size, low=low):
                load = pltpu.make_async_copy(
                    partial_ref.at[:low, :], sums.at[:low, :], partial_sem.at[0]
                )
                load.start()
                for pair in range(pairs):
                    sources = [list(grouped[2 * pair + side]) for side in range(2)]
                    if size > always:
                        for side in range(2):
                            sources[side].append(more_ref.at[2 * pair + side])

                    @pl.when(left(pair) | (size > always))
                    def _(pair=pair, sources=sources):
                        send_weights(
                            place_ref, group_ref, pair, each, width, distances, shard_refs,
                            weight_all.at[pair], weight_sems.at[pair],
                        )
                        send_features(sources, size, width, landed.at[pair], sems.at[pair])

                if size > always:
                    sums[always:, :] = jnp.zeros((total - always, columns), jnp.float32)
                load.wait()

                def add_rows(pair, first, end):
                    sums[first:end, :] += jnp.dot(
                        landed[pair, first:end, :],
                        weight_all[pair],
                        preferred_element_type=jnp.float32,
                    )

                def add(pair, carry):
                    @pl.when(left(pair) | (size > always))
                    def _():
                        wait_all(
                            (weight_all.at[pair], weight_sems.at[pair]),
                            (landed.at[pair, :size, :], sems.at[pair]),
                        )

                    @pl.when(left(pair))
                    def _():
                        add_rows(pair, 0, low)

                    if size > always:
                        add_rows(pair, always, size)
                    return carry

                lax.fori_loop(0, pairs, add, 0)

            below = size
        for mask in range(count):
            position = 0
            for view in range(count):
                position = position + jnp.where(
                    view < (place_ref[0] ^ mask), counts_ref[place_ref[0] ^ view], 0
                )
            moved = sums[rows_at(position * BLOCK, rows), :]
            out_refs[mask][...] = moved.astype(jnp.bfloat16)

    any_spec = pl.BlockSpec(memory_space=pl.ANY)
    inputs = pinned(flat + [more, partial] + [shards[distance] for distance in distances])
    return pl.pallas_call(
        body,
        grid_spec=pltpu.PrefetchScalarGridSpec(
            num_scalar_prefetch=3,
            grid=(1,),
            in_specs=[any_spec] * len(inputs),
            out_specs=[full_spec((rows, columns))] * count,
            scratch_shapes=[
                pltpu.VMEM((pairs, total, 2 * width), jnp.bfloat16),
                pltpu.VMEM((pairs, 2 * width, columns), jnp.bfloat16),
                pltpu.VMEM((total, columns), jnp.float32),
                pltpu.SemaphoreType.DMA((pairs,)),
                pltpu.SemaphoreType.DMA((pairs,)),
                pltpu.SemaphoreType.DMA((1,)),
            ],
        ),
        out_shape=[jax.ShapeDtypeStruct((rows, columns), jnp.bfloat16)] * count,
        compiler_params=params(56),
        cost_estimate=pl.CostEstimate(
            flops=total * count * width * columns // 4,
            bytes_accessed=total * count * width,
            transcendentals=0,
        ),
        name="project",
    )(place, group, counts, *inputs)


def assemble(place, block_counts, row_mask, pieces, count):
    rows, columns = pieces[0].shape
    if columns % HEAD_DIM:
        stacked = jnp.stack(pieces)[jnp.arange(count) ^ place[0]]
        result = jnp.moveaxis(stacked, 0, 1).reshape(rows, count * columns)
        offsets = jnp.arange(rows, dtype=jnp.int32)
        good = (row_mask[0] == 1) & (offsets // BLOCK < block_counts[0, 0])
        return jnp.where(good[:, None], result, jnp.bfloat16(0.0))

    def body(place_ref, blocks_ref, mask_ref, *refs):
        out_ref = refs[-1]
        good = valid_column(mask_ref, blocks_ref[0, 0]) > 0.5
        for mask in range(count):
            start = pl.multiple_of((place_ref[0] ^ mask) * columns, HEAD_DIM)
            out_ref[:, pl.ds(start, columns)] = jnp.where(
                good, refs[mask][...], jnp.bfloat16(0.0)
            )

    return pl.pallas_call(
        body,
        grid_spec=pltpu.PrefetchScalarGridSpec(
            num_scalar_prefetch=2,
            grid=(1,),
            in_specs=[full_spec((1, rows))] + [full_spec((rows, columns))] * count,
            out_specs=full_spec((rows, count * columns)),
        ),
        out_shape=jax.ShapeDtypeStruct((rows, count * columns), jnp.bfloat16),
        compiler_params=params(16),
        cost_estimate=pl.CostEstimate(
            flops=0, bytes_accessed=4 * rows * count * columns, transcendentals=0
        ),
        name="assemble",
    )(
        place,
        block_counts,
        row_mask,
        pltpu.with_memory_space_constraint(pieces[0], pltpu.HBM),
        *pieces[1:],
    )


def local(queries, keys, values, out_weight, block_counts, row_mask):
    rows = queries.shape[1]
    count = lax.axis_size("cam")
    total = count * rows
    place_array = jnp.full((1,), lax.axis_index("cam"), jnp.int32)
    group_array = jnp.full((1,), lax.axis_index("fsdp"), jnp.int32)

    shards = {0: cut_weight(place_array, out_weight, count)}
    queries, shards[0] = lax.optimization_barrier((queries, shards[0]))
    groups = lax.axis_size("fsdp")

    received = [None] * count
    early = [mask for mask in order(count) if mask & 1 == 0]
    late = [mask for mask in order(count) if mask & 1]
    pass_weight(shards, 1)

    def payloads_for(masks):
        packed = pack(place_array, block_counts, row_mask, queries, keys, values, masks, count)
        return dict(zip(masks, packed))

    for mask, block in payloads_for(early).items():
        received[mask] = xor_permute(block, mask, count)
    received[early[0]], queries = lax.optimization_barrier((received[early[0]], queries))
    payloads = payloads_for(late + [0])
    received[0] = payloads[0]
    received[late[0]] = xor_permute(payloads[late[0]], late[0], count)
    gate = [received[mask] for mask in early[1:]]
    gate, shards[1], shards[-1] = lax.optimization_barrier((gate, shards[1], shards[-1]))
    for mask, block in zip(early[1:], gate):
        received[mask] = block
    pass_weight(shards, 2)
    received[late[0]], payloads = lax.optimization_barrier((received[late[0]], payloads))
    for mask in late[1:]:
        received[mask] = xor_permute(payloads[mask], mask, count)
    always = total * 3 // 5
    attended, rest, counts, used = attend(
        place_array, received, rows, (always, total - always)
    )
    shape = jax.ShapeDtypeStruct((count,) + rest.shape, rest.dtype)

    split = rest.shape[0] // 2
    part_shape = jax.ShapeDtypeStruct((count, split, rest.shape[1]), rest.dtype)

    def gather_part(part):
        return jnp.stack([jnp.concatenate(pieces) for pieces in gather_features(part, count)])

    def gather_rest(part):
        first = gather_part(part[:split])
        first, last = lax.optimization_barrier((first, part[split:]))
        second = lax.cond(
            used[0] > always + split, gather_part, lambda piece: unfilled(part_shape), last
        )
        return jnp.concatenate([first, second], axis=1)

    def weight_step(arrived):
        arrived, shards[2], shards[-2] = lax.optimization_barrier((arrived, shards[2], shards[-2]))
        pass_weight(shards, 3)
        return arrived

    features = gather_features(attended, count, weight_step)
    for distance in range(4, groups):
        pass_weight(shards, distance)
    partial = project_near(
        place_array, group_array, counts, features, shards, rows, always
    )
    rest, features, shards, partial = lax.optimization_barrier((rest, features, shards, partial))
    more = lax.cond(used[0] > always, gather_rest, lambda part: unfilled(shape), rest)
    pieces = project(
        place_array, group_array, counts, features, more, shards, partial, rows
    )
    landed = [pieces[0]] + [None] * (count - 1)
    for mask in order(count):
        landed[mask] = xor_permute(pieces[mask], mask, count)
    return assemble(place_array, block_counts, row_mask, landed, count)[None]


def solution(mesh):
    in_specs = (
        P("fsdp", "cam", None),
        P("fsdp", "cam", None),
        P("fsdp", "cam", None),
        P("fsdp", None),
        P("fsdp", "cam"),
        P("fsdp", "cam"),
    )
    out_specs = P("fsdp", "cam", None)
    return jax.shard_map(local, mesh=mesh, in_specs=in_specs, out_specs=out_specs, check_vma=False)
```

```python
import math

import jax
import jax.numpy as jnp
from jax import lax
from jax.experimental import pallas as pl
from jax.experimental.pallas import tpu as pltpu
from jax.sharding import PartitionSpec as P

HEAD_DIM = 128
BLOCK = 32
SENTINEL = 32.0
LIMIT = 24.0
UNIT = 128


def params(mebibytes):
    return pltpu.CompilerParams(vmem_limit_bytes=mebibytes * 1024 * 1024)


def order(count):
    return sorted(range(1, count), key=lambda mask: (mask == 1, mask & 1, -bin(mask).count("1")))


def variants(total):
    return sorted({-(-total * tenths // (10 * UNIT)) * UNIT for tenths in (4, 5, 6, 8, 10)})


def full_spec(shape):
    return pl.BlockSpec(shape, lambda i, *_: (0,) * len(shape))


def column_of(row):
    n = row.shape[1]
    diagonal = lax.broadcasted_iota(jnp.int32, (n, n), 0) == lax.broadcasted_iota(
        jnp.int32, (n, n), 1
    )
    return jnp.sum(jnp.where(diagonal, row, 0.0), axis=1, keepdims=True)


def valid_column(mask_ref, blocks):
    rows = mask_ref.shape[1]
    inside = lax.broadcasted_iota(jnp.int32, (1, rows), 1) < blocks * BLOCK
    return column_of(jnp.where((mask_ref[...] == 1) & inside, 1.0, 0.0))


def xor_permute(array, mask, count):
    return lax.ppermute(array, "cam", [(place, place ^ mask) for place in range(count)])


def cut_weight(place, out_weight, count):
    depth = out_weight.shape[0]
    columns = out_weight.shape[1] // count
    if columns % HEAD_DIM:
        return lax.dynamic_slice_in_dim(out_weight, place[0] * columns, columns, axis=1)
    parts = 4
    step = depth // parts

    def body(place_ref, w_ref, out_ref, held, load_sems, store_sems):
        start = pl.multiple_of(place_ref[0] * columns, HEAD_DIM)
        loads, stores = [], []
        for part in range(parts):
            inside = pl.ds(part * step, step)
            load = pltpu.make_async_copy(
                w_ref.at[inside, pl.ds(start, columns)], held.at[part], load_sems.at[part]
            )
            load.start()
            loads.append(load)
        for part in range(parts):
            inside = pl.ds(part * step, step)
            loads[part].wait()
            store = pltpu.make_async_copy(held.at[part], out_ref.at[inside, :], store_sems.at[part])
            store.start()
            stores.append(store)
        for store in stores:
            store.wait()

    return pl.pallas_call(
        body,
        grid_spec=pltpu.PrefetchScalarGridSpec(
            num_scalar_prefetch=1,
            grid=(1,),
            in_specs=[pl.BlockSpec(memory_space=pl.ANY)],
            out_specs=pl.BlockSpec(memory_space=pl.ANY),
            scratch_shapes=[
                pltpu.VMEM((parts, step, columns), jnp.bfloat16),
                pltpu.SemaphoreType.DMA((parts,)),
                pltpu.SemaphoreType.DMA((parts,)),
            ],
        ),
        out_shape=jax.ShapeDtypeStruct((depth, columns), jnp.bfloat16),
        compiler_params=params(56),
        cost_estimate=pl.CostEstimate(
            flops=0, bytes_accessed=4 * depth * columns, transcendentals=0
        ),
        name="cut_weight",
    )(place, out_weight)


def pack(place, block_counts, row_mask, queries, keys, values, masks, count):
    _, rows, features = queries.shape
    width = features // count
    number = len(masks)

    def body(place_ref, blocks_ref, mask_ref, q_ref, k_ref, v_ref, *refs):
        out_refs = refs[:number]
        held, load_sems, store_sems = refs[number:]

        def copies(index, slot):
            start = pl.multiple_of((place_ref[0] ^ masks[index]) * width, HEAD_DIM)
            source = (q_ref, k_ref, v_ref)[slot].at[0, :, pl.ds(start, width)]
            buffer = held.at[index, slot]
            return (
                pltpu.make_async_copy(source, buffer, load_sems.at[index, slot]),
                pltpu.make_async_copy(
                    buffer, out_refs[index].at[slot], store_sems.at[index, slot]
                ),
            )

        steps = [copies(index, slot) for slot in (1, 0, 2) for index in range(number)]
        for load, _ in steps:
            load.start()
        good = valid_column(mask_ref, blocks_ref[0, 0]) > 0.5
        for step, (load, store) in enumerate(steps):
            load.wait()
            if step < number:
                held[step, 1] = jnp.where(good, held[step, 1], jnp.bfloat16(SENTINEL))
            store.start()
        for _, store in steps:
            store.wait()

    any_spec = pl.BlockSpec(memory_space=pl.ANY)
    return list(
        pl.pallas_call(
            body,
            grid_spec=pltpu.PrefetchScalarGridSpec(
                num_scalar_prefetch=2,
                grid=(1,),
                in_specs=[full_spec((1, rows))] + [any_spec] * 3,
                out_specs=[any_spec] * number,
                scratch_shapes=[
                    pltpu.VMEM((number, 3, rows, width), jnp.bfloat16),
                    pltpu.SemaphoreType.DMA((number, 3)),
                    pltpu.SemaphoreType.DMA((number, 3)),
                ],
            ),
            out_shape=[jax.ShapeDtypeStruct((3, rows, width), jnp.bfloat16)] * number,
            compiler_params=params(56),
            cost_estimate=pl.CostEstimate(
                flops=0, bytes_accessed=12 * rows * width * number, transcendentals=0
            ),
            name="pack",
        )(place, block_counts, row_mask, queries, keys, values)
    )


def pass_weight(shards, distance):
    groups = lax.axis_size("fsdp")
    for sign in (1, -1):
        pairs = []
        for source in range(groups):
            origin, target = source - sign * (distance - 1), source + sign
            if 0 <= origin < groups and 0 <= target < groups:
                pairs.append((source, target))
        shards[sign * distance] = lax.ppermute(shards[sign * (distance - 1)], "fsdp", pairs)


def packed_offsets(place_ref, counts_ref, table, count):
    by_mask, running = [], 0
    for mask in range(count):
        by_mask.append(running)
        table[mask] = running
        running = running + counts_ref[mask] * BLOCK
    by_view, position = [], 0
    for view in range(count):
        by_view.append(position)
        position = position + counts_ref[place_ref[0] ^ view] * BLOCK
    return by_mask, by_view, running


def rows_at(start, size):
    return pl.ds(start if isinstance(start, int) else pl.multiple_of(start, BLOCK), size)


def tile_of(size):
    return max(rows for rows in range(UNIT, 6 * UNIT + 1, UNIT) if size % rows == 0)


def attend(place, received, rows, lengths):
    count = len(received)
    width = received[0].shape[2]
    total = count * rows
    span = 2 * HEAD_DIM
    factor = math.log2(math.e) / math.sqrt(HEAD_DIM)

    def body(place_ref, *refs):
        parts = refs[:count]
        out_refs = refs[count : count + len(lengths)]
        counts_ref, used_ref = refs[count + len(lengths) : count + len(lengths) + 2]
        query_all, key_all, value_all, result, ordered, table = refs[count + len(lengths) + 2 :]

        @pl.when(pl.program_id(0) == 0)
        def _():
            value_all[...] = jnp.zeros_like(value_all)
            for mask in range(count):
                blocks = jnp.zeros((1, HEAD_DIM), jnp.float32)
                for first in range(0, rows, BLOCK):
                    row = parts[mask][1, first : first + 16, :HEAD_DIM].astype(jnp.float32)[:1]
                    blocks = blocks + jnp.where(row < LIMIT, 1.0, 0.0)
                counts_ref[mask] = jnp.max(blocks).astype(jnp.int32)

        by_mask, by_view, used = packed_offsets(place_ref, counts_ref, table, count)
        used_ref[0] = used
        for mask in range(count):
            where = rows_at(by_mask[mask], rows)
            query_all[where, :] = parts[mask][0]
            key_all[where, :] = parts[mask][1]
            value_all[where, :] = parts[mask][2]
        key_all[rows_at(used, total // 5), :] = jnp.full((total // 5, span), SENTINEL, jnp.bfloat16)
        below = 0
        for size in variants(total):

            @pl.when((used > below) & (used <= size))
            def _(size=size):
                step = tile_of(size)
                key_mask = key_all[:size, :HEAD_DIM].astype(jnp.float32) > LIMIT
                bias = jnp.where(key_mask, jnp.float32(-1e30), 0.0)
                bias = jnp.concatenate([bias] * (step // HEAD_DIM), axis=1)
                values_t = [
                    value_all[:size, first : first + HEAD_DIM].T
                    for first in range(0, span, HEAD_DIM)
                ]

                def tile(index, carry):
                    if isinstance(index, int):
                        where = pl.ds(index * step, step)
                    else:
                        where = pl.ds(pl.multiple_of(index * step, UNIT), step)
                    for head in range(span // HEAD_DIM):
                        lanes = slice(head * HEAD_DIM, (head + 1) * HEAD_DIM)
                        scores = lax.dot_general(
                            key_all[:size, lanes],
                            query_all[where, lanes],
                            (((1,), (1,)), ((), ())),
                            preferred_element_type=jnp.float32,
                        )
                        scores = scores + bias
                        top = jnp.max(scores, axis=0, keepdims=True)
                        raised = jnp.exp2((scores - top) * factor)
                        norm = jnp.sum(raised, axis=0, keepdims=True)
                        summed = jnp.dot(
                            values_t[head],
                            raised.astype(jnp.bfloat16),
                            preferred_element_type=jnp.float32,
                        )
                        result[where, lanes] = (summed / norm).T.astype(jnp.bfloat16)
                    return carry

                if size == step:
                    tile(0, 0)
                else:
                    lax.fori_loop(0, size // step, tile, 0)

            below = size
        for view in range(count):
            moved = result[rows_at(table[place_ref[0] ^ view], rows), :]
            ordered[rows_at(by_view[view], rows), :] = moved
        first = 0
        for length, out_ref in zip(lengths, out_refs):
            out_ref[...] = ordered[first : first + length, :]
            first += length

    flops = 4 * total * total * width // 25
    return pl.pallas_call(
        body,
        grid_spec=pltpu.PrefetchScalarGridSpec(
            num_scalar_prefetch=1,
            grid=(width // span,),
            in_specs=[pl.BlockSpec((3, rows, span), lambda h, *_: (0, 0, h))] * count,
            out_specs=[pl.BlockSpec((length, span), lambda h, *_: (0, h)) for length in lengths]
            + [pl.BlockSpec(memory_space=pltpu.SMEM)] * 2,
            scratch_shapes=[
                pltpu.VMEM((total, span), jnp.bfloat16),
                pltpu.VMEM((total + total // 5, span), jnp.bfloat16),
                pltpu.VMEM((total, span), jnp.bfloat16),
                pltpu.VMEM((total, span), jnp.bfloat16),
                pltpu.VMEM((total, span), jnp.bfloat16),
                pltpu.SMEM((count,), jnp.int32),
            ],
        ),
        out_shape=[jax.ShapeDtypeStruct((length, width), jnp.bfloat16) for length in lengths]
        + [jax.ShapeDtypeStruct((count,), jnp.int32), jax.ShapeDtypeStruct((1,), jnp.int32)],
        compiler_params=params(40),
        cost_estimate=pl.CostEstimate(
            flops=flops, bytes_accessed=total * width, transcendentals=flops // 512
        ),
        name="attend",
    )(place, pltpu.with_memory_space_constraint(received[0], pltpu.HBM), *received[1:])


def gather_features(own, count, between=lambda arrived: arrived):
    half = own.shape[0] // 2
    held = {0: [own]}
    if count == 8:
        over_x = xor_permute(own, 2, count)
        over_y = xor_permute(own, 4, count)
        held[1] = [between(xor_permute(own, 1, count))]
        held[1][0], over_x, over_y = lax.optimization_barrier((held[1][0], over_x, over_y))
        held[2], held[4] = [over_x], [over_y]
        held[6] = [xor_permute(over_x[:half], 4, count), xor_permute(over_y[half:], 2, count)]
    else:
        for mask in range(2, count, 2):
            held[mask] = [xor_permute(own, mask, count)]
        held[1] = [between(xor_permute(own, 1, count))]
    for mask in range(2, count, 2):
        if mask == 4:
            held[6], held[4] = lax.optimization_barrier((held[6], held[4]))
        held[mask + 1] = [xor_permute(piece, 1, count) for piece in held[mask]]
    return [held[mask] for mask in range(count)]


def unfilled(shape):
    def body(out_ref):
        pass

    return pl.pallas_call(
        body,
        out_specs=pl.BlockSpec(memory_space=pl.ANY),
        out_shape=shape,
        name="unfilled",
    )()


NEAR = 2


def near_shards(shards):
    return {distance: shards[distance] for distance in shards if abs(distance) <= NEAR}


def shard_apart(place_ref, group_ref, pair, each):
    return group_ref[0] - (place_ref[0] ^ (2 * pair)) // each


def send_weights(place_ref, group_ref, pair, each, width, distances, shard_refs, target, sem):
    apart = shard_apart(place_ref, group_ref, pair, each)
    for distance, shard_ref in zip(distances, shard_refs):

        @pl.when(apart == distance)
        def _():
            for side in range(2):
                owner = place_ref[0] ^ (2 * pair + side)
                start = pl.multiple_of((owner % each) * width, width)
                pltpu.make_async_copy(
                    shard_ref.at[pl.ds(start, width), :],
                    target.at[side * width : (side + 1) * width, :],
                    sem,
                ).start()


def send_features(piece_refs, size, width, target, sem):
    for side, refs in enumerate(piece_refs):
        first = 0
        for ref in refs:
            length = min(ref.shape[0], size - first)
            pltpu.make_async_copy(
                ref.at[:length, :],
                target.at[first : first + length, side * width : (side + 1) * width],
                sem,
            ).start()
            first += length


def wait_all(*buffers_and_sems):
    for buffer, sem in buffers_and_sems:
        pltpu.make_async_copy(buffer, buffer, sem).wait()


def group_refs(refs, features):
    grouped, taken = [], 0
    for pieces in features:
        grouped.append(refs[taken : taken + len(pieces)])
        taken += len(pieces)
    return grouped


def pinned(arrays):
    return [pltpu.with_memory_space_constraint(array, pltpu.HBM) for array in arrays]


def project_near(place, group, counts, features, shards, rows, always):
    count = len(features)
    pairs = count // 2 - 1
    flat = [piece for pieces in features[: 2 * pairs] for piece in pieces]
    width = flat[0].shape[1]
    shards = near_shards(shards)
    distances = sorted(shards)
    columns = shards[0].shape[1]
    each = shards[0].shape[0] // width
    bounds = [size for size in variants(count * rows) if size <= always]

    def body(place_ref, group_ref, counts_ref, *refs):
        grouped = group_refs(refs[: len(flat)], features[: 2 * pairs])
        shard_refs = refs[len(flat) : len(flat) + len(distances)]
        out_ref, landed, weight_all, sums, sems, weight_sems, out_sem = refs[
            len(flat) + len(distances) :
        ]
        used = sum(counts_ref[mask] for mask in range(count)) * BLOCK

        def taken(pair):
            apart = shard_apart(place_ref, group_ref, pair, each)
            return (apart <= NEAR) & (apart >= -NEAR)

        below = 0
        for size in bounds:

            @pl.when((used > below) & ((used <= size) | (size == always)))
            def _(size=size):
                for pair in range(pairs):

                    @pl.when(taken(pair))
                    def _(pair=pair):
                        send_weights(
                            place_ref, group_ref, pair, each, width, distances, shard_refs,
                            weight_all.at[pair], weight_sems.at[pair],
                        )
                        send_features(
                            grouped[2 * pair : 2 * pair + 2], size, width,
                            landed.at[pair], sems.at[pair],
                        )

                sums[:size, :] = jnp.zeros((size, columns), jnp.float32)

                def add(pair, carry):
                    @pl.when(taken(pair))
                    def _():
                        wait_all(
                            (weight_all.at[pair], weight_sems.at[pair]),
                            (landed.at[pair, :size, :], sems.at[pair]),
                        )
                        sums[:size, :] += jnp.dot(
                            landed[pair, :size, :],
                            weight_all[pair],
                            preferred_element_type=jnp.float32,
                        )

                    return carry

                lax.fori_loop(0, pairs, add, 0)
                copy = pltpu.make_async_copy(
                    sums.at[:size, :], out_ref.at[:size, :], out_sem.at[0]
                )
                copy.start()
                copy.wait()

            below = size

    any_spec = pl.BlockSpec(memory_space=pl.ANY)
    inputs = pinned(flat + [shards[distance] for distance in distances])
    return pl.pallas_call(
        body,
        grid_spec=pltpu.PrefetchScalarGridSpec(
            num_scalar_prefetch=3,
            grid=(1,),
            in_specs=[any_spec] * len(inputs),
            out_specs=any_spec,
            scratch_shapes=[
                pltpu.VMEM((pairs, always, 2 * width), jnp.bfloat16),
                pltpu.VMEM((pairs, 2 * width, columns), jnp.bfloat16),
                pltpu.VMEM((always, columns), jnp.float32),
                pltpu.SemaphoreType.DMA((pairs,)),
                pltpu.SemaphoreType.DMA((pairs,)),
                pltpu.SemaphoreType.DMA((1,)),
            ],
        ),
        out_shape=jax.ShapeDtypeStruct((always, columns), jnp.float32),
        compiler_params=params(56),
        cost_estimate=pl.CostEstimate(
            flops=0, bytes_accessed=always * columns, transcendentals=0
        ),
        name="project_near",
    )(place, group, counts, *inputs)


def project(place, group, counts, features, more, shards, partial, rows):
    count = len(features)
    pairs = count // 2
    width = more.shape[2]
    total = count * rows
    always = total - more.shape[1]
    distances = sorted(shards)
    columns = shards[0].shape[1]
    each = shards[0].shape[0] // width
    bounds = [size for size in variants(total) if size <= always] + [total]
    flat = [piece for pieces in features for piece in pieces]

    def body(place_ref, group_ref, counts_ref, *refs):
        grouped = group_refs(refs[: len(flat)], features)
        more_ref, partial_ref = refs[len(flat) : len(flat) + 2]
        refs = refs[len(flat) + 2 :]
        shard_refs = refs[: len(distances)]
        out_refs = refs[len(distances) : len(distances) + count]
        landed, weight_all, sums, sems, weight_sems, partial_sem = refs[len(distances) + count :]
        used = sum(counts_ref[mask] for mask in range(count)) * BLOCK

        def left(pair):
            apart = shard_apart(place_ref, group_ref, pair, each)
            return (pair == pairs - 1) | (apart > NEAR) | (apart < -NEAR)

        below = 0
        for size in bounds:
            low = min(size, always)

            @pl.when((used > below) & (used <= size))
            def _(size=size, low=low):
                load = pltpu.make_async_copy(
                    partial_ref.at[:low, :], sums.at[:low, :], partial_sem.at[0]
                )
                load.start()
                for pair in range(pairs):
                    sources = [list(grouped[2 * pair + side]) for side in range(2)]
                    if size > always:
                        for side in range(2):
                            sources[side].append(more_ref.at[2 * pair + side])

                    @pl.when(left(pair) | (size > always))
                    def _(pair=pair, sources=sources):
                        send_weights(
                            place_ref, group_ref, pair, each, width, distances, shard_refs,
                            weight_all.at[pair], weight_sems.at[pair],
                        )
                        send_features(sources, size, width, landed.at[pair], sems.at[pair])

                if size > always:
                    sums[always:, :] = jnp.zeros((total - always, columns), jnp.float32)
                load.wait()

                def add_rows(pair, first, end):
                    sums[first:end, :] += jnp.dot(
                        landed[pair, first:end, :],
                        weight_all[pair],
                        preferred_element_type=jnp.float32,
                    )

                def add(pair, carry):
                    @pl.when(left(pair) | (size > always))
                    def _():
                        wait_all(
                            (weight_all.at[pair], weight_sems.at[pair]),
                            (landed.at[pair, :size, :], sems.at[pair]),
                        )

                    @pl.when(left(pair))
                    def _():
                        add_rows(pair, 0, low)

                    if size > always:
                        add_rows(pair, always, size)
                    return carry

                lax.fori_loop(0, pairs, add, 0)

            below = size
        for mask in range(count):
            position = 0
            for view in range(count):
                position = position + jnp.where(
                    view < (place_ref[0] ^ mask), counts_ref[place_ref[0] ^ view], 0
                )
            moved = sums[rows_at(position * BLOCK, rows), :]
            out_refs[mask][...] = moved.astype(jnp.bfloat16)

    any_spec = pl.BlockSpec(memory_space=pl.ANY)
    inputs = pinned(flat + [more, partial] + [shards[distance] for distance in distances])
    return pl.pallas_call(
        body,
        grid_spec=pltpu.PrefetchScalarGridSpec(
            num_scalar_prefetch=3,
            grid=(1,),
            in_specs=[any_spec] * len(inputs),
            out_specs=[full_spec((rows, columns))] * count,
            scratch_shapes=[
                pltpu.VMEM((pairs, total, 2 * width), jnp.bfloat16),
                pltpu.VMEM((pairs, 2 * width, columns), jnp.bfloat16),
                pltpu.VMEM((total, columns), jnp.float32),
                pltpu.SemaphoreType.DMA((pairs,)),
                pltpu.SemaphoreType.DMA((pairs,)),
                pltpu.SemaphoreType.DMA((1,)),
            ],
        ),
        out_shape=[jax.ShapeDtypeStruct((rows, columns), jnp.bfloat16)] * count,
        compiler_params=params(56),
        cost_estimate=pl.CostEstimate(
            flops=total * count * width * columns // 4,
            bytes_accessed=total * count * width,
            transcendentals=0,
        ),
        name="project",
    )(place, group, counts, *inputs)


def assemble(place, block_counts, row_mask, pieces, count):
    rows, columns = pieces[0].shape
    if columns % HEAD_DIM:
        stacked = jnp.stack(pieces)[jnp.arange(count) ^ place[0]]
        result = jnp.moveaxis(stacked, 0, 1).reshape(rows, count * columns)
        offsets = jnp.arange(rows, dtype=jnp.int32)
        good = (row_mask[0] == 1) & (offsets // BLOCK < block_counts[0, 0])
        return jnp.where(good[:, None], result, jnp.bfloat16(0.0))

    def body(place_ref, blocks_ref, mask_ref, *refs):
        out_ref = refs[-1]
        good = valid_column(mask_ref, blocks_ref[0, 0]) > 0.5
        for mask in range(count):
            start = pl.multiple_of((place_ref[0] ^ mask) * columns, HEAD_DIM)
            out_ref[:, pl.ds(start, columns)] = jnp.where(
                good, refs[mask][...], jnp.bfloat16(0.0)
            )

    return pl.pallas_call(
        body,
        grid_spec=pltpu.PrefetchScalarGridSpec(
            num_scalar_prefetch=2,
            grid=(1,),
            in_specs=[full_spec((1, rows))] + [full_spec((rows, columns))] * count,
            out_specs=full_spec((rows, count * columns)),
        ),
        out_shape=jax.ShapeDtypeStruct((rows, count * columns), jnp.bfloat16),
        compiler_params=params(16),
        cost_estimate=pl.CostEstimate(
            flops=0, bytes_accessed=4 * rows * count * columns, transcendentals=0
        ),
        name="assemble",
    )(
        place,
        block_counts,
        row_mask,
        pltpu.with_memory_space_constraint(pieces[0], pltpu.HBM),
        *pieces[1:],
    )


def local(queries, keys, values, out_weight, block_counts, row_mask):
    rows = queries.shape[1]
    count = lax.axis_size("cam")
    total = count * rows
    place_array = jnp.full((1,), lax.axis_index("cam"), jnp.int32)
    group_array = jnp.full((1,), lax.axis_index("fsdp"), jnp.int32)

    shards = {0: cut_weight(place_array, out_weight, count)}
    queries, shards[0] = lax.optimization_barrier((queries, shards[0]))
    groups = lax.axis_size("fsdp")

    received = [None] * count
    early = [mask for mask in order(count) if mask & 1 == 0]
    late = [mask for mask in order(count) if mask & 1]
    pass_weight(shards, 1)

    def payloads_for(masks):
        packed = pack(place_array, block_counts, row_mask, queries, keys, values, masks, count)
        return dict(zip(masks, packed))

    for mask, block in payloads_for(early).items():
        received[mask] = xor_permute(block, mask, count)
    received[early[0]], queries = lax.optimization_barrier((received[early[0]], queries))
    payloads = payloads_for(late + [0])
    received[0] = payloads[0]
    for mask in late[1:-1]:
        received[mask] = xor_permute(payloads[mask], mask, count)
    gate = [received[mask] for mask in early[1:]]
    gate, shards[1], shards[-1] = lax.optimization_barrier((gate, shards[1], shards[-1]))
    for mask, block in zip(early[1:], gate):
        received[mask] = block
    pass_weight(shards, 2)
    gate = [received[mask] for mask in late[1:-1]]
    gate, payloads = lax.optimization_barrier((gate, payloads))
    for mask, block in zip(late[1:-1], gate):
        received[mask] = block
    for mask in (late[0], late[-1]):
        received[mask] = xor_permute(payloads[mask], mask, count)
    always = total * 3 // 5
    attended, rest, counts, used = attend(
        place_array, received, rows, (always, total - always)
    )
    shape = jax.ShapeDtypeStruct((count,) + rest.shape, rest.dtype)

    def gather_rest(part):
        return jnp.stack([jnp.concatenate(pieces) for pieces in gather_features(part, count)])

    def weight_step(arrived):
        arrived, shards[2], shards[-2] = lax.optimization_barrier((arrived, shards[2], shards[-2]))
        pass_weight(shards, 3)
        return arrived

    features = gather_features(attended, count, weight_step)
    for distance in range(4, groups):
        pass_weight(shards, distance)
    partial = project_near(
        place_array, group_array, counts, features, shards, rows, always
    )
    rest, features, shards, partial = lax.optimization_barrier((rest, features, shards, partial))
    more = lax.cond(used[0] > always, gather_rest, lambda part: unfilled(shape), rest)
    pieces = project(
        place_array, group_array, counts, features, more, shards, partial, rows
    )
    landed = [pieces[0]] + [None] * (count - 1)
    for mask in order(count):
        landed[mask] = xor_permute(pieces[mask], mask, count)
    return assemble(place_array, block_counts, row_mask, landed, count)[None]


def solution(mesh):
    in_specs = (
        P("fsdp", "cam", None),
        P("fsdp", "cam", None),
        P("fsdp", "cam", None),
        P("fsdp", None),
        P("fsdp", "cam"),
        P("fsdp", "cam"),
    )
    out_specs = P("fsdp", "cam", None)
    return jax.shard_map(local, mesh=mesh, in_specs=in_specs, out_specs=out_specs, check_vma=False)
```

```python
import math

import jax
import jax.numpy as jnp
from jax import lax
from jax.experimental import pallas as pl
from jax.experimental.pallas import tpu as pltpu
from jax.sharding import PartitionSpec as P

HEAD_DIM = 128
BLOCK = 32
SENTINEL = 32.0
LIMIT = 24.0
UNIT = 128


def params(mebibytes):
    return pltpu.CompilerParams(vmem_limit_bytes=mebibytes * 1024 * 1024)


def order(count):
    return sorted(range(1, count), key=lambda mask: (mask == 1, mask & 1, -bin(mask).count("1")))


def variants(total):
    return sorted({-(-total * tenths // (10 * UNIT)) * UNIT for tenths in (4, 5, 6, 8, 10)})


def full_spec(shape):
    return pl.BlockSpec(shape, lambda i, *_: (0,) * len(shape))


def column_of(row):
    n = row.shape[1]
    diagonal = lax.broadcasted_iota(jnp.int32, (n, n), 0) == lax.broadcasted_iota(
        jnp.int32, (n, n), 1
    )
    return jnp.sum(jnp.where(diagonal, row, 0.0), axis=1, keepdims=True)


def valid_column(mask_ref, blocks):
    rows = mask_ref.shape[1]
    inside = lax.broadcasted_iota(jnp.int32, (1, rows), 1) < blocks * BLOCK
    return column_of(jnp.where((mask_ref[...] == 1) & inside, 1.0, 0.0))


def xor_permute(array, mask, count):
    return lax.ppermute(array, "cam", [(place, place ^ mask) for place in range(count)])


def cut_weight(place, out_weight, count):
    depth = out_weight.shape[0]
    columns = out_weight.shape[1] // count
    if columns % HEAD_DIM:
        return lax.dynamic_slice_in_dim(out_weight, place[0] * columns, columns, axis=1)
    parts = 4
    step = depth // parts

    def body(place_ref, w_ref, out_ref, held, load_sems, store_sems):
        start = pl.multiple_of(place_ref[0] * columns, HEAD_DIM)
        loads, stores = [], []
        for part in range(parts):
            inside = pl.ds(part * step, step)
            load = pltpu.make_async_copy(
                w_ref.at[inside, pl.ds(start, columns)], held.at[part], load_sems.at[part]
            )
            load.start()
            loads.append(load)
        for part in range(parts):
            inside = pl.ds(part * step, step)
            loads[part].wait()
            store = pltpu.make_async_copy(held.at[part], out_ref.at[inside, :], store_sems.at[part])
            store.start()
            stores.append(store)
        for store in stores:
            store.wait()

    return pl.pallas_call(
        body,
        grid_spec=pltpu.PrefetchScalarGridSpec(
            num_scalar_prefetch=1,
            grid=(1,),
            in_specs=[pl.BlockSpec(memory_space=pl.ANY)],
            out_specs=pl.BlockSpec(memory_space=pl.ANY),
            scratch_shapes=[
                pltpu.VMEM((parts, step, columns), jnp.bfloat16),
                pltpu.SemaphoreType.DMA((parts,)),
                pltpu.SemaphoreType.DMA((parts,)),
            ],
        ),
        out_shape=jax.ShapeDtypeStruct((depth, columns), jnp.bfloat16),
        compiler_params=params(56),
        cost_estimate=pl.CostEstimate(
            flops=0, bytes_accessed=4 * depth * columns, transcendentals=0
        ),
        name="cut_weight",
    )(place, out_weight)


def pack(place, block_counts, row_mask, queries, keys, values, masks, count):
    _, rows, features = queries.shape
    width = features // count
    number = len(masks)

    def body(place_ref, blocks_ref, mask_ref, q_ref, k_ref, v_ref, *refs):
        out_refs = refs[:number]
        held, load_sems, store_sems = refs[number:]

        def copies(index, slot):
            start = pl.multiple_of((place_ref[0] ^ masks[index]) * width, HEAD_DIM)
            source = (q_ref, k_ref, v_ref)[slot].at[0, :, pl.ds(start, width)]
            buffer = held.at[index, slot]
            return (
                pltpu.make_async_copy(source, buffer, load_sems.at[index, slot]),
                pltpu.make_async_copy(
                    buffer, out_refs[index].at[slot], store_sems.at[index, slot]
                ),
            )

        steps = [copies(index, slot) for slot in (1, 0, 2) for index in range(number)]
        for load, _ in steps:
            load.start()
        good = valid_column(mask_ref, blocks_ref[0, 0]) > 0.5
        for step, (load, store) in enumerate(steps):
            load.wait()
            if step < number:
                held[step, 1] = jnp.where(good, held[step, 1], jnp.bfloat16(SENTINEL))
            store.start()
        for _, store in steps:
            store.wait()

    any_spec = pl.BlockSpec(memory_space=pl.ANY)
    return list(
        pl.pallas_call(
            body,
            grid_spec=pltpu.PrefetchScalarGridSpec(
                num_scalar_prefetch=2,
                grid=(1,),
                in_specs=[full_spec((1, rows))] + [any_spec] * 3,
                out_specs=[any_spec] * number,
                scratch_shapes=[
                    pltpu.VMEM((number, 3, rows, width), jnp.bfloat16),
                    pltpu.SemaphoreType.DMA((number, 3)),
                    pltpu.SemaphoreType.DMA((number, 3)),
                ],
            ),
            out_shape=[jax.ShapeDtypeStruct((3, rows, width), jnp.bfloat16)] * number,
            compiler_params=params(56),
            cost_estimate=pl.CostEstimate(
                flops=0, bytes_accessed=12 * rows * width * number, transcendentals=0
            ),
            name="pack",
        )(place, block_counts, row_mask, queries, keys, values)
    )


def pass_weight(shards, distance):
    groups = lax.axis_size("fsdp")
    for sign in (1, -1):
        pairs = []
        for source in range(groups):
            origin, target = source - sign * (distance - 1), source + sign
            if 0 <= origin < groups and 0 <= target < groups:
                pairs.append((source, target))
        shards[sign * distance] = lax.ppermute(shards[sign * (distance - 1)], "fsdp", pairs)


def packed_offsets(place_ref, counts_ref, table, count):
    by_mask, running = [], 0
    for mask in range(count):
        by_mask.append(running)
        table[mask] = running
        running = running + counts_ref[mask] * BLOCK
    by_view, position = [], 0
    for view in range(count):
        by_view.append(position)
        position = position + counts_ref[place_ref[0] ^ view] * BLOCK
    return by_mask, by_view, running


def rows_at(start, size):
    return pl.ds(start if isinstance(start, int) else pl.multiple_of(start, BLOCK), size)


def tile_of(size):
    return max(rows for rows in range(UNIT, 6 * UNIT + 1, UNIT) if size % rows == 0)


def attend(place, received, rows, lengths):
    count = len(received)
    width = received[0].shape[2]
    total = count * rows
    span = min(width, 4 * HEAD_DIM)
    factor = math.log2(math.e) / math.sqrt(HEAD_DIM)

    def body(place_ref, *refs):
        parts = refs[:count]
        out_refs = refs[count : count + len(lengths)]
        counts_ref, used_ref = refs[count + len(lengths) : count + len(lengths) + 2]
        query_all, key_all, value_all, result, ordered, table = refs[count + len(lengths) + 2 :]

        @pl.when(pl.program_id(0) == 0)
        def _():
            value_all[...] = jnp.zeros_like(value_all)
            for mask in range(count):
                blocks = jnp.zeros((1, HEAD_DIM), jnp.float32)
                for first in range(0, rows, BLOCK):
                    row = parts[mask][1, first : first + 16, :HEAD_DIM].astype(jnp.float32)[:1]
                    blocks = blocks + jnp.where(row < LIMIT, 1.0, 0.0)
                counts_ref[mask] = jnp.max(blocks).astype(jnp.int32)

        by_mask, by_view, used = packed_offsets(place_ref, counts_ref, table, count)
        used_ref[0] = used
        for mask in range(count):
            where = rows_at(by_mask[mask], rows)
            query_all[where, :] = parts[mask][0]
            key_all[where, :] = parts[mask][1]
            value_all[where, :] = parts[mask][2]
        key_all[rows_at(used, total // 5), :] = jnp.full((total // 5, span), SENTINEL, jnp.bfloat16)
        below = 0
        for size in variants(total):

            @pl.when((used > below) & (used <= size))
            def _(size=size):
                step = tile_of(size)
                key_mask = key_all[:size, :HEAD_DIM].astype(jnp.float32) > LIMIT
                bias = jnp.where(key_mask, jnp.float32(-1e30), 0.0)
                bias = jnp.concatenate([bias] * (step // HEAD_DIM), axis=1)
                values_t = [
                    value_all[:size, first : first + HEAD_DIM].T
                    for first in range(0, span, HEAD_DIM)
                ]

                def tile(index, carry):
                    if isinstance(index, int):
                        where = pl.ds(index * step, step)
                    else:
                        where = pl.ds(pl.multiple_of(index * step, UNIT), step)
                    for head in range(span // HEAD_DIM):
                        lanes = slice(head * HEAD_DIM, (head + 1) * HEAD_DIM)
                        scores = lax.dot_general(
                            key_all[:size, lanes],
                            query_all[where, lanes],
                            (((1,), (1,)), ((), ())),
                            preferred_element_type=jnp.float32,
                        )
                        scores = scores + bias
                        top = jnp.max(scores, axis=0, keepdims=True)
                        raised = jnp.exp2((scores - top) * factor)
                        norm = jnp.sum(raised, axis=0, keepdims=True)
                        summed = jnp.dot(
                            values_t[head],
                            raised.astype(jnp.bfloat16),
                            preferred_element_type=jnp.float32,
                        )
                        result[where, lanes] = (summed / norm).T.astype(jnp.bfloat16)
                    return carry

                if size == step:
                    tile(0, 0)
                else:
                    lax.fori_loop(0, size // step, tile, 0)

            below = size
        for view in range(count):
            moved = result[rows_at(table[place_ref[0] ^ view], rows), :]
            ordered[rows_at(by_view[view], rows), :] = moved
        first = 0
        for length, out_ref in zip(lengths, out_refs):
            out_ref[...] = ordered[first : first + length, :]
            first += length

    flops = 4 * total * total * width // 25
    return pl.pallas_call(
        body,
        grid_spec=pltpu.PrefetchScalarGridSpec(
            num_scalar_prefetch=1,
            grid=(width // span,),
            in_specs=[pl.BlockSpec((3, rows, span), lambda h, *_: (0, 0, h))] * count,
            out_specs=[pl.BlockSpec((length, span), lambda h, *_: (0, h)) for length in lengths]
            + [pl.BlockSpec(memory_space=pltpu.SMEM)] * 2,
            scratch_shapes=[
                pltpu.VMEM((total, span), jnp.bfloat16),
                pltpu.VMEM((total + total // 5, span), jnp.bfloat16),
                pltpu.VMEM((total, span), jnp.bfloat16),
                pltpu.VMEM((total, span), jnp.bfloat16),
                pltpu.VMEM((total, span), jnp.bfloat16),
                pltpu.SMEM((count,), jnp.int32),
            ],
        ),
        out_shape=[jax.ShapeDtypeStruct((length, width), jnp.bfloat16) for length in lengths]
        + [jax.ShapeDtypeStruct((count,), jnp.int32), jax.ShapeDtypeStruct((1,), jnp.int32)],
        compiler_params=params(40),
        cost_estimate=pl.CostEstimate(
            flops=flops, bytes_accessed=total * width, transcendentals=flops // 512
        ),
        name="attend",
    )(place, pltpu.with_memory_space_constraint(received[0], pltpu.HBM), *received[1:])


def gather_features(own, count, between=lambda arrived: arrived):
    half = own.shape[0] // 2
    held = {0: [own]}
    if count == 8:
        over_x = xor_permute(own, 2, count)
        over_y = xor_permute(own, 4, count)
        held[1] = [between(xor_permute(own, 1, count))]
        held[1][0], over_x, over_y = lax.optimization_barrier((held[1][0], over_x, over_y))
        held[2], held[4] = [over_x], [over_y]
        held[6] = [xor_permute(over_x[:half], 4, count), xor_permute(over_y[half:], 2, count)]
    else:
        for mask in range(2, count, 2):
            held[mask] = [xor_permute(own, mask, count)]
        held[1] = [between(xor_permute(own, 1, count))]
    for mask in range(2, count, 2):
        if mask == 4:
            held[6], held[4] = lax.optimization_barrier((held[6], held[4]))
        held[mask + 1] = [xor_permute(piece, 1, count) for piece in held[mask]]
    return [held[mask] for mask in range(count)]


def unfilled(shape):
    def body(out_ref):
        pass

    return pl.pallas_call(
        body,
        out_specs=pl.BlockSpec(memory_space=pl.ANY),
        out_shape=shape,
        name="unfilled",
    )()


NEAR = 2


def near_shards(shards):
    return {distance: shards[distance] for distance in shards if abs(distance) <= NEAR}


def shard_apart(place_ref, group_ref, pair, each):
    return group_ref[0] - (place_ref[0] ^ (2 * pair)) // each


def send_weights(place_ref, group_ref, pair, each, width, distances, shard_refs, target, sem):
    apart = shard_apart(place_ref, group_ref, pair, each)
    for distance, shard_ref in zip(distances, shard_refs):

        @pl.when(apart == distance)
        def _():
            for side in range(2):
                owner = place_ref[0] ^ (2 * pair + side)
                start = pl.multiple_of((owner % each) * width, width)
                pltpu.make_async_copy(
                    shard_ref.at[pl.ds(start, width), :],
                    target.at[side * width : (side + 1) * width, :],
                    sem,
                ).start()


def send_features(piece_refs, size, width, target, sem):
    for side, refs in enumerate(piece_refs):
        first = 0
        for ref in refs:
            length = min(ref.shape[0], size - first)
            pltpu.make_async_copy(
                ref.at[:length, :],
                target.at[first : first + length, side * width : (side + 1) * width],
                sem,
            ).start()
            first += length


def wait_all(*buffers_and_sems):
    for buffer, sem in buffers_and_sems:
        pltpu.make_async_copy(buffer, buffer, sem).wait()


def group_refs(refs, features):
    grouped, taken = [], 0
    for pieces in features:
        grouped.append(refs[taken : taken + len(pieces)])
        taken += len(pieces)
    return grouped


def pinned(arrays):
    return [pltpu.with_memory_space_constraint(array, pltpu.HBM) for array in arrays]


def project_near(place, group, counts, features, shards, rows, always):
    count = len(features)
    pairs = count // 2 - 1
    flat = [piece for pieces in features[: 2 * pairs] for piece in pieces]
    width = flat[0].shape[1]
    shards = near_shards(shards)
    distances = sorted(shards)
    columns = shards[0].shape[1]
    each = shards[0].shape[0] // width
    bounds = [size for size in variants(count * rows) if size <= always]

    def body(place_ref, group_ref, counts_ref, *refs):
        grouped = group_refs(refs[: len(flat)], features[: 2 * pairs])
        shard_refs = refs[len(flat) : len(flat) + len(distances)]
        out_ref, landed, weight_all, sums, sems, weight_sems, out_sem = refs[
            len(flat) + len(distances) :
        ]
        used = sum(counts_ref[mask] for mask in range(count)) * BLOCK

        def taken(pair):
            apart = shard_apart(place_ref, group_ref, pair, each)
            return (apart <= NEAR) & (apart >= -NEAR)

        below = 0
        for size in bounds:

            @pl.when((used > below) & ((used <= size) | (size == always)))
            def _(size=size):
                for pair in range(pairs):

                    @pl.when(taken(pair))
                    def _(pair=pair):
                        send_weights(
                            place_ref, group_ref, pair, each, width, distances, shard_refs,
                            weight_all.at[pair], weight_sems.at[pair],
                        )
                        send_features(
                            grouped[2 * pair : 2 * pair + 2], size, width,
                            landed.at[pair], sems.at[pair],
                        )

                sums[:size, :] = jnp.zeros((size, columns), jnp.float32)

                def add(pair, carry):
                    @pl.when(taken(pair))
                    def _():
                        wait_all(
                            (weight_all.at[pair], weight_sems.at[pair]),
                            (landed.at[pair, :size, :], sems.at[pair]),
                        )
                        sums[:size, :] += jnp.dot(
                            landed[pair, :size, :],
                            weight_all[pair],
                            preferred_element_type=jnp.float32,
                        )

                    return carry

                lax.fori_loop(0, pairs, add, 0)
                copy = pltpu.make_async_copy(
                    sums.at[:size, :], out_ref.at[:size, :], out_sem.at[0]
                )
                copy.start()
                copy.wait()

            below = size

    any_spec = pl.BlockSpec(memory_space=pl.ANY)
    inputs = pinned(flat + [shards[distance] for distance in distances])
    return pl.pallas_call(
        body,
        grid_spec=pltpu.PrefetchScalarGridSpec(
            num_scalar_prefetch=3,
            grid=(1,),
            in_specs=[any_spec] * len(inputs),
            out_specs=any_spec,
            scratch_shapes=[
                pltpu.VMEM((pairs, always, 2 * width), jnp.bfloat16),
                pltpu.VMEM((pairs, 2 * width, columns), jnp.bfloat16),
                pltpu.VMEM((always, columns), jnp.float32),
                pltpu.SemaphoreType.DMA((pairs,)),
                pltpu.SemaphoreType.DMA((pairs,)),
                pltpu.SemaphoreType.DMA((1,)),
            ],
        ),
        out_shape=jax.ShapeDtypeStruct((always, columns), jnp.float32),
        compiler_params=params(56),
        cost_estimate=pl.CostEstimate(
            flops=0, bytes_accessed=always * columns, transcendentals=0
        ),
        name="project_near",
    )(place, group, counts, *inputs)


def project(place, group, counts, features, more, shards, partial, rows):
    count = len(features)
    pairs = count // 2
    width = more.shape[2]
    total = count * rows
    always = total - more.shape[1]
    distances = sorted(shards)
    columns = shards[0].shape[1]
    each = shards[0].shape[0] // width
    bounds = [size for size in variants(total) if size <= always] + [total]
    flat = [piece for pieces in features for piece in pieces]

    def body(place_ref, group_ref, counts_ref, *refs):
        grouped = group_refs(refs[: len(flat)], features)
        more_ref, partial_ref = refs[len(flat) : len(flat) + 2]
        refs = refs[len(flat) + 2 :]
        shard_refs = refs[: len(distances)]
        out_refs = refs[len(distances) : len(distances) + count]
        landed, weight_all, sums, sems, weight_sems, partial_sem = refs[len(distances) + count :]
        used = sum(counts_ref[mask] for mask in range(count)) * BLOCK

        def left(pair):
            apart = shard_apart(place_ref, group_ref, pair, each)
            return (pair == pairs - 1) | (apart > NEAR) | (apart < -NEAR)

        below = 0
        for size in bounds:
            low = min(size, always)

            @pl.when((used > below) & (used <= size))
            def _(size=size, low=low):
                load = pltpu.make_async_copy(
                    partial_ref.at[:low, :], sums.at[:low, :], partial_sem.at[0]
                )
                load.start()
                for pair in range(pairs):
                    sources = [list(grouped[2 * pair + side]) for side in range(2)]
                    if size > always:
                        for side in range(2):
                            sources[side].append(more_ref.at[2 * pair + side])

                    @pl.when(left(pair) | (size > always))
                    def _(pair=pair, sources=sources):
                        send_weights(
                            place_ref, group_ref, pair, each, width, distances, shard_refs,
                            weight_all.at[pair], weight_sems.at[pair],
                        )
                        send_features(sources, size, width, landed.at[pair], sems.at[pair])

                if size > always:
                    sums[always:, :] = jnp.zeros((total - always, columns), jnp.float32)
                load.wait()

                def add_rows(pair, first, end):
                    sums[first:end, :] += jnp.dot(
                        landed[pair, first:end, :],
                        weight_all[pair],
                        preferred_element_type=jnp.float32,
                    )

                def add(pair, carry):
                    @pl.when(left(pair) | (size > always))
                    def _():
                        wait_all(
                            (weight_all.at[pair], weight_sems.at[pair]),
                            (landed.at[pair, :size, :], sems.at[pair]),
                        )

                    @pl.when(left(pair))
                    def _():
                        add_rows(pair, 0, low)

                    if size > always:
                        add_rows(pair, always, size)
                    return carry

                lax.fori_loop(0, pairs, add, 0)

            below = size
        for mask in range(count):
            position = 0
            for view in range(count):
                position = position + jnp.where(
                    view < (place_ref[0] ^ mask), counts_ref[place_ref[0] ^ view], 0
                )
            moved = sums[rows_at(position * BLOCK, rows), :]
            out_refs[mask][...] = moved.astype(jnp.bfloat16)

    any_spec = pl.BlockSpec(memory_space=pl.ANY)
    inputs = pinned(flat + [more, partial] + [shards[distance] for distance in distances])
    return pl.pallas_call(
        body,
        grid_spec=pltpu.PrefetchScalarGridSpec(
            num_scalar_prefetch=3,
            grid=(1,),
            in_specs=[any_spec] * len(inputs),
            out_specs=[full_spec((rows, columns))] * count,
            scratch_shapes=[
                pltpu.VMEM((pairs, total, 2 * width), jnp.bfloat16),
                pltpu.VMEM((pairs, 2 * width, columns), jnp.bfloat16),
                pltpu.VMEM((total, columns), jnp.float32),
                pltpu.SemaphoreType.DMA((pairs,)),
                pltpu.SemaphoreType.DMA((pairs,)),
                pltpu.SemaphoreType.DMA((1,)),
            ],
        ),
        out_shape=[jax.ShapeDtypeStruct((rows, columns), jnp.bfloat16)] * count,
        compiler_params=params(56),
        cost_estimate=pl.CostEstimate(
            flops=total * count * width * columns // 4,
            bytes_accessed=total * count * width,
            transcendentals=0,
        ),
        name="project",
    )(place, group, counts, *inputs)


def assemble(place, block_counts, row_mask, pieces, count):
    rows, columns = pieces[0].shape
    if columns % HEAD_DIM:
        stacked = jnp.stack(pieces)[jnp.arange(count) ^ place[0]]
        result = jnp.moveaxis(stacked, 0, 1).reshape(rows, count * columns)
        offsets = jnp.arange(rows, dtype=jnp.int32)
        good = (row_mask[0] == 1) & (offsets // BLOCK < block_counts[0, 0])
        return jnp.where(good[:, None], result, jnp.bfloat16(0.0))

    def body(place_ref, blocks_ref, mask_ref, *refs):
        out_ref = refs[-1]
        good = valid_column(mask_ref, blocks_ref[0, 0]) > 0.5
        for mask in range(count):
            start = pl.multiple_of((place_ref[0] ^ mask) * columns, HEAD_DIM)
            out_ref[:, pl.ds(start, columns)] = jnp.where(
                good, refs[mask][...], jnp.bfloat16(0.0)
            )

    return pl.pallas_call(
        body,
        grid_spec=pltpu.PrefetchScalarGridSpec(
            num_scalar_prefetch=2,
            grid=(1,),
            in_specs=[full_spec((1, rows))] + [full_spec((rows, columns))] * count,
            out_specs=full_spec((rows, count * columns)),
        ),
        out_shape=jax.ShapeDtypeStruct((rows, count * columns), jnp.bfloat16),
        compiler_params=params(16),
        cost_estimate=pl.CostEstimate(
            flops=0, bytes_accessed=4 * rows * count * columns, transcendentals=0
        ),
        name="assemble",
    )(
        place,
        block_counts,
        row_mask,
        pltpu.with_memory_space_constraint(pieces[0], pltpu.HBM),
        *pieces[1:],
    )


def local(queries, keys, values, out_weight, block_counts, row_mask):
    rows = queries.shape[1]
    count = lax.axis_size("cam")
    total = count * rows
    place_array = jnp.full((1,), lax.axis_index("cam"), jnp.int32)
    group_array = jnp.full((1,), lax.axis_index("fsdp"), jnp.int32)

    shards = {0: cut_weight(place_array, out_weight, count)}
    queries, shards[0] = lax.optimization_barrier((queries, shards[0]))
    groups = lax.axis_size("fsdp")

    received = [None] * count
    early = [mask for mask in order(count) if mask & 1 == 0]
    late = [mask for mask in order(count) if mask & 1]
    pass_weight(shards, 1)

    def payloads_for(masks):
        packed = pack(place_array, block_counts, row_mask, queries, keys, values, masks, count)
        return dict(zip(masks, packed))

    for mask, block in payloads_for(early).items():
        received[mask] = xor_permute(block, mask, count)
    received[early[0]], queries = lax.optimization_barrier((received[early[0]], queries))
    payloads = payloads_for(late + [0])
    received[0] = payloads[0]
    received[late[0]] = xor_permute(payloads[late[0]], late[0], count)
    gate = [received[mask] for mask in early[1:]]
    gate, shards[1], shards[-1] = lax.optimization_barrier((gate, shards[1], shards[-1]))
    for mask, block in zip(early[1:], gate):
        received[mask] = block
    pass_weight(shards, 2)
    received[late[0]], payloads = lax.optimization_barrier((received[late[0]], payloads))
    for mask in late[1:]:
        received[mask] = xor_permute(payloads[mask], mask, count)
    always = total * 3 // 5
    attended, rest, counts, used = attend(
        place_array, received, rows, (always, total - always)
    )
    shape = jax.ShapeDtypeStruct((count,) + rest.shape, rest.dtype)

    def gather_rest(part):
        return jnp.stack([jnp.concatenate(pieces) for pieces in gather_features(part, count)])

    def weight_step(arrived):
        arrived, shards[2], shards[-2] = lax.optimization_barrier((arrived, shards[2], shards[-2]))
        pass_weight(shards, 3)
        return arrived

    features = gather_features(attended, count, weight_step)
    for distance in range(4, groups):
        pass_weight(shards, distance)
    partial = project_near(
        place_array, group_array, counts, features, shards, rows, always
    )
    rest, features, shards, partial = lax.optimization_barrier((rest, features, shards, partial))
    more = lax.cond(used[0] > always, gather_rest, lambda part: unfilled(shape), rest)
    pieces = project(
        place_array, group_array, counts, features, more, shards, partial, rows
    )
    landed = [pieces[0]] + [None] * (count - 1)
    for mask in order(count):
        landed[mask] = xor_permute(pieces[mask], mask, count)
    return assemble(place_array, block_counts, row_mask, landed, count)[None]


def solution(mesh):
    in_specs = (
        P("fsdp", "cam", None),
        P("fsdp", "cam", None),
        P("fsdp", "cam", None),
        P("fsdp", None),
        P("fsdp", "cam"),
        P("fsdp", "cam"),
    )
    out_specs = P("fsdp", "cam", None)
    return jax.shard_map(local, mesh=mesh, in_specs=in_specs, out_specs=out_specs, check_vma=False)
```
